32 devices in a mesh: dp: 8 (over z, y), cent: 4 (over x, core).
Axes of the slice: x: 2, y: 2, z: 4, core: 2. Of those that a mesh axis runs over, the one named last changes fastest.
Arguments:
- frames: bfloat16 [32768, 1024], P(('dp', 'cent')), may hold values from -6 to 6
- video_length: int32 [32, 128], P(('dp', 'cent')), may hold values from 1 to 16, 1024 in all within a row
- video_owner: int32 [32, 128], P(('dp', 'cent')), may hold values from 0 to 7, as said below
- video_cluster: int32 [32, 128], P(('dp', 'cent')), may hold values from 0 to 255
- frame_code: int32 [32768], P(('dp', 'cent')), may hold values from 0 to 511, as said below
- old_coarse: bfloat16 [2048, 1024], P('dp'), may hold values from -6 to 6
- old_codes: float32 [512, 1024], P(('dp', 'cent')), may hold values from -6 to 6
Outputs:
- new_coarse: float32 [2048, 1024], P(('dp', 'cent'))
- new_codes: float32 [512, 1024], P(('dp', 'cent'))
The draws below stay inside these ranges and needn't reach their ends.
Inputs may be any that keep to these rules, and one draw needn't show every extreme that they name: `video_owner`: each device's row of 128 videos names one index of dp at most 32 times; in every draw some index of dp is named exactly 32 times in every device's row. `frame_code`: among each device's 1024 frames at most 256 have codes in one block of 64 codes (codes b * 64 to (b + 1) * 64 - 1); in every draw some block gets exactly 256 from every device.
All inputs are finite; a program needn't handle non-finite values.
Results may differ from the reference program's by a relative error of at most 0.0015.
Values may be sent and summed in bfloat16 or wider, within the bound.
No kernel may reach another device: no remote copies, remote signals or barrier semaphores. Data moves between devices by JAX's collectives and lax.ppermute only.
A program may use at most 64 MiB of HBM per device.

```python
import math
import jax
import jax.numpy as jnp
import numpy as np
from jax import lax

D = 1024
FR_DEV = 1024
MAXLEN = 16
KC_DEV = 256
KR_DEV = 64
VID_DEV = 128
KC = 2048
KR = 512
CAPV = 32
CAPC = 256
FRAMES = 32768
N_DP = 8
N_CENT = 4
DEVICES = 32


def spread_block(block_key, item_total, targets, capacity, forced):
    first_key, second_key = jax.random.split(block_key)
    free_places = jax.random.permutation(first_key, (targets - 1) * capacity)[:item_total - capacity]
    other_targets = (free_places // capacity).astype(jnp.int32)
    other_targets = other_targets + (other_targets >= forced).astype(jnp.int32)
    chosen = jnp.concatenate([jnp.full((capacity,), forced, jnp.int32), other_targets])
    return jax.random.permutation(second_key, chosen)


def route_blocks(base_key, item_total, capacity):
    forced = jax.random.randint(jax.random.fold_in(base_key, 1), (), 0, N_DP).astype(jnp.int32)
    block_keys = jax.random.split(jax.random.fold_in(base_key, 2), N_DP * N_CENT)
    return jax.vmap(lambda block_key: spread_block(block_key, item_total, N_DP, capacity, forced))(block_keys)


def draw_video_owner(key, part):
    return route_blocks(jax.random.fold_in(key, 31), VID_DEV, CAPV).astype(jnp.int32)


def draw_frame_code(key, part):
    owners = route_blocks(jax.random.fold_in(key, 47), FR_DEV, CAPC)
    offsets = jax.random.randint(jax.random.fold_in(key, 53), owners.shape, 0, KR_DEV)
    return (owners * KR_DEV + offsets).astype(jnp.int32).reshape(-1)


def touch_ends(array, rng, least, top_value):
    place = [jax.random.randint(jax.random.fold_in(rng, axis), (), 0, length) for axis, length in enumerate(array.shape)]
    widest = array.shape.index(max(array.shape))
    beside = place[:widest] + [(place[widest] + 1) % array.shape[widest]] + place[widest + 1:]
    return array.at[tuple(place)].set(least).at[tuple(beside)].set(top_value)


def block_levels(stream_key, extent, cuts, smallest, largest):
    loudness = 1.0
    for axis_at, shards_of in cuts:
        heights = jax.random.uniform(jax.random.fold_in(jax.random.fold_in(stream_key, 6), axis_at), (shards_of,), jnp.float32, smallest / len(cuts), largest / len(cuts))
        loudness = loudness * jnp.repeat(jnp.exp(heights), extent[axis_at] // shards_of).reshape((-1,) + (1,) * (len(extent) - 1 - axis_at))
    return loudness


def profile(amount, total, reach, skew):
    weights = [(1 << 20) // math.isqrt(rank ** skew) + 1 for rank in range(2, amount + 1)]
    spare, given = total - reach - (amount - 1), [1] * (amount - 1)
    while spare > 0:
        candidates = [i for i in range(amount - 1) if given[i] < reach]
        whole, remaining = sum([weights[i] for i in candidates]), spare
        for i in candidates:
            more = min(reach - given[i], max(1, remaining * weights[i] // whole), spare)
            given[i] = given[i] + more
            spare = spare - more
    return np.array([reach] + given)


def uneven_parts(key, amount, total, reach, lean):
    if amount == 2:
        one = jax.random.randint(key, (), max(1, total - reach), min(reach, total - 1) + 1)
        return jnp.stack([one, total - one])
    sizes = jnp.asarray(profile(amount, total, reach, lean), jnp.int32)
    twos = (amount - 1) // 2
    source_of, taker = sizes[1:1 + 2 * twos:2], sizes[2:2 + 2 * twos:2]
    margin = jnp.minimum(source_of - 1, reach - taker)
    moved = jax.random.randint(jax.random.fold_in(key, 1), (twos,), 0, 1 << 20) % (margin + 1)
    sizes = sizes.at[1:1 + 2 * twos:2].set(source_of - moved).at[2:2 + 2 * twos:2].set(taker + moved)
    return sizes[jax.random.permutation(jax.random.fold_in(key, 2), amount)]


def gaussian(rng, dims, scale, most, cuts=(), kind=jnp.bfloat16):
    entries = scale * jax.random.normal(rng, dims, jnp.float32)
    if cuts:
        entries = entries * block_levels(rng, dims, cuts, -0.22, 0.18)
    return jnp.clip(entries, -most, most).astype(kind)


def setup_inputs(seed: int = 0) -> dict:
    arg_keys = jax.random.split(jax.random.key(seed), 8)
    frames = gaussian(arg_keys[0], (FRAMES, D), 1.0, 6.0, ((0, 32),))
    video_length = jax.vmap(lambda own: uneven_parts(own, VID_DEV, FR_DEV, MAXLEN, 2))(jax.random.split(arg_keys[1], DEVICES)).reshape((DEVICES, VID_DEV)).astype(jnp.int32)
    video_owner = draw_video_owner(jax.random.fold_in(arg_keys[7], 71), 0)
    video_cluster = touch_ends(jax.random.randint(arg_keys[3], (DEVICES, VID_DEV), 0, KC_DEV), jax.random.fold_in(arg_keys[3], 1), 0, KC_DEV - 1).astype(jnp.int32)
    frame_code = draw_frame_code(jax.random.fold_in(arg_keys[7], 71), 0)
    old_coarse = gaussian(arg_keys[5], (KC, D), 1.0, 6.0, ((0, 8),))
    old_codes = gaussian(arg_keys[6], (KR, D), 1.0, 6.0, ((0, 32),), jnp.float32)
    return dict(frames=frames, video_length=video_length, video_owner=video_owner, video_cluster=video_cluster, frame_code=frame_code, old_coarse=old_coarse, old_codes=old_codes)


code_prior = 16.0


def reference(frames, video_length, video_owner, video_cluster, frame_code, old_coarse, old_codes):
    blocks = N_DP * N_CENT
    video_ends = jnp.cumsum(video_length, axis=1)
    position = jnp.arange(FR_DEV, dtype=jnp.int32)
    local_video = jax.vmap(lambda ends_row: jnp.searchsorted(ends_row, position, side="right"))(video_ends).astype(jnp.int32)
    frame_blocks = frames.reshape(blocks, FR_DEV, D)

    def pool_block(packed):
        frame_rows, local_index, lengths = packed
        totals = jax.ops.segment_sum(frame_rows.astype(jnp.float32), local_index, num_segments=VID_DEV)
        return (totals / lengths[:, None].astype(jnp.float32)).astype(jnp.bfloat16)

    pooled = lax.map(pool_block, (frame_blocks, local_video, video_length))
    coarse_ids = (video_owner * KC_DEV + video_cluster).astype(jnp.int32)
    flat_ids = coarse_ids.reshape(-1)
    coarse_sum = jax.ops.segment_sum(pooled.reshape(-1, D).astype(jnp.float32), flat_ids, num_segments=KC)
    coarse_count = jax.ops.segment_sum(jnp.ones(flat_ids.shape, jnp.float32), flat_ids, num_segments=KC)
    new_coarse = (coarse_sum + old_coarse.astype(jnp.float32)) / (coarse_count[:, None] + 1.0)
    anchors = new_coarse.astype(jnp.bfloat16)
    code_blocks = frame_code.reshape(blocks, FR_DEV)

    def add_codes(state, packed):
        frame_rows, local_index, block_ids, code_ids = packed
        frame_coarse = block_ids[local_index]
        residual = (frame_rows.astype(jnp.float32) - anchors[frame_coarse].astype(jnp.float32)).astype(jnp.bfloat16)
        totals, counts = state
        totals = totals + jax.ops.segment_sum(residual.astype(jnp.float32), code_ids, num_segments=KR)
        counts = counts + jax.ops.segment_sum(jnp.ones(code_ids.shape, jnp.float32), code_ids, num_segments=KR)
        return (totals, counts), None

    initial = (jnp.zeros((KR, D), jnp.float32), jnp.zeros((KR,), jnp.float32))
    results = lax.scan(add_codes, initial, (frame_blocks, local_video, coarse_ids, code_blocks))
    code_sum, code_count = results[0]
    new_codes = (code_sum + code_prior * old_codes) / (code_count[:, None] + code_prior)
    return new_coarse, new_codes
```

```python
import functools

import jax
import jax.numpy as jnp
from jax import lax
from jax.experimental import pallas as pl
from jax.experimental.pallas import tpu as pltpu
from jax.sharding import PartitionSpec as P

code_prior = 16.0
LANES = 128
EXACT = 256
f32 = jnp.float32
bf16 = jnp.bfloat16


def iota(shape, axis):
    return lax.broadcasted_iota(jnp.int32, shape, axis)


def dot(left, right):
    return jnp.dot(left, right, preferred_element_type=f32)


def dot_rows(left, right):
    return lax.dot_general(left, right, (((1,), (1,)), ((), ())), preferred_element_type=f32)


def member_of_slots(length_ref, owner_ref, owners, capacity, frame_count):
    videos = length_ref.shape[1]
    slots = owners * capacity
    lengths = length_ref[...].astype(f32)
    owner = owner_ref[...]
    match = (iota((owners, videos), 0) == owner).astype(f32)
    earlier = (iota((videos, videos), 0) < iota((videos, videos), 1)).astype(bf16)
    stacked = jnp.concatenate([match, jnp.broadcast_to(lengths, (8, videos))], axis=0)
    before = dot(stacked.astype(bf16), earlier)
    rank = jnp.sum(before[:owners] * match, axis=0, keepdims=True)
    starts = before[owners : owners + 1]
    slot = owner * capacity + rank.astype(jnp.int32)
    video_of_slot = (iota((slots, videos), 0) == slot).astype(f32).astype(bf16)
    high = jnp.floor(starts / 16.0) * 16.0
    low = starts - high
    tall = lambda row: jnp.broadcast_to(row, (LANES, videos)).astype(bf16)
    start = dot_rows(video_of_slot, tall(high)) + dot_rows(video_of_slot, tall(low))
    length = dot_rows(video_of_slot, tall(lengths))
    first, last = start.astype(jnp.int32), (start + length).astype(jnp.int32)
    member = jnp.concatenate(
        [
            (
                (iota((slots, LANES), 1) + at >= first) & (iota((slots, LANES), 1) + at < last)
            ).astype(f32)
            for at in range(0, frame_count, LANES)
        ],
        axis=1,
    ).astype(bf16)
    return video_of_slot, first, length, member


def code_matches(code_ref, code_total):
    frame_count = code_ref.shape[1]
    return (iota((code_total, frame_count), 0) == code_ref[...]).astype(f32).astype(bf16)


def pool_kernel(sizes, length_ref, owner_ref, cluster_ref, code_ref, frames_hbm, send_ref, frames_ref, sem):
    owners, cents, capacity, longest, code_total = sizes
    copy = pltpu.make_async_copy(frames_hbm, frames_ref, sem)
    copy.start()
    me = lax.axis_index("cent")
    frame_count, features = frames_hbm.shape
    slots = owners * capacity
    share = features // cents
    video_of_slot, first, length, member = member_of_slots(
        length_ref, owner_ref, owners, capacity, frame_count
    )
    code = (code_ref[...] - EXACT).astype(f32)
    shifted = pltpu.roll(
        jnp.broadcast_to(code, (longest, frame_count)),
        frame_count - (longest - 1),
        1,
        stride=1,
        stride_axis=0,
    ).astype(bf16)
    at_start = jnp.concatenate(
        [
            ((iota((slots, LANES), 1) + at == first) & (length > 0)).astype(f32)
            for at in range(0, frame_count, LANES)
        ],
        axis=1,
    ).astype(bf16)
    slot_codes = dot_rows(shifted, at_start)
    rows = lambda ref: jnp.broadcast_to(ref[...], (longest, ref.shape[1])).astype(f32).astype(bf16)
    slot_length = dot_rows(rows(length_ref), video_of_slot)
    slot_cluster = dot_rows(rows(cluster_ref), video_of_slot)
    back = (longest - 1 - iota((longest, slots), 0)).astype(f32)
    slot_codes = jnp.where(back < slot_length, slot_codes, 2.0 * EXACT).astype(bf16)
    slot_cluster = jnp.where(slot_length > 0, slot_cluster, -1.0).astype(bf16)
    lane = iota((slots, owners * LANES), 1)
    place_owner, place_lane = lane // LANES, lane % LANES
    wanted = iota((slots, owners * LANES), 0) - place_owner * capacity
    code_lane = me * capacity
    cluster_lane = lax.rem(me + 1, cents) * capacity
    count_lane = lax.rem(me + 2, cents) * capacity
    inside = (wanted >= 0) & (wanted < capacity)
    place_codes = (inside & (place_lane == wanted + code_lane)).astype(f32).astype(bf16)
    place_cluster = (inside & (place_lane == wanted + cluster_lane)).astype(f32).astype(bf16)
    notes = dot(slot_codes, place_codes) + dot(slot_cluster, place_cluster)
    counts = dot(code_matches(code_ref, code_total), jnp.ones((frame_count, LANES), bf16))
    part = code_total // (owners * cents)
    note_lane = iota((part, LANES), 1)
    counted = (note_lane >= count_lane) & (note_lane < count_lane + capacity)
    for owner in range(owners):
        for cent in range(cents):
            at = (owner * cents + cent) * part
            note = jnp.where(
                counted, counts[at : at + part], notes[:, owner * LANES : (owner + 1) * LANES]
            )
            send_ref[owner, cent, 2 * capacity :, :] = note.astype(bf16)
    weight = 1.0 / jnp.maximum(length, 1.0)
    copy.wait()
    half = share // 2
    for cent in range(cents):
        sums = dot(member, frames_ref[:, cent * share : (cent + 1) * share])
        for side in range(2):
            pooled = (sums[:, side * half : (side + 1) * half] * weight).astype(bf16)
            send_ref[:, cent, side * capacity : (side + 1) * capacity, :] = pooled.reshape(
                owners, capacity, half
            )


def code_kernel(sizes, length_ref, owner_ref, code_ref, frames_hbm, pooled_ref, keep_ref, give_ref, frames_ref, sem):
    owners, cents, capacity, longest, code_total = sizes
    copy = pltpu.make_async_copy(frames_hbm, frames_ref, sem)
    copy.start()
    me = lax.axis_index("cent")
    frame_count, features = frames_hbm.shape
    share = features // cents
    slots = owners * capacity
    half = share // 2
    _, _, _, member = member_of_slots(length_ref, owner_ref, owners, capacity, frame_count)
    matches = code_matches(code_ref, code_total)
    slot_counts = dot_rows(matches, member).astype(bf16)
    copy.wait()
    for step in range(cents):
        cent = me ^ step
        columns = pl.ds(pl.multiple_of(cent * share, share), share)
        sums = dot(matches, frames_ref[:, columns])
        for side in range(2):
            pooled = pooled_ref[:, cent, side * capacity : (side + 1) * capacity, :].reshape(
                slots, half
            )
            lanes = slice(side * half, (side + 1) * half)
            centred = sums[:, lanes] - dot(slot_counts, pooled)
            if step % 2:
                give_ref[step // 2, :, lanes] = centred.astype(bf16)
            else:
                keep_ref[step // 2, :, lanes] = centred


def owner_kernel(sizes, got_ref, old_hbm, keep_ref, near_ref, far_ref, code_ref, new_ref, count_ref, old_ref, sem):
    owners, cents, capacity, longest, code_total = sizes
    me = lax.axis_index("cent")
    share = old_ref.shape[1]
    copy = pltpu.make_async_copy(
        old_hbm.at[:, pl.ds(pl.multiple_of(me * share, share), share)], old_ref, sem
    )
    copy.start()
    clusters = old_ref.shape[0]
    sources = owners * cents
    segment = iota((longest, LANES), 1) // capacity
    count = jnp.zeros((longest, LANES), f32)
    picks, slot_counts = [], []
    code_row = (iota((code_total, LANES), 0) - EXACT).astype(f32).astype(bf16)
    cluster_row = iota((clusters, LANES), 0).astype(f32).astype(bf16)
    for owner in range(owners):
        codes = jnp.zeros((longest, LANES), f32)
        cluster = jnp.zeros((longest, LANES), f32)
        for cent in range(cents):
            note = got_ref[owner * cents + cent, 2 * capacity :, :].astype(f32)
            codes = jnp.where(segment == cent, note, codes)
            cluster = jnp.where(segment == (cent + 1) % cents, note, cluster)
            count = count + jnp.where(segment == (cent + 2) % cents, note, 0.0)
        cluster = pltpu.roll(cluster, LANES - capacity, 1).astype(bf16)
        codes = codes.astype(bf16)
        picks.append((cluster_row == cluster[0:1]).astype(bf16))
        held = jnp.zeros((code_total, LANES), bf16)
        for row in range(longest):
            held = held + (code_row == codes[row : row + 1]).astype(bf16)
        slot_counts.append(held)
    for step in range(cents.bit_length() - 1):
        count = count + pltpu.roll(count, capacity << step, 1)
    count_ref[...] = count
    pick = jnp.concatenate(picks, axis=1)
    slot_count = jnp.concatenate(slot_counts, axis=1)
    rows = jnp.concatenate(
        [
            got_ref[:, side * capacity : (side + 1) * capacity, :].reshape(
                sources * capacity, share // 2
            )
            for side in range(2)
        ],
        axis=1,
    )
    sums = dot(pick, rows)
    number = dot(pick, jnp.ones((sources * capacity, LANES), bf16))
    number = jnp.concatenate([number] * (share // LANES), axis=1)
    copy.wait()
    new = (sums + old_ref[...].astype(f32)) / (number + 1.0)
    new_ref[...] = new
    anchor = new.astype(bf16)
    cluster_count = dot_rows(slot_count, pick)
    high = jnp.floor(cluster_count * (1.0 / EXACT))
    low = cluster_count - high * EXACT
    moved = dot(low.astype(bf16), anchor) + EXACT * dot(high.astype(bf16), anchor)
    total = keep_ref[0] + near_ref[0].astype(f32) + far_ref[...].astype(f32)
    total = total + (dot(slot_count, rows) - moved)
    code_ref[...] = total.astype(bf16)


def finish_kernel(sizes, got_ref, count_ref, old_ref, out_ref):
    owners, cents, capacity, longest, code_total = sizes
    share = got_ref.shape[2]
    prior = jnp.concatenate([count_ref[...] + code_prior] * (share // LANES), axis=1)
    for cent in range(cents):
        total = got_ref[cent].astype(f32)
        for owner in range(1, owners):
            total = total + got_ref[owner * cents + cent].astype(f32)
        lanes = slice(cent * share, (cent + 1) * share)
        out_ref[:, lanes] = (total + code_prior * old_ref[:, lanes]) / prior


def coarse_kernel(cents, own_ref, near_ref, far_ref, out_ref):
    me = lax.axis_index("cent")
    rows = out_ref.shape[0]
    share = own_ref.shape[1]
    put = lambda step, value: out_ref.__setitem__(
        (slice(None), pl.ds(pl.multiple_of((me ^ step) * share, share), share)), value
    )
    put(0, own_ref[pl.ds(pl.multiple_of(me * rows, rows), rows), :])
    put(1, near_ref[0])
    put(2, far_ref[0])
    put(3, far_ref[1])


def summed_body(frames, video_length, video_owner, video_cluster, frame_code, old_coarse, old_codes):
    owners = lax.axis_size("dp")
    cents = lax.axis_size("cent")
    frame_count, features = frames.shape
    videos = video_length.shape[1]
    clusters = old_coarse.shape[0]
    part = old_codes.shape[0]
    code_total = part * owners * cents
    capacity = max(2, 2 * videos // owners)
    longest = 2 * frame_count // videos
    share = features // cents
    devices = owners * cents
    sizes = (owners, cents, capacity, longest, code_total)
    me = lax.axis_index("cent")
    frame_code = frame_code.reshape(1, frame_count)
    vmem = pl.BlockSpec(memory_space=pltpu.VMEM)
    anywhere = pl.BlockSpec(memory_space=pl.ANY)
    params = pltpu.CompilerParams(vmem_limit_bytes=32 * 1024 * 1024)
    chunk = 2 * capacity + longest
    swap = lambda array, bit: lax.ppermute(
        array, "cent", [(index, index ^ bit) for index in range(cents)]
    )
    frames_scratch = [pltpu.VMEM((frame_count, features), bf16), pltpu.SemaphoreType.DMA]
    send = pl.pallas_call(
        functools.partial(pool_kernel, sizes),
        out_shape=jax.ShapeDtypeStruct((owners, cents, chunk, share // 2), bf16),
        in_specs=[vmem] * 4 + [anywhere],
        out_specs=vmem,
        scratch_shapes=frames_scratch,
        compiler_params=params,
        name="pool",
    )(video_length, video_owner, video_cluster, frame_code, frames)
    got = lax.all_to_all(
        send.reshape(devices, chunk, share // 2), ("dp", "cent"), 0, 0, tiled=True
    )
    keep, give = pl.pallas_call(
        functools.partial(code_kernel, sizes),
        out_shape=(
            jax.ShapeDtypeStruct((cents // 2, code_total, share), f32),
            jax.ShapeDtypeStruct((cents // 2, code_total, share), bf16),
        ),
        in_specs=[vmem] * 3 + [anywhere, vmem],
        out_specs=(vmem, vmem),
        scratch_shapes=frames_scratch,
        compiler_params=params,
        cost_estimate=pl.CostEstimate(
            flops=3 * code_total * frame_count * features,
            bytes_accessed=6 * frame_count * features,
            transcendentals=0,
        ),
        name="codes",
    )(video_length, video_owner, frame_code, frames, send)
    near = swap(give, 1)
    far = swap((keep[1] + near[1].astype(f32)).astype(bf16), 2)
    sums, new, count = pl.pallas_call(
        functools.partial(owner_kernel, sizes),
        out_shape=(
            jax.ShapeDtypeStruct((code_total, share), bf16),
            jax.ShapeDtypeStruct((clusters, share), f32),
            jax.ShapeDtypeStruct((part, LANES), f32),
        ),
        in_specs=[vmem, anywhere, vmem, vmem, vmem],
        out_specs=(vmem, vmem, vmem),
        scratch_shapes=[pltpu.VMEM((clusters, share), bf16), pltpu.SemaphoreType.DMA],
        compiler_params=params,
        name="owner",
    )(got, old_coarse, keep, near, far)
    last = lax.all_to_all(sums.reshape(devices, part, share), ("dp", "cent"), 0, 0, tiled=True)
    quarter = clusters // cents
    rows_of = lambda step: lax.dynamic_slice_in_dim(new, (me ^ step) * quarter, quarter, 0)
    beside = swap(jnp.stack([rows_of(1), rows_of(3)]), 1)
    across = swap(jnp.stack([rows_of(2), beside[1]]), 2)
    new_coarse = pl.pallas_call(
        functools.partial(coarse_kernel, cents),
        out_shape=jax.ShapeDtypeStruct((quarter, features), f32),
        in_specs=[vmem] * 3,
        out_specs=vmem,
        compiler_params=params,
        name="coarse",
    )(new, beside, across)
    new_codes = pl.pallas_call(
        functools.partial(finish_kernel, sizes),
        out_shape=jax.ShapeDtypeStruct((part, features), f32),
        in_specs=[vmem] * 3,
        out_specs=vmem,
        compiler_params=params,
        name="finish",
    )(last, count, old_codes)
    return new_coarse, new_codes


def owner_slots(target, target_count, capacity):
    matches = (target[:, None] == jnp.arange(target_count, dtype=jnp.int32)[None, :]).astype(
        jnp.int32
    )
    before = jnp.cumsum(matches, axis=0) - matches
    slot_rank = jnp.sum(before * matches, axis=1)
    return target * capacity + slot_rank


def invert_slots(slot_list, slot_total):
    item_index = jnp.arange(slot_list.shape[0], dtype=jnp.int32)
    source = jnp.zeros((slot_total,), jnp.int32).at[slot_list].set(item_index)
    filled = jnp.zeros((slot_total,), jnp.int32).at[slot_list].set(1)
    return (source, filled)


def routed_body(frames, video_length, video_owner, video_cluster, frame_code, old_coarse, old_codes):
    dp_count = lax.axis_size("dp")
    cent_count = lax.axis_size("cent")
    frame_count, features = frames.shape
    video_count = video_length.shape[1]
    coarse_rows = old_coarse.shape[0]
    code_share = old_codes.shape[0]
    code_block = code_share * cent_count
    cap_video = max(2, 2 * video_count // dp_count)
    cap_frame = max(2, 2 * frame_count // dp_count)
    lengths = video_length[0]
    target = video_owner[0]
    cluster = video_cluster[0]
    video_ends = jnp.cumsum(lengths)
    video_starts = video_ends - lengths
    position = jnp.arange(frame_count, dtype=jnp.int32)
    member = (
        (position[None, :] >= video_starts[:, None]) & (position[None, :] < video_ends[:, None])
    ).astype(jnp.bfloat16)
    video_sums = jnp.dot(member, frames, preferred_element_type=jnp.float32)
    pooled = (video_sums / lengths[:, None].astype(jnp.float32)).astype(jnp.bfloat16)
    video_slot = owner_slots(target, dp_count, cap_video)
    source, filled = invert_slots(video_slot, dp_count * cap_video)
    send_rows = jnp.where(filled[:, None] > 0, pooled[source], jnp.zeros((), jnp.bfloat16))
    send_codes = jnp.where(filled > 0, cluster[source], -1)
    got_rows, got_codes = (
        lax.all_to_all(
            send_rows.reshape(dp_count, cap_video, features),
            "dp",
            split_axis=0,
            concat_axis=0,
            tiled=True,
        ),
        lax.all_to_all(
            send_codes.reshape(dp_count, cap_video), "dp", split_axis=0, concat_axis=0, tiled=True
        ),
    )
    got_rows = got_rows.reshape(-1, features)
    got_codes = got_codes.reshape(-1)
    table_index = jnp.arange(coarse_rows, dtype=jnp.int32)
    coarse_pick = (got_codes[None, :] == table_index[:, None]).astype(jnp.bfloat16)
    coarse_sum = jnp.dot(coarse_pick, got_rows, preferred_element_type=jnp.float32)
    coarse_count = jnp.sum(coarse_pick.astype(jnp.float32), axis=1)
    quarter = coarse_rows // cent_count
    part_sum, part_count = (
        lax.psum_scatter(coarse_sum, "cent", scatter_dimension=0, tiled=True),
        lax.psum_scatter(coarse_count, "cent", scatter_dimension=0, tiled=True),
    )
    first_row = lax.axis_index("cent") * quarter
    old_part = lax.dynamic_slice_in_dim(old_coarse, first_row, quarter, 0).astype(jnp.float32)
    new_coarse = (part_sum + old_part) / (part_count[:, None] + 1.0)
    anchor_table = lax.all_gather(new_coarse.astype(jnp.bfloat16), "cent", axis=0, tiled=True)
    slot_anchor = jnp.dot(coarse_pick.T, anchor_table, preferred_element_type=jnp.float32).astype(
        jnp.bfloat16
    )
    returned = lax.all_to_all(
        slot_anchor.reshape(dp_count, cap_video, features),
        "dp",
        split_axis=0,
        concat_axis=0,
        tiled=True,
    )
    video_anchor = returned.reshape(-1, features)[video_slot]
    frame_anchor = jnp.dot(member.T, video_anchor, preferred_element_type=jnp.float32)
    residual = (frames - frame_anchor).astype(jnp.bfloat16)
    code_target = frame_code // code_block
    code_offset = frame_code - code_target * code_block
    frame_slot = owner_slots(code_target, dp_count, cap_frame)
    source, filled = invert_slots(frame_slot, dp_count * cap_frame)
    slot_rows = jnp.where(filled[:, None] > 0, residual[source], jnp.zeros((), jnp.bfloat16))
    slot_codes = jnp.where(filled > 0, code_offset[source], -1)
    code_rows, code_ids = (
        lax.all_to_all(
            slot_rows.reshape(dp_count, cap_frame, features),
            "dp",
            split_axis=0,
            concat_axis=0,
            tiled=True,
        ),
        lax.all_to_all(
            slot_codes.reshape(dp_count, cap_frame), "dp", split_axis=0, concat_axis=0, tiled=True
        ),
    )
    code_index = jnp.arange(code_block, dtype=jnp.int32)
    code_pick = (code_ids.reshape(-1)[None, :] == code_index[:, None]).astype(jnp.bfloat16)
    code_sum = jnp.dot(
        code_pick, code_rows.reshape(-1, features), preferred_element_type=jnp.float32
    )
    code_count = jnp.sum(code_pick.astype(jnp.float32), axis=1)
    own_sum, own_count = (
        lax.psum_scatter(code_sum, "cent", scatter_dimension=0, tiled=True),
        lax.psum_scatter(code_count, "cent", scatter_dimension=0, tiled=True),
    )
    new_codes = (own_sum + code_prior * old_codes) / (own_count[:, None] + code_prior)
    return (new_coarse, new_codes)


def choose(mesh):
    owners, cents = mesh.shape["dp"], mesh.shape["cent"]

    def body(*arrays):
        frame_count, features = arrays[0].shape
        videos = arrays[1].shape[1]
        part = arrays[6].shape[0]
        small = (
            part * owners * cents <= 2 * EXACT
            and arrays[5].shape[0] <= EXACT
            and cents == 4
            and cents * max(2, 2 * videos // owners) == LANES
            and part == 2 * frame_count // videos
            and features % (2 * cents * LANES) == 0
        )
        return (summed_body if small else routed_body)(*arrays)

    return body


def solution(mesh):
    placed = (
        P(("dp", "cent"), None),
        P(("dp", "cent"), None),
        P(("dp", "cent"), None),
        P(("dp", "cent"), None),
        P(("dp", "cent")),
        P("dp", None),
        P(("dp", "cent"), None),
    )
    return jax.shard_map(
        choose(mesh),
        mesh=mesh,
        in_specs=placed,
        out_specs=(P(("dp", "cent"), None), P(("dp", "cent"), None)),
        check_vma=False,
    )
```

```python
import functools

import jax
import jax.numpy as jnp
from jax import lax
from jax.experimental import pallas as pl
from jax.experimental.pallas import tpu as pltpu
from jax.sharding import PartitionSpec as P

code_prior = 16.0
LANES = 128
EXACT = 256
f32 = jnp.float32
bf16 = jnp.bfloat16


def iota(shape, axis):
    return lax.broadcasted_iota(jnp.int32, shape, axis)


def ones_where(mask):
    return jnp.where(mask, jnp.ones((), bf16), jnp.zeros((), bf16))


def fetch(sources, targets, sems):
    copies = [
        pltpu.make_async_copy(source, target, sems.at[at])
        for at, (source, target) in enumerate(zip(sources, targets))
    ]
    for copy in copies:
        copy.start()
    return copies


def dot(left, right):
    return jnp.dot(left, right, preferred_element_type=f32)


def dot_rows(left, right):
    return lax.dot_general(left, right, (((1,), (1,)), ((), ())), preferred_element_type=f32)


def member_of_slots(length_ref, owner_ref, owners, capacity, frame_count):
    videos = length_ref.shape[1]
    slots = owners * capacity
    lengths = length_ref[...].astype(f32)
    owner = owner_ref[...]
    match = (iota((owners, videos), 0) == owner).astype(f32)
    earlier = (iota((videos, videos), 0) < iota((videos, videos), 1)).astype(bf16)
    stacked = jnp.concatenate([match, jnp.broadcast_to(lengths, (8, videos))], axis=0)
    before = dot(stacked.astype(bf16), earlier)
    rank = jnp.sum(before[:owners] * match, axis=0, keepdims=True)
    starts = before[owners : owners + 1]
    slot = owner * capacity + rank.astype(jnp.int32)
    video_of_slot = (iota((slots, videos), 0) == slot).astype(f32).astype(bf16)
    high = jnp.floor(starts / 16.0) * 16.0
    low = starts - high
    tall = lambda row: jnp.broadcast_to(row, (LANES, videos)).astype(bf16)
    start = dot_rows(video_of_slot, tall(high)) + dot_rows(video_of_slot, tall(low))
    length = dot_rows(video_of_slot, tall(lengths))
    first, last = start.astype(jnp.int32), (start + length).astype(jnp.int32)
    member = jnp.concatenate(
        [
            (
                (iota((slots, LANES), 1) + at >= first) & (iota((slots, LANES), 1) + at < last)
            ).astype(f32)
            for at in range(0, frame_count, LANES)
        ],
        axis=1,
    ).astype(bf16)
    return video_of_slot, first, length, member


def code_matches(code_ref, code_total):
    frame_count = code_ref.shape[1]
    return (iota((code_total, frame_count), 0) == code_ref[...]).astype(f32).astype(bf16)


def pool_kernel(sizes, length_hbm, owner_hbm, cluster_hbm, code_hbm, frames_hbm, send_ref, *scratch):
    owners, cents, capacity, longest, code_total = sizes
    length_ref, owner_ref, cluster_ref, code_ref, frames_ref, sems = scratch
    copies = fetch(
        (length_hbm, owner_hbm, cluster_hbm, code_hbm, frames_hbm), scratch[:-1], sems
    )
    me = lax.axis_index("cent")
    frame_count, features = frames_hbm.shape
    for copy in copies[:-1]:
        copy.wait()
    slots = owners * capacity
    share = features // cents
    video_of_slot, first, length, member = member_of_slots(
        length_ref, owner_ref, owners, capacity, frame_count
    )
    code = (code_ref[...] - EXACT).astype(f32)
    shifted = pltpu.roll(
        jnp.broadcast_to(code, (longest, frame_count)),
        frame_count - (longest - 1),
        1,
        stride=1,
        stride_axis=0,
    ).astype(bf16)
    at_start = jnp.concatenate(
        [
            ((iota((slots, LANES), 1) + at == first) & (length > 0)).astype(f32)
            for at in range(0, frame_count, LANES)
        ],
        axis=1,
    ).astype(bf16)
    slot_codes = dot_rows(shifted, at_start)
    rows = lambda ref: jnp.broadcast_to(ref[...], (longest, ref.shape[1])).astype(f32).astype(bf16)
    slot_length = dot_rows(rows(length_ref), video_of_slot)
    slot_cluster = dot_rows(rows(cluster_ref), video_of_slot)
    back = (longest - 1 - iota((longest, slots), 0)).astype(f32)
    slot_codes = jnp.where(back < slot_length, slot_codes, 2.0 * EXACT).astype(bf16)
    slot_cluster = jnp.where(slot_length > 0, slot_cluster, -1.0).astype(bf16)
    lane = iota((slots, owners * LANES), 1)
    place_owner, place_lane = lane // LANES, lane % LANES
    wanted = iota((slots, owners * LANES), 0) - place_owner * capacity
    code_lane = me * capacity
    cluster_lane = lax.rem(me + 1, cents) * capacity
    count_lane = lax.rem(me + 2, cents) * capacity
    inside = (wanted >= 0) & (wanted < capacity)
    place_codes = (inside & (place_lane == wanted + code_lane)).astype(f32).astype(bf16)
    place_cluster = (inside & (place_lane == wanted + cluster_lane)).astype(f32).astype(bf16)
    notes = dot(slot_codes, place_codes) + dot(slot_cluster, place_cluster)
    counts = dot(code_matches(code_ref, code_total), jnp.ones((frame_count, LANES), bf16))
    part = code_total // (owners * cents)
    note_lane = iota((part, LANES), 1)
    counted = (note_lane >= count_lane) & (note_lane < count_lane + capacity)
    for owner in range(owners):
        for cent in range(cents):
            at = (owner * cents + cent) * part
            note = jnp.where(
                counted, counts[at : at + part], notes[:, owner * LANES : (owner + 1) * LANES]
            )
            send_ref[owner, cent, 2 * capacity :, :] = note.astype(bf16)
    weight = 1.0 / jnp.maximum(length, 1.0)
    copies[-1].wait()
    half = share // 2
    for cent in range(cents):
        sums = dot(member, frames_ref[:, cent * share : (cent + 1) * share])
        for side in range(2):
            pooled = (sums[:, side * half : (side + 1) * half] * weight).astype(bf16)
            send_ref[:, cent, side * capacity : (side + 1) * capacity, :] = pooled.reshape(
                owners, capacity, half
            )


def code_kernel(sizes, length_hbm, owner_hbm, code_hbm, frames_hbm, pooled_ref, keep_ref, give_ref, *scratch):
    owners, cents, capacity, longest, code_total = sizes
    length_ref, owner_ref, code_ref, frames_ref, sems = scratch
    copies = fetch((length_hbm, owner_hbm, code_hbm, frames_hbm), scratch[:-1], sems)
    me = lax.axis_index("cent")
    for copy in copies[:-1]:
        copy.wait()
    frame_count, features = frames_hbm.shape
    share = features // cents
    slots = owners * capacity
    half = share // 2
    _, _, _, member = member_of_slots(length_ref, owner_ref, owners, capacity, frame_count)
    matches = code_matches(code_ref, code_total)
    slot_counts = dot_rows(matches, member).astype(bf16)
    copies[-1].wait()
    for step in range(cents):
        cent = me ^ step
        columns = pl.ds(pl.multiple_of(cent * share, share), share)
        sums = dot(matches, frames_ref[:, columns])
        for side in range(2):
            pooled = pooled_ref[:, cent, side * capacity : (side + 1) * capacity, :].reshape(
                slots, half
            )
            lanes = slice(side * half, (side + 1) * half)
            centred = sums[:, lanes] - dot(slot_counts, pooled)
            if step % 2:
                give_ref[step // 2, :, lanes] = centred.astype(bf16)
            else:
                keep_ref[step // 2, :, lanes] = centred


def slot_rows(got_ref, capacity):
    sources, _, half = got_ref.shape
    return jnp.concatenate(
        [
            got_ref[:, side * capacity : (side + 1) * capacity, :].reshape(sources * capacity, half)
            for side in range(2)
        ],
        axis=1,
    )


def cluster_picks(sizes, got_ref, clusters):
    owners, cents, capacity, longest, code_total = sizes
    segment = iota((longest, LANES), 1) // capacity
    cluster_row = iota((clusters, LANES), 0).astype(f32).astype(bf16)
    picks = []
    for owner in range(owners):
        cluster = jnp.zeros((longest, LANES), f32)
        for cent in range(cents):
            note = got_ref[owner * cents + cent, 2 * capacity :, :].astype(f32)
            cluster = jnp.where(segment == (cent + 1) % cents, note, cluster)
        cluster = pltpu.roll(cluster, LANES - capacity, 1).astype(bf16)
        picks.append(ones_where(cluster_row == cluster[0:1]))
    return jnp.concatenate(picks, axis=1)


def coarse_kernel(sizes, got_ref, old_hbm, across_ref, here_ref, beside_ref, anchor_ref, old_ref, new_ref, sems):
    owners, cents, capacity, longest, code_total = sizes
    me = lax.axis_index("cent")
    clusters, share = old_ref.shape
    columns = pl.ds(pl.multiple_of(me * share, share), share)
    copies = fetch((old_hbm.at[:, columns],), (old_ref,), sems)
    pick = cluster_picks(sizes, got_ref, clusters)
    rows = slot_rows(got_ref, capacity)
    sums = dot(pick, rows)
    number = dot(pick, jnp.ones((rows.shape[0], LANES), bf16))
    number = jnp.concatenate([number] * (share // LANES), axis=1)
    copies[0].wait()
    new = (sums + old_ref[...].astype(f32)) / (number + 1.0)
    anchor_ref[...] = new.astype(bf16)
    new_ref[...] = new
    quarter = clusters // cents
    rows_of = lambda step: new_ref[pl.ds(pl.multiple_of((me ^ step) * quarter, quarter), quarter), :]
    across_ref[0] = rows_of(2)
    across_ref[1] = rows_of(3)
    here_ref[...] = rows_of(0)
    beside_ref[...] = rows_of(1)


def owner_kernel(sizes, got_ref, anchor_ref, keep_ref, near_ref, far_ref, code_ref, count_ref):
    owners, cents, capacity, longest, code_total = sizes
    segment = iota((longest, LANES), 1) // capacity
    count = jnp.zeros((longest, LANES), f32)
    slot_counts = []
    code_row = (iota((code_total, LANES), 0) - EXACT).astype(f32).astype(bf16)
    for owner in range(owners):
        codes = jnp.zeros((longest, LANES), f32)
        for cent in range(cents):
            note = got_ref[owner * cents + cent, 2 * capacity :, :].astype(f32)
            codes = jnp.where(segment == cent, note, codes)
            count = count + jnp.where(segment == (cent + 2) % cents, note, 0.0)
        codes = codes.astype(bf16)
        held = jnp.zeros((code_total, LANES), bf16)
        for row in range(longest):
            held = held + ones_where(code_row == codes[row : row + 1])
        slot_counts.append(held)
    for step in range(cents.bit_length() - 1):
        count = count + pltpu.roll(count, capacity << step, 1)
    count_ref[...] = count
    slot_count = jnp.concatenate(slot_counts, axis=1)
    pick = cluster_picks(sizes, got_ref, anchor_ref.shape[0])
    anchor = anchor_ref[...]
    cluster_count = dot_rows(slot_count, pick)
    high = jnp.floor(cluster_count * (1.0 / EXACT))
    low = cluster_count - high * EXACT
    moved = dot(low.astype(bf16), anchor) + EXACT * dot(high.astype(bf16), anchor)
    total = keep_ref[0] + near_ref[0].astype(f32) + far_ref[...].astype(f32)
    total = total + (dot(slot_count, slot_rows(got_ref, capacity)) - moved)
    code_ref[...] = total.astype(bf16)


def finish_kernel(sizes, got_ref, count_ref, old_ref, out_ref):
    owners, cents, capacity, longest, code_total = sizes
    share = got_ref.shape[2]
    prior = jnp.concatenate([count_ref[...] + code_prior] * (share // LANES), axis=1)
    for cent in range(cents):
        total = got_ref[cent].astype(f32)
        for owner in range(1, owners):
            total = total + got_ref[owner * cents + cent].astype(f32)
        lanes = slice(cent * share, (cent + 1) * share)
        out_ref[:, lanes] = (total + code_prior * old_ref[:, lanes]) / prior


def join_kernel(here_ref, across_ref, near_ref, far_ref, out_ref):
    me = lax.axis_index("cent")
    share = here_ref.shape[1]
    for step, value in enumerate((here_ref[...], near_ref[...], across_ref[0], far_ref[...])):
        out_ref[:, pl.ds(pl.multiple_of((me ^ step) * share, share), share)] = value


def summed_body(frames, video_length, video_owner, video_cluster, frame_code, old_coarse, old_codes):
    owners = lax.axis_size("dp")
    cents = lax.axis_size("cent")
    frame_count, features = frames.shape
    videos = video_length.shape[1]
    clusters = old_coarse.shape[0]
    part = old_codes.shape[0]
    code_total = part * owners * cents
    capacity = max(2, 2 * videos // owners)
    longest = 2 * frame_count // videos
    share = features // cents
    devices = owners * cents
    sizes = (owners, cents, capacity, longest, code_total)
    frame_code = frame_code.reshape(1, frame_count)
    vmem = pl.BlockSpec(memory_space=pltpu.VMEM)
    hbm = pl.BlockSpec(memory_space=pltpu.HBM)
    params = pltpu.CompilerParams(vmem_limit_bytes=32 * 1024 * 1024)
    chunk = 2 * capacity + longest
    stay = lambda array: pltpu.with_memory_space_constraint(array, pltpu.HBM)
    swap = lambda array, bit: lax.ppermute(
        array, "cent", [(index, index ^ bit) for index in range(cents)]
    )
    row = lambda length: pltpu.VMEM((1, length), jnp.int32)
    frames_scratch = [row(frame_count), pltpu.VMEM((frame_count, features), bf16)]
    quarter = clusters // cents
    send = pl.pallas_call(
        functools.partial(pool_kernel, sizes),
        out_shape=jax.ShapeDtypeStruct((owners, cents, chunk, share // 2), bf16),
        in_specs=[hbm] * 5,
        out_specs=vmem,
        scratch_shapes=[row(videos)] * 3 + frames_scratch + [pltpu.SemaphoreType.DMA((5,))],
        compiler_params=params,
        name="pool",
    )(*map(stay, (video_length, video_owner, video_cluster, frame_code, frames)))
    got = lax.all_to_all(
        send.reshape(devices, chunk, share // 2), ("dp", "cent"), 0, 0, tiled=True
    )
    keep, give = pl.pallas_call(
        functools.partial(code_kernel, sizes),
        out_shape=(
            jax.ShapeDtypeStruct((cents // 2, code_total, share), f32),
            jax.ShapeDtypeStruct((cents // 2, code_total, share), bf16),
        ),
        in_specs=[hbm] * 4 + [vmem],
        out_specs=(vmem, vmem),
        scratch_shapes=[row(videos)] * 2 + frames_scratch + [pltpu.SemaphoreType.DMA((4,))],
        compiler_params=params,
        cost_estimate=pl.CostEstimate(
            flops=3 * code_total * frame_count * features,
            bytes_accessed=6 * frame_count * features,
            transcendentals=0,
        ),
        name="codes",
    )(*map(stay, (video_length, video_owner, frame_code, frames)), send)
    near = swap(give, 1)
    far = swap((keep[1] + near[1].astype(f32)).astype(bf16), 2)
    piece = jax.ShapeDtypeStruct((quarter, share), f32)
    across, here, beside, anchor = pl.pallas_call(
        functools.partial(coarse_kernel, sizes),
        out_shape=(
            jax.ShapeDtypeStruct((2, quarter, share), f32),
            piece,
            piece,
            jax.ShapeDtypeStruct((clusters, share), bf16),
        ),
        in_specs=[vmem, hbm],
        out_specs=(vmem,) * 4,
        scratch_shapes=[
            pltpu.VMEM((clusters, share), bf16),
            pltpu.VMEM((clusters, share), f32),
            pltpu.SemaphoreType.DMA((1,)),
        ],
        compiler_params=params,
        name="coarse",
    )(got, stay(old_coarse))
    across = swap(across, 2)
    sums, count = pl.pallas_call(
        functools.partial(owner_kernel, sizes),
        out_shape=(
            jax.ShapeDtypeStruct((code_total, share), bf16),
            jax.ShapeDtypeStruct((part, LANES), f32),
        ),
        in_specs=[vmem] * 5,
        out_specs=(vmem, vmem),
        compiler_params=params,
        cost_estimate=pl.CostEstimate(
            flops=4 * code_total * devices * capacity * share,
            bytes_accessed=6 * code_total * share,
            transcendentals=0,
        ),
        name="owner",
    )(got, anchor, keep, near, far)
    last = lax.all_to_all(sums.reshape(devices, part, share), ("dp", "cent"), 0, 0, tiled=True)
    new_coarse = pl.pallas_call(
        join_kernel,
        out_shape=jax.ShapeDtypeStruct((quarter, features), f32),
        in_specs=[vmem] * 4,
        out_specs=vmem,
        compiler_params=params,
        name="join",
    )(here, across, swap(beside, 1), swap(across[1], 1))
    new_codes = pl.pallas_call(
        functools.partial(finish_kernel, sizes),
        out_shape=jax.ShapeDtypeStruct((part, features), f32),
        in_specs=[vmem] * 3,
        out_specs=vmem,
        compiler_params=params,
        name="finish",
    )(last, count, old_codes)
    return new_coarse, new_codes


def owner_slots(target, target_count, capacity):
    matches = (target[:, None] == jnp.arange(target_count, dtype=jnp.int32)[None, :]).astype(
        jnp.int32
    )
    before = jnp.cumsum(matches, axis=0) - matches
    slot_rank = jnp.sum(before * matches, axis=1)
    return target * capacity + slot_rank


def invert_slots(slot_list, slot_total):
    item_index = jnp.arange(slot_list.shape[0], dtype=jnp.int32)
    source = jnp.zeros((slot_total,), jnp.int32).at[slot_list].set(item_index)
    filled = jnp.zeros((slot_total,), jnp.int32).at[slot_list].set(1)
    return (source, filled)


def routed_body(frames, video_length, video_owner, video_cluster, frame_code, old_coarse, old_codes):
    dp_count = lax.axis_size("dp")
    cent_count = lax.axis_size("cent")
    frame_count, features = frames.shape
    video_count = video_length.shape[1]
    coarse_rows = old_coarse.shape[0]
    code_share = old_codes.shape[0]
    code_block = code_share * cent_count
    cap_video = max(2, 2 * video_count // dp_count)
    cap_frame = max(2, 2 * frame_count // dp_count)
    lengths = video_length[0]
    target = video_owner[0]
    cluster = video_cluster[0]
    video_ends = jnp.cumsum(lengths)
    video_starts = video_ends - lengths
    position = jnp.arange(frame_count, dtype=jnp.int32)
    member = (
        (position[None, :] >= video_starts[:, None]) & (position[None, :] < video_ends[:, None])
    ).astype(jnp.bfloat16)
    video_sums = jnp.dot(member, frames, preferred_element_type=jnp.float32)
    pooled = (video_sums / lengths[:, None].astype(jnp.float32)).astype(jnp.bfloat16)
    video_slot = owner_slots(target, dp_count, cap_video)
    source, filled = invert_slots(video_slot, dp_count * cap_video)
    send_rows = jnp.where(filled[:, None] > 0, pooled[source], jnp.zeros((), jnp.bfloat16))
    send_codes = jnp.where(filled > 0, cluster[source], -1)
    got_rows, got_codes = (
        lax.all_to_all(
            send_rows.reshape(dp_count, cap_video, features),
            "dp",
            split_axis=0,
            concat_axis=0,
            tiled=True,
        ),
        lax.all_to_all(
            send_codes.reshape(dp_count, cap_video), "dp", split_axis=0, concat_axis=0, tiled=True
        ),
    )
    got_rows = got_rows.reshape(-1, features)
    got_codes = got_codes.reshape(-1)
    table_index = jnp.arange(coarse_rows, dtype=jnp.int32)
    coarse_pick = (got_codes[None, :] == table_index[:, None]).astype(jnp.bfloat16)
    coarse_sum = jnp.dot(coarse_pick, got_rows, preferred_element_type=jnp.float32)
    coarse_count = jnp.sum(coarse_pick.astype(jnp.float32), axis=1)
    quarter = coarse_rows // cent_count
    part_sum, part_count = (
        lax.psum_scatter(coarse_sum, "cent", scatter_dimension=0, tiled=True),
        lax.psum_scatter(coarse_count, "cent", scatter_dimension=0, tiled=True),
    )
    first_row = lax.axis_index("cent") * quarter
    old_part = lax.dynamic_slice_in_dim(old_coarse, first_row, quarter, 0).astype(jnp.float32)
    new_coarse = (part_sum + old_part) / (part_count[:, None] + 1.0)
    anchor_table = lax.all_gather(new_coarse.astype(jnp.bfloat16), "cent", axis=0, tiled=True)
    slot_anchor = jnp.dot(coarse_pick.T, anchor_table, preferred_element_type=jnp.float32).astype(
        jnp.bfloat16
    )
    returned = lax.all_to_all(
        slot_anchor.reshape(dp_count, cap_video, features),
        "dp",
        split_axis=0,
        concat_axis=0,
        tiled=True,
    )
    video_anchor = returned.reshape(-1, features)[video_slot]
    frame_anchor = jnp.dot(member.T, video_anchor, preferred_element_type=jnp.float32)
    residual = (frames - frame_anchor).astype(jnp.bfloat16)
    code_target = frame_code // code_block
    code_offset = frame_code - code_target * code_block
    frame_slot = owner_slots(code_target, dp_count, cap_frame)
    source, filled = invert_slots(frame_slot, dp_count * cap_frame)
    slot_rows = jnp.where(filled[:, None] > 0, residual[source], jnp.zeros((), jnp.bfloat16))
    slot_codes = jnp.where(filled > 0, code_offset[source], -1)
    code_rows, code_ids = (
        lax.all_to_all(
            slot_rows.reshape(dp_count, cap_frame, features),
            "dp",
            split_axis=0,
            concat_axis=0,
            tiled=True,
        ),
        lax.all_to_all(
            slot_codes.reshape(dp_count, cap_frame), "dp", split_axis=0, concat_axis=0, tiled=True
        ),
    )
    code_index = jnp.arange(code_block, dtype=jnp.int32)
    code_pick = (code_ids.reshape(-1)[None, :] == code_index[:, None]).astype(jnp.bfloat16)
    code_sum = jnp.dot(
        code_pick, code_rows.reshape(-1, features), preferred_element_type=jnp.float32
    )
    code_count = jnp.sum(code_pick.astype(jnp.float32), axis=1)
    own_sum, own_count = (
        lax.psum_scatter(code_sum, "cent", scatter_dimension=0, tiled=True),
        lax.psum_scatter(code_count, "cent", scatter_dimension=0, tiled=True),
    )
    new_codes = (own_sum + code_prior * old_codes) / (own_count[:, None] + code_prior)
    return (new_coarse, new_codes)


def choose(mesh):
    owners, cents = mesh.shape["dp"], mesh.shape["cent"]

    def body(*arrays):
        frame_count, features = arrays[0].shape
        videos = arrays[1].shape[1]
        part = arrays[6].shape[0]
        small = (
            part * owners * cents <= 2 * EXACT
            and arrays[5].shape[0] <= EXACT
            and cents == 4
            and cents * max(2, 2 * videos // owners) == LANES
            and part == 2 * frame_count // videos
            and features % (2 * cents * LANES) == 0
        )
        return (summed_body if small else routed_body)(*arrays)

    return body


def solution(mesh):
    placed = (
        P(("dp", "cent"), None),
        P(("dp", "cent"), None),
        P(("dp", "cent"), None),
        P(("dp", "cent"), None),
        P(("dp", "cent")),
        P("dp", None),
        P(("dp", "cent"), None),
    )
    return jax.shard_map(
        choose(mesh),
        mesh=mesh,
        in_specs=placed,
        out_specs=(P(("dp", "cent"), None), P(("dp", "cent"), None)),
        check_vma=False,
    )
```

```python
import functools

import jax
import jax.numpy as jnp
from jax import lax
from jax.experimental import pallas as pl
from jax.experimental.pallas import tpu as pltpu
from jax.sharding import PartitionSpec as P

code_prior = 16.0
LANES = 128
EXACT = 256
f32 = jnp.float32
bf16 = jnp.bfloat16


def iota(shape, axis):
    return lax.broadcasted_iota(jnp.int32, shape, axis)


def ones_where(mask):
    return jnp.where(mask, jnp.ones((), bf16), jnp.zeros((), bf16))


def fetch(sources, targets, sems):
    copies = [
        pltpu.make_async_copy(source, target, sems.at[at])
        for at, (source, target) in enumerate(zip(sources, targets))
    ]
    for copy in copies:
        copy.start()
    return copies


def dot(left, right):
    return jnp.dot(left, right, preferred_element_type=f32)


def dot_rows(left, right):
    return lax.dot_general(left, right, (((1,), (1,)), ((), ())), preferred_element_type=f32)


def member_of_slots(length_ref, owner_ref, owners, capacity, frame_count):
    videos = length_ref.shape[1]
    slots = owners * capacity
    lengths = length_ref[...].astype(f32)
    owner = owner_ref[...]
    match = (iota((owners, videos), 0) == owner).astype(f32)
    earlier = (iota((videos, videos), 0) < iota((videos, videos), 1)).astype(bf16)
    stacked = jnp.concatenate([match, jnp.broadcast_to(lengths, (8, videos))], axis=0)
    before = dot(stacked.astype(bf16), earlier)
    rank = jnp.sum(before[:owners] * match, axis=0, keepdims=True)
    starts = before[owners : owners + 1]
    slot = owner * capacity + rank.astype(jnp.int32)
    video_of_slot = (iota((slots, videos), 0) == slot).astype(f32).astype(bf16)
    high = jnp.floor(starts / 16.0) * 16.0
    low = starts - high
    tall = lambda row: jnp.broadcast_to(row, (LANES, videos)).astype(bf16)
    start = dot_rows(video_of_slot, tall(high)) + dot_rows(video_of_slot, tall(low))
    length = dot_rows(video_of_slot, tall(lengths))
    first, last = start.astype(jnp.int32), (start + length).astype(jnp.int32)
    member = jnp.concatenate(
        [
            (
                (iota((slots, LANES), 1) + at >= first) & (iota((slots, LANES), 1) + at < last)
            ).astype(f32)
            for at in range(0, frame_count, LANES)
        ],
        axis=1,
    ).astype(bf16)
    return video_of_slot, first, length, member


def code_matches(code_ref, code_total):
    frame_count = code_ref.shape[1]
    return (iota((code_total, frame_count), 0) == code_ref[...]).astype(f32).astype(bf16)


def pool_kernel(sizes, length_hbm, owner_hbm, cluster_hbm, code_hbm, frames_hbm, send_ref, *scratch):
    owners, cents, capacity, longest, code_total = sizes
    length_ref, owner_ref, cluster_ref, code_ref, frames_ref, sems = scratch
    copies = fetch(
        (length_hbm, owner_hbm, cluster_hbm, code_hbm, frames_hbm), scratch[:-1], sems
    )
    me = lax.axis_index("cent")
    frame_count, features = frames_hbm.shape
    for copy in copies[:-1]:
        copy.wait()
    slots = owners * capacity
    share = features // cents
    video_of_slot, first, length, member = member_of_slots(
        length_ref, owner_ref, owners, capacity, frame_count
    )
    code = (code_ref[...] - EXACT).astype(f32)
    shifted = pltpu.roll(
        jnp.broadcast_to(code, (longest, frame_count)),
        frame_count - (longest - 1),
        1,
        stride=1,
        stride_axis=0,
    ).astype(bf16)
    at_start = jnp.concatenate(
        [
            ((iota((slots, LANES), 1) + at == first) & (length > 0)).astype(f32)
            for at in range(0, frame_count, LANES)
        ],
        axis=1,
    ).astype(bf16)
    slot_codes = dot_rows(shifted, at_start)
    rows = lambda ref: jnp.broadcast_to(ref[...], (longest, ref.shape[1])).astype(f32).astype(bf16)
    slot_length = dot_rows(rows(length_ref), video_of_slot)
    slot_cluster = dot_rows(rows(cluster_ref), video_of_slot)
    back = (longest - 1 - iota((longest, slots), 0)).astype(f32)
    slot_codes = jnp.where(back < slot_length, slot_codes, 2.0 * EXACT)
    slot_cluster = jnp.where(slot_length > 0, slot_cluster, -1.0)
    part = code_total // (owners * cents)
    high = code_ref[...] // part
    high_match = (iota((owners * cents, frame_count), 0) == high).astype(f32).astype(bf16)
    low_match = (iota((part, frame_count), 0) + high * part == code_ref[...]).astype(f32)
    counts = dot_rows(low_match.astype(bf16), high_match)
    segment = iota((part, LANES), 1) // capacity
    code_segment, cluster_segment = me, lax.rem(me + 1, cents)
    counted = segment == lax.rem(me + 2, cents)
    for owner in range(owners):
        tile, place = divmod(owner * capacity, LANES)
        lanes = slice(tile * LANES, (tile + 1) * LANES)
        turn = lax.rem(code_segment * capacity + LANES - place, LANES)
        codes = pltpu.roll(slot_codes[:, lanes], turn, 1)
        turn = lax.rem(cluster_segment * capacity + LANES - place, LANES)
        cluster = pltpu.roll(slot_cluster[:, lanes], turn, 1)
        note = jnp.where(segment == code_segment, codes, cluster)
        for cent in range(cents):
            at = owner * cents + cent
            count = jnp.broadcast_to(counts[:, at : at + 1], (part, LANES))
            send_ref[owner, cent, 2 * capacity :, :] = jnp.where(counted, count, note).astype(bf16)
    weight = 1.0 / jnp.maximum(length, 1.0)
    copies[-1].wait()
    half = share // 2
    for cent in range(cents):
        sums = dot(member, frames_ref[:, cent * share : (cent + 1) * share])
        for side in range(2):
            pooled = (sums[:, side * half : (side + 1) * half] * weight).astype(bf16)
            send_ref[:, cent, side * capacity : (side + 1) * capacity, :] = pooled.reshape(
                owners, capacity, half
            )


def code_kernel(sizes, length_hbm, owner_hbm, code_hbm, frames_hbm, pooled_ref, keep_ref, give_ref, *scratch):
    owners, cents, capacity, longest, code_total = sizes
    length_ref, owner_ref, code_ref, frames_ref, sems = scratch
    copies = fetch((length_hbm, owner_hbm, code_hbm, frames_hbm), scratch[:-1], sems)
    me = lax.axis_index("cent")
    for copy in copies[:-1]:
        copy.wait()
    frame_count, features = frames_hbm.shape
    share = features // cents
    slots = owners * capacity
    half = share // 2
    _, _, _, member = member_of_slots(length_ref, owner_ref, owners, capacity, frame_count)
    matches = code_matches(code_ref, code_total)
    slot_counts = dot_rows(matches, member).astype(bf16)
    copies[-1].wait()
    for step in range(cents):
        cent = me ^ step
        columns = pl.ds(pl.multiple_of(cent * share, share), share)
        sums = dot(matches, frames_ref[:, columns])
        for side in range(2):
            pooled = pooled_ref[:, cent, side * capacity : (side + 1) * capacity, :].reshape(
                slots, half
            )
            lanes = slice(side * half, (side + 1) * half)
            centred = sums[:, lanes] - dot(slot_counts, pooled)
            if step % 2:
                give_ref[step // 2, :, lanes] = centred.astype(bf16)
            else:
                keep_ref[step // 2, :, lanes] = centred


def slot_rows(got_ref, capacity):
    sources, _, half = got_ref.shape
    return jnp.concatenate(
        [
            got_ref[:, side * capacity : (side + 1) * capacity, :].reshape(sources * capacity, half)
            for side in range(2)
        ],
        axis=1,
    )


def cluster_picks(sizes, got_ref, clusters):
    owners, cents, capacity, longest, code_total = sizes
    segment = iota((longest, LANES), 1) // capacity
    cluster_row = iota((clusters, LANES), 0).astype(f32).astype(bf16)
    picks = []
    for owner in range(owners):
        cluster = jnp.zeros((longest, LANES), f32)
        for cent in range(cents):
            note = got_ref[owner * cents + cent, 2 * capacity :, :].astype(f32)
            cluster = jnp.where(segment == (cent + 1) % cents, note, cluster)
        cluster = pltpu.roll(cluster, LANES - capacity, 1).astype(bf16)
        picks.append(ones_where(cluster_row == cluster[0:1]))
    return jnp.concatenate(picks, axis=1)


def owner_kernel(sizes, got_ref, old_hbm, keep_ref, near_ref, far_ref, code_ref, count_ref, across_ref, here_ref, beside_ref, old_ref, new_ref, sems):
    owners, cents, capacity, longest, code_total = sizes
    me = lax.axis_index("cent")
    clusters, share = old_ref.shape
    columns = pl.ds(pl.multiple_of(me * share, share), share)
    copies = fetch((old_hbm.at[:, columns],), (old_ref,), sems)
    pick = cluster_picks(sizes, got_ref, clusters)
    rows = slot_rows(got_ref, capacity)
    sums = dot(pick, rows)
    number = dot(pick, jnp.ones((rows.shape[0], LANES), bf16))
    number = jnp.concatenate([number] * (share // LANES), axis=1)
    copies[0].wait()
    new = (sums + old_ref[...].astype(f32)) / (number + 1.0)
    new_ref[...] = new
    anchor = new.astype(bf16)
    bits = longest.bit_length()
    digits = 30 // bits
    block = -(-code_total // digits)
    block = -(-block // 16) * 16
    segment = iota((longest, LANES), 1) // capacity
    count = jnp.zeros((longest, LANES), f32)
    word_row = iota((block, LANES), 0)
    slot_counts = []
    for owner in range(owners):
        codes = jnp.zeros((longest, LANES), f32)
        for cent in range(cents):
            note = got_ref[owner * cents + cent, 2 * capacity :, :].astype(f32)
            codes = jnp.where(segment == cent, note, codes)
            count = count + jnp.where(segment == (cent + 2) % cents, note, 0.0)
        codes = codes.astype(jnp.int32) + EXACT
        place = jnp.where(codes < code_total, codes, -1)
        one = jnp.ones((longest, LANES), jnp.int32)
        for digit in range(1, -(-code_total // block)):
            above = (codes >= digit * block) & (codes < code_total)
            place = place - jnp.where(above, block, 0)
            one = jnp.where(above, 1 << (bits * digit), one)
        words = jnp.zeros((block, LANES), jnp.int32)
        for row in range(longest):
            words = words + jnp.where(word_row == place[row : row + 1], one[row : row + 1], 0)
        held = []
        for digit in range(-(-code_total // block)):
            height = min(block, code_total - digit * block)
            word = words[:height] >> (bits * digit) & ((1 << bits) - 1)
            held.append(word.astype(f32).astype(bf16))
        slot_counts.append(jnp.concatenate(held, axis=0))
    for step in range(cents.bit_length() - 1):
        count = count + pltpu.roll(count, capacity << step, 1)
    count_ref[...] = count
    slot_count = jnp.concatenate(slot_counts, axis=1)
    cluster_count = dot_rows(slot_count, pick)
    high = jnp.floor(cluster_count * (1.0 / EXACT))
    low = cluster_count - high * EXACT
    moved = dot(low.astype(bf16), anchor) + EXACT * dot(high.astype(bf16), anchor)
    total = keep_ref[0] + near_ref[0].astype(f32) + far_ref[...].astype(f32)
    total = total + (dot(slot_count, rows) - moved)
    code_ref[...] = total.astype(bf16)
    quarter = clusters // cents
    rows_of = lambda step: new_ref[pl.ds(pl.multiple_of((me ^ step) * quarter, quarter), quarter), :]
    across_ref[0] = rows_of(2)
    across_ref[1] = rows_of(3)
    here_ref[...] = rows_of(0)
    beside_ref[...] = rows_of(1)


def finish_kernel(sizes, got_ref, count_ref, old_ref, out_ref):
    owners, cents, capacity, longest, code_total = sizes
    share = got_ref.shape[2]
    prior = jnp.concatenate([count_ref[...] + code_prior] * (share // LANES), axis=1)
    for cent in range(cents):
        total = got_ref[cent].astype(f32)
        for owner in range(1, owners):
            total = total + got_ref[owner * cents + cent].astype(f32)
        lanes = slice(cent * share, (cent + 1) * share)
        out_ref[:, lanes] = (total + code_prior * old_ref[:, lanes]) / prior


def join_kernel(here_ref, across_ref, near_ref, far_ref, out_ref):
    me = lax.axis_index("cent")
    share = here_ref.shape[1]
    for step, value in enumerate((here_ref[...], near_ref[...], across_ref[0], far_ref[...])):
        out_ref[:, pl.ds(pl.multiple_of((me ^ step) * share, share), share)] = value


def summed_body(frames, video_length, video_owner, video_cluster, frame_code, old_coarse, old_codes):
    owners = lax.axis_size("dp")
    cents = lax.axis_size("cent")
    frame_count, features = frames.shape
    videos = video_length.shape[1]
    clusters = old_coarse.shape[0]
    part = old_codes.shape[0]
    code_total = part * owners * cents
    capacity = max(2, 2 * videos // owners)
    longest = 2 * frame_count // videos
    share = features // cents
    devices = owners * cents
    sizes = (owners, cents, capacity, longest, code_total)
    frame_code = frame_code.reshape(1, frame_count)
    vmem = pl.BlockSpec(memory_space=pltpu.VMEM)
    hbm = pl.BlockSpec(memory_space=pltpu.HBM)
    params = pltpu.CompilerParams(vmem_limit_bytes=32 * 1024 * 1024)
    chunk = 2 * capacity + longest
    stay = lambda array: pltpu.with_memory_space_constraint(array, pltpu.HBM)
    swap = lambda array, bit: lax.ppermute(
        array, "cent", [(index, index ^ bit) for index in range(cents)]
    )
    row = lambda length: pltpu.VMEM((1, length), jnp.int32)
    frames_scratch = [row(frame_count), pltpu.VMEM((frame_count, features), bf16)]
    quarter = clusters // cents
    send = pl.pallas_call(
        functools.partial(pool_kernel, sizes),
        out_shape=jax.ShapeDtypeStruct((owners, cents, chunk, share // 2), bf16),
        in_specs=[hbm] * 5,
        out_specs=vmem,
        scratch_shapes=[row(videos)] * 3 + frames_scratch + [pltpu.SemaphoreType.DMA((5,))],
        compiler_params=params,
        name="pool",
    )(*map(stay, (video_length, video_owner, video_cluster, frame_code, frames)))
    got = lax.all_to_all(
        send.reshape(devices, chunk, share // 2), ("dp", "cent"), 0, 0, tiled=True
    )
    keep, give = pl.pallas_call(
        functools.partial(code_kernel, sizes),
        out_shape=(
            jax.ShapeDtypeStruct((cents // 2, code_total, share), f32),
            jax.ShapeDtypeStruct((cents // 2, code_total, share), bf16),
        ),
        in_specs=[hbm] * 4 + [vmem],
        out_specs=(vmem, vmem),
        scratch_shapes=[row(videos)] * 2 + frames_scratch + [pltpu.SemaphoreType.DMA((4,))],
        compiler_params=params,
        cost_estimate=pl.CostEstimate(
            flops=3 * code_total * frame_count * features,
            bytes_accessed=6 * frame_count * features,
            transcendentals=0,
        ),
        name="codes",
    )(*map(stay, (video_length, video_owner, frame_code, frames)), send)
    near = swap(give, 1)
    far = swap((keep[1] + near[1].astype(f32)).astype(bf16), 2)
    piece = jax.ShapeDtypeStruct((quarter, share), f32)
    sums, count, across, here, beside = pl.pallas_call(
        functools.partial(owner_kernel, sizes),
        out_shape=(
            jax.ShapeDtypeStruct((code_total, share), bf16),
            jax.ShapeDtypeStruct((part, LANES), f32),
            jax.ShapeDtypeStruct((2, quarter, share), f32),
            piece,
            piece,
        ),
        in_specs=[vmem, hbm, vmem, vmem, vmem],
        out_specs=(vmem,) * 5,
        scratch_shapes=[
            pltpu.VMEM((clusters, share), bf16),
            pltpu.VMEM((clusters, share), f32),
            pltpu.SemaphoreType.DMA((1,)),
        ],
        compiler_params=params,
        name="owner",
    )(got, stay(old_coarse), keep, near, far)
    across = swap(across, 2)
    last = lax.all_to_all(sums.reshape(devices, part, share), ("dp", "cent"), 0, 0, tiled=True)
    new_coarse = pl.pallas_call(
        join_kernel,
        out_shape=jax.ShapeDtypeStruct((quarter, features), f32),
        in_specs=[vmem] * 4,
        out_specs=vmem,
        compiler_params=params,
        name="join",
    )(here, across, swap(beside, 1), swap(across[1], 1))
    new_codes = pl.pallas_call(
        functools.partial(finish_kernel, sizes),
        out_shape=jax.ShapeDtypeStruct((part, features), f32),
        in_specs=[vmem] * 3,
        out_specs=vmem,
        compiler_params=params,
        name="finish",
    )(last, count, old_codes)
    return new_coarse, new_codes


def owner_slots(target, target_count, capacity):
    matches = (target[:, None] == jnp.arange(target_count, dtype=jnp.int32)[None, :]).astype(
        jnp.int32
    )
    before = jnp.cumsum(matches, axis=0) - matches
    slot_rank = jnp.sum(before * matches, axis=1)
    return target * capacity + slot_rank


def invert_slots(slot_list, slot_total):
    item_index = jnp.arange(slot_list.shape[0], dtype=jnp.int32)
    source = jnp.zeros((slot_total,), jnp.int32).at[slot_list].set(item_index)
    filled = jnp.zeros((slot_total,), jnp.int32).at[slot_list].set(1)
    return (source, filled)


def routed_body(frames, video_length, video_owner, video_cluster, frame_code, old_coarse, old_codes):
    dp_count = lax.axis_size("dp")
    cent_count = lax.axis_size("cent")
    frame_count, features = frames.shape
    video_count = video_length.shape[1]
    coarse_rows = old_coarse.shape[0]
    code_share = old_codes.shape[0]
    code_block = code_share * cent_count
    cap_video = max(2, 2 * video_count // dp_count)
    cap_frame = max(2, 2 * frame_count // dp_count)
    lengths = video_length[0]
    target = video_owner[0]
    cluster = video_cluster[0]
    video_ends = jnp.cumsum(lengths)
    video_starts = video_ends - lengths
    position = jnp.arange(frame_count, dtype=jnp.int32)
    member = (
        (position[None, :] >= video_starts[:, None]) & (position[None, :] < video_ends[:, None])
    ).astype(jnp.bfloat16)
    video_sums = jnp.dot(member, frames, preferred_element_type=jnp.float32)
    pooled = (video_sums / lengths[:, None].astype(jnp.float32)).astype(jnp.bfloat16)
    video_slot = owner_slots(target, dp_count, cap_video)
    source, filled = invert_slots(video_slot, dp_count * cap_video)
    send_rows = jnp.where(filled[:, None] > 0, pooled[source], jnp.zeros((), jnp.bfloat16))
    send_codes = jnp.where(filled > 0, cluster[source], -1)
    got_rows, got_codes = (
        lax.all_to_all(
            send_rows.reshape(dp_count, cap_video, features),
            "dp",
            split_axis=0,
            concat_axis=0,
            tiled=True,
        ),
        lax.all_to_all(
            send_codes.reshape(dp_count, cap_video), "dp", split_axis=0, concat_axis=0, tiled=True
        ),
    )
    got_rows = got_rows.reshape(-1, features)
    got_codes = got_codes.reshape(-1)
    table_index = jnp.arange(coarse_rows, dtype=jnp.int32)
    coarse_pick = (got_codes[None, :] == table_index[:, None]).astype(jnp.bfloat16)
    coarse_sum = jnp.dot(coarse_pick, got_rows, preferred_element_type=jnp.float32)
    coarse_count = jnp.sum(coarse_pick.astype(jnp.float32), axis=1)
    quarter = coarse_rows // cent_count
    part_sum, part_count = (
        lax.psum_scatter(coarse_sum, "cent", scatter_dimension=0, tiled=True),
        lax.psum_scatter(coarse_count, "cent", scatter_dimension=0, tiled=True),
    )
    first_row = lax.axis_index("cent") * quarter
    old_part = lax.dynamic_slice_in_dim(old_coarse, first_row, quarter, 0).astype(jnp.float32)
    new_coarse = (part_sum + old_part) / (part_count[:, None] + 1.0)
    anchor_table = lax.all_gather(new_coarse.astype(jnp.bfloat16), "cent", axis=0, tiled=True)
    slot_anchor = jnp.dot(coarse_pick.T, anchor_table, preferred_element_type=jnp.float32).astype(
        jnp.bfloat16
    )
    returned = lax.all_to_all(
        slot_anchor.reshape(dp_count, cap_video, features),
        "dp",
        split_axis=0,
        concat_axis=0,
        tiled=True,
    )
    video_anchor = returned.reshape(-1, features)[video_slot]
    frame_anchor = jnp.dot(member.T, video_anchor, preferred_element_type=jnp.float32)
    residual = (frames - frame_anchor).astype(jnp.bfloat16)
    code_target = frame_code // code_block
    code_offset = frame_code - code_target * code_block
    frame_slot = owner_slots(code_target, dp_count, cap_frame)
    source, filled = invert_slots(frame_slot, dp_count * cap_frame)
    slot_rows = jnp.where(filled[:, None] > 0, residual[source], jnp.zeros((), jnp.bfloat16))
    slot_codes = jnp.where(filled > 0, code_offset[source], -1)
    code_rows, code_ids = (
        lax.all_to_all(
            slot_rows.reshape(dp_count, cap_frame, features),
            "dp",
            split_axis=0,
            concat_axis=0,
            tiled=True,
        ),
        lax.all_to_all(
            slot_codes.reshape(dp_count, cap_frame), "dp", split_axis=0, concat_axis=0, tiled=True
        ),
    )
    code_index = jnp.arange(code_block, dtype=jnp.int32)
    code_pick = (code_ids.reshape(-1)[None, :] == code_index[:, None]).astype(jnp.bfloat16)
    code_sum = jnp.dot(
        code_pick, code_rows.reshape(-1, features), preferred_element_type=jnp.float32
    )
    code_count = jnp.sum(code_pick.astype(jnp.float32), axis=1)
    own_sum, own_count = (
        lax.psum_scatter(code_sum, "cent", scatter_dimension=0, tiled=True),
        lax.psum_scatter(code_count, "cent", scatter_dimension=0, tiled=True),
    )
    new_codes = (own_sum + code_prior * old_codes) / (own_count[:, None] + code_prior)
    return (new_coarse, new_codes)


def choose(mesh):
    owners, cents = mesh.shape["dp"], mesh.shape["cent"]

    def body(*arrays):
        frame_count, features = arrays[0].shape
        videos = arrays[1].shape[1]
        part = arrays[6].shape[0]
        small = (
            part * owners * cents <= 2 * EXACT
            and arrays[5].shape[0] <= EXACT
            and cents == 4
            and cents * max(2, 2 * videos // owners) == LANES
            and part == 2 * frame_count // videos
            and features % (2 * cents * LANES) == 0
        )
        return (summed_body if small else routed_body)(*arrays)

    return body


def solution(mesh):
    placed = (
        P(("dp", "cent"), None),
        P(("dp", "cent"), None),
        P(("dp", "cent"), None),
        P(("dp", "cent"), None),
        P(("dp", "cent")),
        P("dp", None),
        P(("dp", "cent"), None),
    )
    return jax.shard_map(
        choose(mesh),
        mesh=mesh,
        in_specs=placed,
        out_specs=(P(("dp", "cent"), None), P(("dp", "cent"), None)),
        check_vma=False,
    )
```

```python
import functools

import jax
import jax.numpy as jnp
from jax import lax
from jax.experimental import pallas as pl
from jax.experimental.pallas import tpu as pltpu
from jax.sharding import PartitionSpec as P

code_prior = 16.0
LANES = 128
EXACT = 256
f32 = jnp.float32
bf16 = jnp.bfloat16


def iota(shape, axis):
    return lax.broadcasted_iota(jnp.int32, shape, axis)


def ones_where(mask):
    return jnp.where(mask, jnp.ones((), bf16), jnp.zeros((), bf16))


def fetch(sources, targets, sems):
    copies = [
        pltpu.make_async_copy(source, target, sems.at[at])
        for at, (source, target) in enumerate(zip(sources, targets))
    ]
    for copy in copies:
        copy.start()
    return copies


def dot(left, right):
    return jnp.dot(left, right, preferred_element_type=f32)


def dot_rows(left, right):
    return lax.dot_general(left, right, (((1,), (1,)), ((), ())), preferred_element_type=f32)


def member_of_slots(length_ref, owner_ref, owners, capacity, frame_count):
    videos = length_ref.shape[1]
    slots = owners * capacity
    lengths = length_ref[...].astype(f32)
    owner = owner_ref[...]
    match = (iota((owners, videos), 0) == owner).astype(f32)
    earlier = (iota((videos, videos), 0) < iota((videos, videos), 1)).astype(bf16)
    stacked = jnp.concatenate([match, jnp.broadcast_to(lengths, (8, videos))], axis=0)
    before = dot(stacked.astype(bf16), earlier)
    rank = jnp.sum(before[:owners] * match, axis=0, keepdims=True)
    starts = before[owners : owners + 1]
    slot = owner * capacity + rank.astype(jnp.int32)
    video_of_slot = (iota((slots, videos), 0) == slot).astype(f32).astype(bf16)
    high = jnp.floor(starts / 16.0) * 16.0
    low = starts - high
    tall = lambda row: jnp.broadcast_to(row, (LANES, videos)).astype(bf16)
    start = dot_rows(video_of_slot, tall(high)) + dot_rows(video_of_slot, tall(low))
    length = dot_rows(video_of_slot, tall(lengths))
    first, last = start.astype(jnp.int32), (start + length).astype(jnp.int32)
    member = jnp.concatenate(
        [
            (
                (iota((slots, LANES), 1) + at >= first) & (iota((slots, LANES), 1) + at < last)
            ).astype(f32)
            for at in range(0, frame_count, LANES)
        ],
        axis=1,
    ).astype(bf16)
    return video_of_slot, first, length, member


def code_matches(code_ref, code_total):
    frame_count = code_ref.shape[1]
    return (iota((code_total, frame_count), 0) == code_ref[...]).astype(f32).astype(bf16)


def pool_kernel(
    sizes,
    length_hbm,
    owner_hbm,
    cluster_hbm,
    code_hbm,
    frames_hbm,
    send_hbm,
    pooled_ref,
    member_ref,
    *scratch,
):
    owners, cents, capacity, longest, code_total = sizes
    length_ref, owner_ref, cluster_ref, code_ref, frames_ref, send_ref, sems, out_sems = scratch
    copies = fetch(
        (length_hbm, owner_hbm, cluster_hbm, code_hbm, frames_hbm), scratch[:5], sems
    )
    me = lax.axis_index("cent")
    frame_count, features = frames_hbm.shape
    for copy in copies[:-1]:
        copy.wait()
    slots = owners * capacity
    share = features // cents
    video_of_slot, first, length, member = member_of_slots(
        length_ref, owner_ref, owners, capacity, frame_count
    )
    member_ref[...] = member
    code = (code_ref[...] - EXACT).astype(f32)
    shifted = pltpu.roll(
        jnp.broadcast_to(code, (longest, frame_count)),
        frame_count - (longest - 1),
        1,
        stride=1,
        stride_axis=0,
    ).astype(bf16)
    at_start = jnp.concatenate(
        [
            ((iota((slots, LANES), 1) + at == first) & (length > 0)).astype(f32)
            for at in range(0, frame_count, LANES)
        ],
        axis=1,
    ).astype(bf16)
    slot_codes = dot_rows(shifted, at_start)
    rows = lambda ref: jnp.broadcast_to(ref[...], (longest, ref.shape[1])).astype(f32).astype(bf16)
    slot_length = dot_rows(rows(length_ref), video_of_slot)
    slot_cluster = dot_rows(rows(cluster_ref), video_of_slot)
    back = (longest - 1 - iota((longest, slots), 0)).astype(f32)
    slot_codes = jnp.where(back < slot_length, slot_codes, 2.0 * EXACT)
    slot_cluster = jnp.where(slot_length > 0, slot_cluster, -1.0)
    part = code_total // (owners * cents)
    high = code_ref[...] // part
    high_match = (iota((owners * cents, frame_count), 0) == high).astype(f32).astype(bf16)
    low_match = (iota((part, frame_count), 0) + high * part == code_ref[...]).astype(f32)
    counts = dot_rows(low_match.astype(bf16), high_match)
    half = part // 2
    lane = iota((half, LANES), 1)
    segment = lane // capacity
    last_codes, cluster_place, count_place = (
        segment == lax.rem(me + step, cents) for step in range(1, 4)
    )
    front = lane % capacity < capacity // 2
    for owner in range(owners):
        tile, place = divmod(owner * capacity, LANES)
        lanes = slice(tile * LANES, (tile + 1) * LANES)
        turned = lambda value, step: pltpu.roll(
            value, lax.rem((me + step) * capacity + LANES - place, LANES), 1
        )
        codes = turned(slot_codes[:half, lanes], 0)
        codes = jnp.where(last_codes, turned(slot_codes[half:, lanes], 1), codes)
        note = jnp.where(cluster_place, turned(slot_cluster[:half, lanes], 2), codes)
        for cent in range(cents):
            at = owner * cents + cent
            spread = lambda value: jnp.broadcast_to(value, (half, LANES))
            count = jnp.where(
                front, spread(counts[:half, at : at + 1]), spread(counts[half:, at : at + 1])
            )
            send_ref[owner, cent, 2 * capacity :, :] = jnp.where(count_place, count, note).astype(
                bf16
            )
    weight = 1.0 / jnp.maximum(length, 1.0)
    copies[-1].wait()
    half = share // 2
    out = []
    for cent in range(cents):
        sums = dot(member, frames_ref[:, cent * share : (cent + 1) * share])
        for side in range(2):
            pooled = (sums[:, side * half : (side + 1) * half] * weight).astype(bf16)
            at = cent * share + side * half
            pooled_ref[:, at : at + half] = pooled
            send_ref[:, cent, side * capacity : (side + 1) * capacity, :] = pooled.reshape(
                owners, capacity, half
            )
        out.append(
            pltpu.make_async_copy(send_ref.at[:, cent], send_hbm.at[:, cent], out_sems.at[cent])
        )
        out[-1].start()
    for copy in out:
        copy.wait()


def code_kernel(
    sizes, code_hbm, frames_hbm, pooled_ref, member_ref, keep_ref, give_ref, code_ref, frames_ref, sems
):
    owners, cents, capacity, longest, code_total = sizes
    copies = fetch((code_hbm, frames_hbm), (code_ref, frames_ref), sems)
    me = lax.axis_index("cent")
    share = frames_hbm.shape[1] // cents
    copies[0].wait()
    matches = code_matches(code_ref, code_total)
    slot_counts = dot_rows(matches, member_ref[...]).astype(bf16)
    copies[1].wait()
    for step in range(cents):
        columns = pl.ds(pl.multiple_of((me ^ step) * share, share), share)
        centred = dot(matches, frames_ref[:, columns]) - dot(slot_counts, pooled_ref[:, columns])
        if step % 2:
            give_ref[step // 2] = centred.astype(bf16)
        else:
            keep_ref[step // 2] = centred


def slot_rows(got_ref, capacity):
    sources, _, half = got_ref.shape
    return jnp.concatenate(
        [
            got_ref[:, side * capacity : (side + 1) * capacity, :].reshape(sources * capacity, half)
            for side in range(2)
        ],
        axis=1,
    )


def owner_kernel(sizes, got_ref, old_hbm, keep_ref, near_ref, far_ref, code_hbm, count_ref, across_ref, here_ref, beside_ref, old_ref, new_ref, code_ref, sems, out_sems):
    owners, cents, capacity, longest, code_total = sizes
    me = lax.axis_index("cent")
    clusters, share = old_ref.shape
    columns = pl.ds(pl.multiple_of(me * share, share), share)
    copies = fetch((old_hbm.at[:, columns],), (old_ref,), sems)
    half = longest // 2
    lane = iota((half, LANES), 1)
    segment = lane // capacity
    zeros = jnp.zeros((half, LANES), f32)
    count = zeros
    cluster_row = iota((clusters, LANES), 0).astype(f32).astype(bf16)
    picks, code_tiles = [], []
    for owner in range(owners):
        front, back, cluster = zeros, zeros, zeros
        for cent in range(cents):
            note = got_ref[owner * cents + cent, 2 * capacity :, :].astype(f32)
            placed = [segment == (cent + step) % cents for step in range(4)]
            front = jnp.where(placed[0], note, front)
            back = jnp.where(placed[1], note, back)
            cluster = jnp.where(placed[2], note, cluster)
            count = count + jnp.where(placed[3], note, 0.0)
        back = pltpu.roll(back, LANES - capacity, 1)
        cluster = pltpu.roll(cluster, LANES - 2 * capacity, 1).astype(bf16)
        picks.append(ones_where(cluster_row == cluster[0:1]))
        code_tiles.append(jnp.concatenate([front, back], axis=0))
    for step in range(cents.bit_length() - 1):
        count = count + pltpu.roll(count, capacity << step, 1)
    other = pltpu.roll(count, capacity // 2, 1)
    first = lane % capacity < capacity // 2
    count_ref[...] = jnp.concatenate(
        [jnp.where(first, count, other), jnp.where(first, other, count)], axis=0
    )
    pick = jnp.concatenate(picks, axis=1)
    rows = slot_rows(got_ref, capacity)
    sums = dot(pick, rows)
    number = dot(pick, jnp.ones((rows.shape[0], LANES), bf16))
    number = jnp.concatenate([number] * (share // LANES), axis=1)
    copies[0].wait()
    new = (sums + old_ref[...].astype(f32)) / (number + 1.0)
    new_ref[...] = new
    anchor = new.astype(bf16)
    bits = longest.bit_length()
    digits = 30 // bits
    block = -(-code_total // digits)
    block = -(-block // 16) * 16
    word_row = iota((block, LANES), 0)
    slot_counts = []
    for codes in code_tiles:
        codes = codes.astype(jnp.int32) + EXACT
        place = jnp.where(codes < code_total, codes, -1)
        one = jnp.ones((longest, LANES), jnp.int32)
        for digit in range(1, -(-code_total // block)):
            above = (codes >= digit * block) & (codes < code_total)
            place = place - jnp.where(above, block, 0)
            one = jnp.where(above, 1 << (bits * digit), one)
        words = jnp.zeros((block, LANES), jnp.int32)
        for row in range(longest):
            words = words + jnp.where(word_row == place[row : row + 1], one[row : row + 1], 0)
        held = []
        for digit in range(-(-code_total // block)):
            height = min(block, code_total - digit * block)
            word = words[:height] >> (bits * digit) & ((1 << bits) - 1)
            held.append(word.astype(f32).astype(bf16))
        slot_counts.append(jnp.concatenate(held, axis=0))
    slot_count = jnp.concatenate(slot_counts, axis=1)
    cluster_count = dot_rows(slot_count, pick)
    high = jnp.floor(cluster_count * (1.0 / EXACT))
    low = cluster_count - high * EXACT
    moved = dot(low.astype(bf16), anchor) + EXACT * dot(high.astype(bf16), anchor)
    out = []
    height = code_total // 2
    for side in range(2):
        part = slice(side * height, (side + 1) * height)
        total = keep_ref[0, part] + near_ref[0, part].astype(f32) + far_ref[part].astype(f32)
        total = total + (dot(slot_count[part], rows) - moved[part])
        code_ref[part] = total.astype(bf16)
        out.append(pltpu.make_async_copy(code_ref.at[part], code_hbm.at[part], out_sems.at[side]))
        out[-1].start()
    quarter = clusters // cents
    rows_of = lambda step: new_ref[pl.ds(pl.multiple_of((me ^ step) * quarter, quarter), quarter), :]
    across_ref[0] = rows_of(2)
    across_ref[1] = rows_of(3)
    here_ref[...] = rows_of(0)
    beside_ref[...] = rows_of(1)
    for copy in out:
        copy.wait()


def finish_kernel(sizes, got_ref, count_ref, old_ref, out_ref):
    owners, cents, capacity, longest, code_total = sizes
    share = got_ref.shape[2]
    prior = jnp.concatenate([count_ref[...] + code_prior] * (share // LANES), axis=1)
    for cent in range(cents):
        total = got_ref[cent].astype(f32)
        for owner in range(1, owners):
            total = total + got_ref[owner * cents + cent].astype(f32)
        lanes = slice(cent * share, (cent + 1) * share)
        out_ref[:, lanes] = (total + code_prior * old_ref[:, lanes]) / prior


def join_kernel(here_ref, across_ref, near_ref, far_ref, out_ref):
    me = lax.axis_index("cent")
    share = here_ref.shape[1]
    for step, value in enumerate((here_ref[...], near_ref[...], across_ref[0], far_ref[...])):
        out_ref[:, pl.ds(pl.multiple_of((me ^ step) * share, share), share)] = value


def summed_body(frames, video_length, video_owner, video_cluster, frame_code, old_coarse, old_codes):
    owners = lax.axis_size("dp")
    cents = lax.axis_size("cent")
    frame_count, features = frames.shape
    videos = video_length.shape[1]
    clusters = old_coarse.shape[0]
    part = old_codes.shape[0]
    code_total = part * owners * cents
    capacity = max(2, 2 * videos // owners)
    longest = 2 * frame_count // videos
    share = features // cents
    devices = owners * cents
    sizes = (owners, cents, capacity, longest, code_total)
    frame_code = frame_code.reshape(1, frame_count)
    vmem = pl.BlockSpec(memory_space=pltpu.VMEM)
    hbm = pl.BlockSpec(memory_space=pltpu.HBM)
    params = pltpu.CompilerParams(vmem_limit_bytes=32 * 1024 * 1024)
    chunk = 2 * capacity + longest // 2
    slots = owners * capacity
    stay = lambda array: pltpu.with_memory_space_constraint(array, pltpu.HBM)
    swap = lambda array, bit: lax.ppermute(
        array, "cent", [(index, index ^ bit) for index in range(cents)]
    )
    row = lambda length: pltpu.VMEM((1, length), jnp.int32)
    frames_scratch = [row(frame_count), pltpu.VMEM((frame_count, features), bf16)]
    quarter = clusters // cents
    send, pooled, member = pl.pallas_call(
        functools.partial(pool_kernel, sizes),
        out_shape=(
            jax.ShapeDtypeStruct((owners, cents, chunk, share // 2), bf16),
            jax.ShapeDtypeStruct((slots, features), bf16),
            jax.ShapeDtypeStruct((slots, frame_count), bf16),
        ),
        in_specs=[hbm] * 5,
        out_specs=(hbm, vmem, vmem),
        scratch_shapes=[row(videos)] * 3
        + frames_scratch
        + [
            pltpu.VMEM((owners, cents, chunk, share // 2), bf16),
            pltpu.SemaphoreType.DMA((5,)),
            pltpu.SemaphoreType.DMA((cents,)),
        ],
        compiler_params=params,
        name="pool",
    )(*map(stay, (video_length, video_owner, video_cluster, frame_code, frames)))
    got = lax.all_to_all(
        send.reshape(devices, chunk, share // 2), ("dp", "cent"), 0, 0, tiled=True
    )
    keep, give = pl.pallas_call(
        functools.partial(code_kernel, sizes),
        out_shape=(
            jax.ShapeDtypeStruct((cents // 2, code_total, share), f32),
            jax.ShapeDtypeStruct((cents // 2, code_total, share), bf16),
        ),
        in_specs=[hbm] * 2 + [vmem] * 2,
        out_specs=(vmem, vmem),
        scratch_shapes=frames_scratch + [pltpu.SemaphoreType.DMA((2,))],
        compiler_params=params,
        cost_estimate=pl.CostEstimate(
            flops=3 * code_total * frame_count * features,
            bytes_accessed=6 * frame_count * features,
            transcendentals=0,
        ),
        name="codes",
    )(stay(frame_code), stay(frames), pooled, member)
    near = swap(give, 1)
    far = swap((keep[1] + near[1].astype(f32)).astype(bf16), 2)
    piece = jax.ShapeDtypeStruct((quarter, share), f32)
    sums, count, across, here, beside = pl.pallas_call(
        functools.partial(owner_kernel, sizes),
        out_shape=(
            jax.ShapeDtypeStruct((code_total, share), bf16),
            jax.ShapeDtypeStruct((part, LANES), f32),
            jax.ShapeDtypeStruct((2, quarter, share), f32),
            piece,
            piece,
        ),
        in_specs=[vmem, hbm, vmem, vmem, vmem],
        out_specs=(hbm,) + (vmem,) * 4,
        scratch_shapes=[
            pltpu.VMEM((clusters, share), bf16),
            pltpu.VMEM((clusters, share), f32),
            pltpu.VMEM((code_total, share), bf16),
            pltpu.SemaphoreType.DMA((1,)),
            pltpu.SemaphoreType.DMA((2,)),
        ],
        compiler_params=params,
        name="owner",
    )(got, stay(old_coarse), keep, near, far)
    across = swap(across, 2)
    last = lax.all_to_all(sums.reshape(devices, part, share), ("dp", "cent"), 0, 0, tiled=True)
    new_coarse = pl.pallas_call(
        join_kernel,
        out_shape=jax.ShapeDtypeStruct((quarter, features), f32),
        in_specs=[vmem] * 4,
        out_specs=vmem,
        compiler_params=params,
        name="join",
    )(here, across, swap(beside, 1), swap(across[1], 1))
    new_codes = pl.pallas_call(
        functools.partial(finish_kernel, sizes),
        out_shape=jax.ShapeDtypeStruct((part, features), f32),
        in_specs=[vmem] * 3,
        out_specs=vmem,
        compiler_params=params,
        name="finish",
    )(last, count, old_codes)
    return new_coarse, new_codes


def owner_slots(target, target_count, capacity):
    matches = (target[:, None] == jnp.arange(target_count, dtype=jnp.int32)[None, :]).astype(
        jnp.int32
    )
    before = jnp.cumsum(matches, axis=0) - matches
    slot_rank = jnp.sum(before * matches, axis=1)
    return target * capacity + slot_rank


def invert_slots(slot_list, slot_total):
    item_index = jnp.arange(slot_list.shape[0], dtype=jnp.int32)
    source = jnp.zeros((slot_total,), jnp.int32).at[slot_list].set(item_index)
    filled = jnp.zeros((slot_total,), jnp.int32).at[slot_list].set(1)
    return (source, filled)


def routed_body(frames, video_length, video_owner, video_cluster, frame_code, old_coarse, old_codes):
    dp_count = lax.axis_size("dp")
    cent_count = lax.axis_size("cent")
    frame_count, features = frames.shape
    video_count = video_length.shape[1]
    coarse_rows = old_coarse.shape[0]
    code_share = old_codes.shape[0]
    code_block = code_share * cent_count
    cap_video = max(2, 2 * video_count // dp_count)
    cap_frame = max(2, 2 * frame_count // dp_count)
    lengths = video_length[0]
    target = video_owner[0]
    cluster = video_cluster[0]
    video_ends = jnp.cumsum(lengths)
    video_starts = video_ends - lengths
    position = jnp.arange(frame_count, dtype=jnp.int32)
    member = (
        (position[None, :] >= video_starts[:, None]) & (position[None, :] < video_ends[:, None])
    ).astype(jnp.bfloat16)
    video_sums = jnp.dot(member, frames, preferred_element_type=jnp.float32)
    pooled = (video_sums / lengths[:, None].astype(jnp.float32)).astype(jnp.bfloat16)
    video_slot = owner_slots(target, dp_count, cap_video)
    source, filled = invert_slots(video_slot, dp_count * cap_video)
    send_rows = jnp.where(filled[:, None] > 0, pooled[source], jnp.zeros((), jnp.bfloat16))
    send_codes = jnp.where(filled > 0, cluster[source], -1)
    got_rows, got_codes = (
        lax.all_to_all(
            send_rows.reshape(dp_count, cap_video, features),
            "dp",
            split_axis=0,
            concat_axis=0,
            tiled=True,
        ),
        lax.all_to_all(
            send_codes.reshape(dp_count, cap_video), "dp", split_axis=0, concat_axis=0, tiled=True
        ),
    )
    got_rows = got_rows.reshape(-1, features)
    got_codes = got_codes.reshape(-1)
    table_index = jnp.arange(coarse_rows, dtype=jnp.int32)
    coarse_pick = (got_codes[None, :] == table_index[:, None]).astype(jnp.bfloat16)
    coarse_sum = jnp.dot(coarse_pick, got_rows, preferred_element_type=jnp.float32)
    coarse_count = jnp.sum(coarse_pick.astype(jnp.float32), axis=1)
    quarter = coarse_rows // cent_count
    part_sum, part_count = (
        lax.psum_scatter(coarse_sum, "cent", scatter_dimension=0, tiled=True),
        lax.psum_scatter(coarse_count, "cent", scatter_dimension=0, tiled=True),
    )
    first_row = lax.axis_index("cent") * quarter
    old_part = lax.dynamic_slice_in_dim(old_coarse, first_row, quarter, 0).astype(jnp.float32)
    new_coarse = (part_sum + old_part) / (part_count[:, None] + 1.0)
    anchor_table = lax.all_gather(new_coarse.astype(jnp.bfloat16), "cent", axis=0, tiled=True)
    slot_anchor = jnp.dot(coarse_pick.T, anchor_table, preferred_element_type=jnp.float32).astype(
        jnp.bfloat16
    )
    returned = lax.all_to_all(
        slot_anchor.reshape(dp_count, cap_video, features),
        "dp",
        split_axis=0,
        concat_axis=0,
        tiled=True,
    )
    video_anchor = returned.reshape(-1, features)[video_slot]
    frame_anchor = jnp.dot(member.T, video_anchor, preferred_element_type=jnp.float32)
    residual = (frames - frame_anchor).astype(jnp.bfloat16)
    code_target = frame_code // code_block
    code_offset = frame_code - code_target * code_block
    frame_slot = owner_slots(code_target, dp_count, cap_frame)
    source, filled = invert_slots(frame_slot, dp_count * cap_frame)
    slot_rows = jnp.where(filled[:, None] > 0, residual[source], jnp.zeros((), jnp.bfloat16))
    slot_codes = jnp.where(filled > 0, code_offset[source], -1)
    code_rows, code_ids = (
        lax.all_to_all(
            slot_rows.reshape(dp_count, cap_frame, features),
            "dp",
            split_axis=0,
            concat_axis=0,
            tiled=True,
        ),
        lax.all_to_all(
            slot_codes.reshape(dp_count, cap_frame), "dp", split_axis=0, concat_axis=0, tiled=True
        ),
    )
    code_index = jnp.arange(code_block, dtype=jnp.int32)
    code_pick = (code_ids.reshape(-1)[None, :] == code_index[:, None]).astype(jnp.bfloat16)
    code_sum = jnp.dot(
        code_pick, code_rows.reshape(-1, features), preferred_element_type=jnp.float32
    )
    code_count = jnp.sum(code_pick.astype(jnp.float32), axis=1)
    own_sum, own_count = (
        lax.psum_scatter(code_sum, "cent", scatter_dimension=0, tiled=True),
        lax.psum_scatter(code_count, "cent", scatter_dimension=0, tiled=True),
    )
    new_codes = (own_sum + code_prior * old_codes) / (own_count[:, None] + code_prior)
    return (new_coarse, new_codes)


def choose(mesh):
    owners, cents = mesh.shape["dp"], mesh.shape["cent"]

    def body(*arrays):
        frame_count, features = arrays[0].shape
        videos = arrays[1].shape[1]
        part = arrays[6].shape[0]
        small = (
            part * owners * cents <= 2 * EXACT
            and arrays[5].shape[0] <= EXACT
            and cents == 4
            and cents * max(2, 2 * videos // owners) == LANES
            and part == 2 * frame_count // videos
            and features % (2 * cents * LANES) == 0
        )
        return (summed_body if small else routed_body)(*arrays)

    return body


def solution(mesh):
    placed = (
        P(("dp", "cent"), None),
        P(("dp", "cent"), None),
        P(("dp", "cent"), None),
        P(("dp", "cent"), None),
        P(("dp", "cent")),
        P("dp", None),
        P(("dp", "cent"), None),
    )
    return jax.shard_map(
        choose(mesh),
        mesh=mesh,
        in_specs=placed,
        out_specs=(P(("dp", "cent"), None), P(("dp", "cent"), None)),
        check_vma=False,
    )
```

```python
import functools

import jax
import jax.numpy as jnp
from jax import lax
from jax.experimental import pallas as pl
from jax.experimental.pallas import tpu as pltpu
from jax.sharding import PartitionSpec as P

code_prior = 16.0
LANES = 128
EXACT = 256
f32 = jnp.float32
bf16 = jnp.bfloat16


def iota(shape, axis):
    return lax.broadcasted_iota(jnp.int32, shape, axis)


def ones_where(mask):
    return jnp.where(mask, jnp.ones((), bf16), jnp.zeros((), bf16))


def fetch(sources, targets, sems):
    copies = [
        pltpu.make_async_copy(source, target, sems.at[at])
        for at, (source, target) in enumerate(zip(sources, targets))
    ]
    for copy in copies:
        copy.start()
    return copies


def dot(left, right):
    return jnp.dot(left, right, preferred_element_type=f32)


def dot_rows(left, right):
    return lax.dot_general(left, right, (((1,), (1,)), ((), ())), preferred_element_type=f32)


def member_of_slots(length_ref, owner_ref, owners, capacity, frame_count):
    videos = length_ref.shape[1]
    slots = owners * capacity
    lengths = length_ref[...].astype(f32)
    owner = owner_ref[...]
    match = (iota((owners, videos), 0) == owner).astype(f32)
    earlier = (iota((videos, videos), 0) < iota((videos, videos), 1)).astype(bf16)
    stacked = jnp.concatenate([match, jnp.broadcast_to(lengths, (8, videos))], axis=0)
    before = dot(stacked.astype(bf16), earlier)
    rank = jnp.sum(before[:owners] * match, axis=0, keepdims=True)
    starts = before[owners : owners + 1]
    slot = owner * capacity + rank.astype(jnp.int32)
    video_of_slot = (iota((slots, videos), 0) == slot).astype(f32).astype(bf16)
    high = jnp.floor(starts / 16.0) * 16.0
    low = starts - high
    tall = lambda row: jnp.broadcast_to(row, (LANES, videos)).astype(bf16)
    start = dot_rows(video_of_slot, tall(high)) + dot_rows(video_of_slot, tall(low))
    length = dot_rows(video_of_slot, tall(lengths))
    first, last = start.astype(jnp.int32), (start + length).astype(jnp.int32)
    member = jnp.concatenate(
        [
            (
                (iota((slots, LANES), 1) + at >= first) & (iota((slots, LANES), 1) + at < last)
            ).astype(f32)
            for at in range(0, frame_count, LANES)
        ],
        axis=1,
    ).astype(bf16)
    return video_of_slot, first, length, member


def code_matches(code_ref, code_total):
    frame_count = code_ref.shape[1]
    return (iota((code_total, frame_count), 0) == code_ref[...]).astype(f32).astype(bf16)


def pool_kernel(
    sizes,
    length_hbm,
    owner_hbm,
    cluster_hbm,
    code_hbm,
    frames_hbm,
    send_hbm,
    pooled_ref,
    member_ref,
    *scratch,
):
    owners, cents, capacity, longest, code_total = sizes
    length_ref, owner_ref, cluster_ref, code_ref, frames_ref, send_ref, sems, out_sems = scratch
    copies = fetch(
        (length_hbm, owner_hbm, cluster_hbm, code_hbm, frames_hbm), scratch[:5], sems
    )
    me = lax.axis_index("cent")
    frame_count, features = frames_hbm.shape
    for copy in copies[:-1]:
        copy.wait()
    slots = owners * capacity
    share = features // cents
    video_of_slot, first, length, member = member_of_slots(
        length_ref, owner_ref, owners, capacity, frame_count
    )
    member_ref[...] = member
    code = (code_ref[...] - EXACT).astype(f32)
    shifted = pltpu.roll(
        jnp.broadcast_to(code, (longest, frame_count)),
        frame_count - (longest - 1),
        1,
        stride=1,
        stride_axis=0,
    ).astype(bf16)
    at_start = jnp.concatenate(
        [
            ((iota((slots, LANES), 1) + at == first) & (length > 0)).astype(f32)
            for at in range(0, frame_count, LANES)
        ],
        axis=1,
    ).astype(bf16)
    slot_codes = dot_rows(shifted, at_start)
    rows = lambda ref: jnp.broadcast_to(ref[...], (longest, ref.shape[1])).astype(f32).astype(bf16)
    slot_length = dot_rows(rows(length_ref), video_of_slot)
    slot_cluster = dot_rows(rows(cluster_ref), video_of_slot)
    back = (longest - 1 - iota((longest, slots), 0)).astype(f32)
    slot_codes = jnp.where(back < slot_length, slot_codes, 2.0 * EXACT)
    slot_cluster = jnp.where(slot_length > 0, slot_cluster, -1.0)
    part = code_total // (owners * cents)
    high = code_ref[...] // part
    high_match = (iota((owners * cents, frame_count), 0) == high).astype(f32).astype(bf16)
    low_match = (iota((part, frame_count), 0) + high * part == code_ref[...]).astype(f32)
    counts = dot_rows(low_match.astype(bf16), high_match)
    half = part // 2
    lane = iota((half, LANES), 1)
    segment = lane // capacity
    last_codes, cluster_place, count_place = (
        segment == lax.rem(me + step, cents) for step in range(1, 4)
    )
    front = lane % capacity < capacity // 2
    for owner in range(owners):
        tile, place = divmod(owner * capacity, LANES)
        lanes = slice(tile * LANES, (tile + 1) * LANES)
        turned = lambda value, step: pltpu.roll(
            value, lax.rem((me + step) * capacity + LANES - place, LANES), 1
        )
        codes = turned(slot_codes[:half, lanes], 0)
        codes = jnp.where(last_codes, turned(slot_codes[half:, lanes], 1), codes)
        note = jnp.where(cluster_place, turned(slot_cluster[:half, lanes], 2), codes)
        for cent in range(cents):
            at = owner * cents + cent
            spread = lambda value: jnp.broadcast_to(value, (half, LANES))
            count = jnp.where(
                front, spread(counts[:half, at : at + 1]), spread(counts[half:, at : at + 1])
            )
            send_ref[owner, cent, 2 * capacity :, :] = jnp.where(count_place, count, note).astype(
                bf16
            )
    weight = 1.0 / jnp.maximum(length, 1.0)
    copies[-1].wait()
    half = share // 2
    out = []
    for cent in range(cents):
        sums = dot(member, frames_ref[:, cent * share : (cent + 1) * share])
        for side in range(2):
            pooled = (sums[:, side * half : (side + 1) * half] * weight).astype(bf16)
            at = cent * share + side * half
            pooled_ref[:, at : at + half] = pooled
            send_ref[:, cent, side * capacity : (side + 1) * capacity, :] = pooled.reshape(
                owners, capacity, half
            )
        out.append(
            pltpu.make_async_copy(send_ref.at[:, cent], send_hbm.at[:, cent], out_sems.at[cent])
        )
        out[-1].start()
    for copy in out:
        copy.wait()


def give_kernel(
    sizes,
    code_hbm,
    frames_hbm,
    pooled_ref,
    member_ref,
    give_ref,
    matches_ref,
    counts_ref,
    code_ref,
    frames_ref,
    sems,
):
    owners, cents, capacity, longest, code_total = sizes
    copies = fetch((code_hbm, frames_hbm), (code_ref, frames_ref), sems)
    me = lax.axis_index("cent")
    share = frames_hbm.shape[1] // cents
    copies[0].wait()
    matches_ref[...] = code_matches(code_ref, code_total)
    counts_ref[...] = dot_rows(matches_ref[...], member_ref[...]).astype(bf16)
    copies[1].wait()
    for step in range(1, cents, 2):
        columns = pl.ds(pl.multiple_of((me ^ step) * share, share), share)
        sums = dot(matches_ref[...], frames_ref[:, columns])
        give_ref[step // 2] = (sums - dot(counts_ref[...], pooled_ref[:, columns])).astype(bf16)


def keep_kernel(sizes, frames_hbm, pooled_ref, matches_ref, counts_ref, keep_ref, frames_ref, sems):
    owners, cents, capacity, longest, code_total = sizes
    me = lax.axis_index("cent")
    share = frames_hbm.shape[1] // cents
    spans = [
        pl.ds(pl.multiple_of((me ^ step) * share, share), share) for step in range(0, cents, 2)
    ]
    copies = fetch(
        [frames_hbm.at[:, span] for span in spans],
        [frames_ref.at[at] for at in range(cents // 2)],
        sems,
    )
    for at, span in enumerate(spans):
        removed = dot(counts_ref[...], pooled_ref[:, span])
        copies[at].wait()
        keep_ref[at] = dot(matches_ref[...], frames_ref[at]) - removed


def slot_rows(got_ref, capacity):
    sources, _, half = got_ref.shape
    return jnp.concatenate(
        [
            got_ref[:, side * capacity : (side + 1) * capacity, :].reshape(sources * capacity, half)
            for side in range(2)
        ],
        axis=1,
    )


def owner_kernel(sizes, got_ref, old_hbm, code_ref, count_ref, here_ref, beside_ref, across_ref, diagonal_ref, old_ref, new_ref, sems):
    owners, cents, capacity, longest, code_total = sizes
    me = lax.axis_index("cent")
    clusters, share = old_ref.shape
    columns = pl.ds(pl.multiple_of(me * share, share), share)
    copies = fetch((old_hbm.at[:, columns],), (old_ref,), sems)
    half = longest // 2
    lane = iota((half, LANES), 1)
    segment = lane // capacity
    zeros = jnp.zeros((half, LANES), f32)
    count = zeros
    cluster_row = iota((clusters, LANES), 0).astype(f32).astype(bf16)
    picks, code_tiles = [], []
    for owner in range(owners):
        front, back, cluster = zeros, zeros, zeros
        for cent in range(cents):
            note = got_ref[owner * cents + cent, 2 * capacity :, :].astype(f32)
            placed = [segment == (cent + step) % cents for step in range(4)]
            front = jnp.where(placed[0], note, front)
            back = jnp.where(placed[1], note, back)
            cluster = jnp.where(placed[2], note, cluster)
            count = count + jnp.where(placed[3], note, 0.0)
        back = pltpu.roll(back, LANES - capacity, 1)
        cluster = pltpu.roll(cluster, LANES - 2 * capacity, 1).astype(bf16)
        picks.append(ones_where(cluster_row == cluster[0:1]))
        code_tiles.append(jnp.concatenate([front, back], axis=0))
    for step in range(cents.bit_length() - 1):
        count = count + pltpu.roll(count, capacity << step, 1)
    other = pltpu.roll(count, capacity // 2, 1)
    first = lane % capacity < capacity // 2
    count_ref[...] = jnp.concatenate(
        [jnp.where(first, count, other), jnp.where(first, other, count)], axis=0
    )
    pick = jnp.concatenate(picks, axis=1)
    rows = slot_rows(got_ref, capacity)
    sums = dot(pick, rows)
    number = dot(pick, jnp.ones((rows.shape[0], LANES), bf16))
    number = jnp.concatenate([number] * (share // LANES), axis=1)
    copies[0].wait()
    new = (sums + old_ref[...].astype(f32)) / (number + 1.0)
    new_ref[...] = new
    anchor = new.astype(bf16)
    bits = longest.bit_length()
    digits = 30 // bits
    block = -(-code_total // digits)
    block = -(-block // 16) * 16
    word_row = iota((block, LANES), 0)
    slot_counts = []
    for codes in code_tiles:
        codes = codes.astype(jnp.int32) + EXACT
        place = jnp.where(codes < code_total, codes, -1)
        one = jnp.ones((longest, LANES), jnp.int32)
        for digit in range(1, -(-code_total // block)):
            above = (codes >= digit * block) & (codes < code_total)
            place = place - jnp.where(above, block, 0)
            one = jnp.where(above, 1 << (bits * digit), one)
        words = jnp.zeros((block, LANES), jnp.int32)
        for row in range(longest):
            words = words + jnp.where(word_row == place[row : row + 1], one[row : row + 1], 0)
        held = []
        for digit in range(-(-code_total // block)):
            height = min(block, code_total - digit * block)
            word = words[:height] >> (bits * digit) & ((1 << bits) - 1)
            held.append(word.astype(f32).astype(bf16))
        slot_counts.append(jnp.concatenate(held, axis=0))
    slot_count = jnp.concatenate(slot_counts, axis=1)
    cluster_count = dot_rows(slot_count, pick)
    high = jnp.floor(cluster_count * (1.0 / EXACT))
    low = cluster_count - high * EXACT
    moved = dot(low.astype(bf16), anchor) + EXACT * dot(high.astype(bf16), anchor)
    code_ref[...] = dot(slot_count, rows) - moved
    quarter = clusters // cents
    rows_of = lambda step: new_ref[pl.ds(pl.multiple_of((me ^ step) * quarter, quarter), quarter), :]
    for step, ref in enumerate((here_ref, beside_ref, across_ref, diagonal_ref)):
        ref[...] = rows_of(step)


def finish_kernel(sizes, got_ref, count_ref, old_ref, out_ref):
    owners, cents, capacity, longest, code_total = sizes
    share = got_ref.shape[2]
    prior = jnp.concatenate([count_ref[...] + code_prior] * (share // LANES), axis=1)
    for cent in range(cents):
        total = got_ref[cent].astype(f32)
        for owner in range(1, owners):
            total = total + got_ref[owner * cents + cent].astype(f32)
        lanes = slice(cent * share, (cent + 1) * share)
        out_ref[:, lanes] = (total + code_prior * old_ref[:, lanes]) / prior


def join_kernel(here_ref, beside_ref, across_ref, diagonal_ref, out_ref):
    me = lax.axis_index("cent")
    share = here_ref.shape[1]
    for step, ref in enumerate((here_ref, beside_ref, across_ref, diagonal_ref)):
        out_ref[:, pl.ds(pl.multiple_of((me ^ step) * share, share), share)] = ref[...]


def summed_body(frames, video_length, video_owner, video_cluster, frame_code, old_coarse, old_codes):
    owners = lax.axis_size("dp")
    cents = lax.axis_size("cent")
    frame_count, features = frames.shape
    videos = video_length.shape[1]
    clusters = old_coarse.shape[0]
    part = old_codes.shape[0]
    code_total = part * owners * cents
    capacity = max(2, 2 * videos // owners)
    longest = 2 * frame_count // videos
    share = features // cents
    devices = owners * cents
    sizes = (owners, cents, capacity, longest, code_total)
    frame_code = frame_code.reshape(1, frame_count)
    vmem = pl.BlockSpec(memory_space=pltpu.VMEM)
    hbm = pl.BlockSpec(memory_space=pltpu.HBM)
    params = pltpu.CompilerParams(vmem_limit_bytes=32 * 1024 * 1024)
    chunk = 2 * capacity + longest // 2
    slots = owners * capacity
    stay = lambda array: pltpu.with_memory_space_constraint(array, pltpu.HBM)
    swap = lambda array, bit: lax.ppermute(
        array, "cent", [(index, index ^ bit) for index in range(cents)]
    )
    row = lambda length: pltpu.VMEM((1, length), jnp.int32)
    frames_scratch = [row(frame_count), pltpu.VMEM((frame_count, features), bf16)]
    quarter = clusters // cents
    send, pooled, member = pl.pallas_call(
        functools.partial(pool_kernel, sizes),
        out_shape=(
            jax.ShapeDtypeStruct((owners, cents, chunk, share // 2), bf16),
            jax.ShapeDtypeStruct((slots, features), bf16),
            jax.ShapeDtypeStruct((slots, frame_count), bf16),
        ),
        in_specs=[hbm] * 5,
        out_specs=(hbm, vmem, vmem),
        scratch_shapes=[row(videos)] * 3
        + frames_scratch
        + [
            pltpu.VMEM((owners, cents, chunk, share // 2), bf16),
            pltpu.SemaphoreType.DMA((5,)),
            pltpu.SemaphoreType.DMA((cents,)),
        ],
        compiler_params=params,
        name="pool",
    )(*map(stay, (video_length, video_owner, video_cluster, frame_code, frames)))
    got = lax.all_to_all(
        send.reshape(devices, chunk, share // 2), ("dp", "cent"), 0, 0, tiled=True
    )
    table = (cents // 2, code_total, share)
    give, matches, slot_counts = pl.pallas_call(
        functools.partial(give_kernel, sizes),
        out_shape=(
            jax.ShapeDtypeStruct(table, bf16),
            jax.ShapeDtypeStruct((code_total, frame_count), bf16),
            jax.ShapeDtypeStruct((code_total, slots), bf16),
        ),
        in_specs=[hbm] * 2 + [vmem] * 2,
        out_specs=(vmem,) * 3,
        scratch_shapes=frames_scratch + [pltpu.SemaphoreType.DMA((2,))],
        compiler_params=params,
        cost_estimate=pl.CostEstimate(
            flops=2 * code_total * frame_count * features,
            bytes_accessed=4 * frame_count * features,
            transcendentals=0,
        ),
        name="give",
    )(stay(frame_code), stay(frames), pooled, member)
    near = swap(give, 1)
    keep = pl.pallas_call(
        functools.partial(keep_kernel, sizes),
        out_shape=jax.ShapeDtypeStruct(table, f32),
        in_specs=[hbm] + [vmem] * 3,
        out_specs=vmem,
        scratch_shapes=[
            pltpu.VMEM((cents // 2, frame_count, share), bf16),
            pltpu.SemaphoreType.DMA((cents // 2,)),
        ],
        compiler_params=params,
        cost_estimate=pl.CostEstimate(
            flops=2 * code_total * frame_count * features,
            bytes_accessed=4 * frame_count * features,
            transcendentals=0,
        ),
        name="keep",
    )(stay(frames), pooled, matches, slot_counts)
    far = swap((keep[1] + near[1].astype(f32)).astype(bf16), 2)
    piece = jax.ShapeDtypeStruct((quarter, share), f32)
    sums, count, here, beside, across, diagonal = pl.pallas_call(
        functools.partial(owner_kernel, sizes),
        out_shape=(
            jax.ShapeDtypeStruct((code_total, share), f32),
            jax.ShapeDtypeStruct((part, LANES), f32),
        )
        + (piece,) * cents,
        in_specs=[vmem, hbm],
        out_specs=(vmem,) * (2 + cents),
        scratch_shapes=[
            pltpu.VMEM((clusters, share), bf16),
            pltpu.VMEM((clusters, share), f32),
            pltpu.SemaphoreType.DMA((1,)),
        ],
        compiler_params=params,
        name="owner",
    )(got, stay(old_coarse))
    sums = (sums + (keep[0] + near[0].astype(f32) + far.astype(f32))).astype(bf16)
    last = lax.all_to_all(sums.reshape(devices, part, share), ("dp", "cent"), 0, 0, tiled=True)
    new_coarse = pl.pallas_call(
        join_kernel,
        out_shape=jax.ShapeDtypeStruct((quarter, features), f32),
        in_specs=[vmem] * 4,
        out_specs=vmem,
        compiler_params=params,
        name="join",
    )(here, swap(beside, 1), swap(across, 2), swap(diagonal, 3))
    new_codes = pl.pallas_call(
        functools.partial(finish_kernel, sizes),
        out_shape=jax.ShapeDtypeStruct((part, features), f32),
        in_specs=[vmem] * 3,
        out_specs=vmem,
        compiler_params=params,
        name="finish",
    )(last, count, old_codes)
    return new_coarse, new_codes


def owner_slots(target, target_count, capacity):
    matches = (target[:, None] == jnp.arange(target_count, dtype=jnp.int32)[None, :]).astype(
        jnp.int32
    )
    before = jnp.cumsum(matches, axis=0) - matches
    slot_rank = jnp.sum(before * matches, axis=1)
    return target * capacity + slot_rank


def invert_slots(slot_list, slot_total):
    item_index = jnp.arange(slot_list.shape[0], dtype=jnp.int32)
    source = jnp.zeros((slot_total,), jnp.int32).at[slot_list].set(item_index)
    filled = jnp.zeros((slot_total,), jnp.int32).at[slot_list].set(1)
    return (source, filled)


def routed_body(frames, video_length, video_owner, video_cluster, frame_code, old_coarse, old_codes):
    dp_count = lax.axis_size("dp")
    cent_count = lax.axis_size("cent")
    frame_count, features = frames.shape
    video_count = video_length.shape[1]
    coarse_rows = old_coarse.shape[0]
    code_share = old_codes.shape[0]
    code_block = code_share * cent_count
    cap_video = max(2, 2 * video_count // dp_count)
    cap_frame = max(2, 2 * frame_count // dp_count)
    lengths = video_length[0]
    target = video_owner[0]
    cluster = video_cluster[0]
    video_ends = jnp.cumsum(lengths)
    video_starts = video_ends - lengths
    position = jnp.arange(frame_count, dtype=jnp.int32)
    member = (
        (position[None, :] >= video_starts[:, None]) & (position[None, :] < video_ends[:, None])
    ).astype(jnp.bfloat16)
    video_sums = jnp.dot(member, frames, preferred_element_type=jnp.float32)
    pooled = (video_sums / lengths[:, None].astype(jnp.float32)).astype(jnp.bfloat16)
    video_slot = owner_slots(target, dp_count, cap_video)
    source, filled = invert_slots(video_slot, dp_count * cap_video)
    send_rows = jnp.where(filled[:, None] > 0, pooled[source], jnp.zeros((), jnp.bfloat16))
    send_codes = jnp.where(filled > 0, cluster[source], -1)
    got_rows, got_codes = (
        lax.all_to_all(
            send_rows.reshape(dp_count, cap_video, features),
            "dp",
            split_axis=0,
            concat_axis=0,
            tiled=True,
        ),
        lax.all_to_all(
            send_codes.reshape(dp_count, cap_video), "dp", split_axis=0, concat_axis=0, tiled=True
        ),
    )
    got_rows = got_rows.reshape(-1, features)
    got_codes = got_codes.reshape(-1)
    table_index = jnp.arange(coarse_rows, dtype=jnp.int32)
    coarse_pick = (got_codes[None, :] == table_index[:, None]).astype(jnp.bfloat16)
    coarse_sum = jnp.dot(coarse_pick, got_rows, preferred_element_type=jnp.float32)
    coarse_count = jnp.sum(coarse_pick.astype(jnp.float32), axis=1)
    quarter = coarse_rows // cent_count
    part_sum, part_count = (
        lax.psum_scatter(coarse_sum, "cent", scatter_dimension=0, tiled=True),
        lax.psum_scatter(coarse_count, "cent", scatter_dimension=0, tiled=True),
    )
    first_row = lax.axis_index("cent") * quarter
    old_part = lax.dynamic_slice_in_dim(old_coarse, first_row, quarter, 0).astype(jnp.float32)
    new_coarse = (part_sum + old_part) / (part_count[:, None] + 1.0)
    anchor_table = lax.all_gather(new_coarse.astype(jnp.bfloat16), "cent", axis=0, tiled=True)
    slot_anchor = jnp.dot(coarse_pick.T, anchor_table, preferred_element_type=jnp.float32).astype(
        jnp.bfloat16
    )
    returned = lax.all_to_all(
        slot_anchor.reshape(dp_count, cap_video, features),
        "dp",
        split_axis=0,
        concat_axis=0,
        tiled=True,
    )
    video_anchor = returned.reshape(-1, features)[video_slot]
    frame_anchor = jnp.dot(member.T, video_anchor, preferred_element_type=jnp.float32)
    residual = (frames - frame_anchor).astype(jnp.bfloat16)
    code_target = frame_code // code_block
    code_offset = frame_code - code_target * code_block
    frame_slot = owner_slots(code_target, dp_count, cap_frame)
    source, filled = invert_slots(frame_slot, dp_count * cap_frame)
    slot_rows = jnp.where(filled[:, None] > 0, residual[source], jnp.zeros((), jnp.bfloat16))
    slot_codes = jnp.where(filled > 0, code_offset[source], -1)
    code_rows, code_ids = (
        lax.all_to_all(
            slot_rows.reshape(dp_count, cap_frame, features),
            "dp",
            split_axis=0,
            concat_axis=0,
            tiled=True,
        ),
        lax.all_to_all(
            slot_codes.reshape(dp_count, cap_frame), "dp", split_axis=0, concat_axis=0, tiled=True
        ),
    )
    code_index = jnp.arange(code_block, dtype=jnp.int32)
    code_pick = (code_ids.reshape(-1)[None, :] == code_index[:, None]).astype(jnp.bfloat16)
    code_sum = jnp.dot(
        code_pick, code_rows.reshape(-1, features), preferred_element_type=jnp.float32
    )
    code_count = jnp.sum(code_pick.astype(jnp.float32), axis=1)
    own_sum, own_count = (
        lax.psum_scatter(code_sum, "cent", scatter_dimension=0, tiled=True),
        lax.psum_scatter(code_count, "cent", scatter_dimension=0, tiled=True),
    )
    new_codes = (own_sum + code_prior * old_codes) / (own_count[:, None] + code_prior)
    return (new_coarse, new_codes)


def choose(mesh):
    owners, cents = mesh.shape["dp"], mesh.shape["cent"]

    def body(*arrays):
        frame_count, features = arrays[0].shape
        videos = arrays[1].shape[1]
        part = arrays[6].shape[0]
        small = (
            part * owners * cents <= 2 * EXACT
            and arrays[5].shape[0] <= EXACT
            and cents == 4
            and cents * max(2, 2 * videos // owners) == LANES
            and part == 2 * frame_count // videos
            and features % (2 * cents * LANES) == 0
        )
        return (summed_body if small else routed_body)(*arrays)

    return body


def solution(mesh):
    placed = (
        P(("dp", "cent"), None),
        P(("dp", "cent"), None),
        P(("dp", "cent"), None),
        P(("dp", "cent"), None),
        P(("dp", "cent")),
        P("dp", None),
        P(("dp", "cent"), None),
    )
    return jax.shard_map(
        choose(mesh),
        mesh=mesh,
        in_specs=placed,
        out_specs=(P(("dp", "cent"), None), P(("dp", "cent"), None)),
        check_vma=False,
    )
```

```python
import functools

import jax
import jax.numpy as jnp
from jax import lax
from jax.experimental import pallas as pl
from jax.experimental.pallas import tpu as pltpu
from jax.sharding import PartitionSpec as P

code_prior = 16.0
LANES = 128
EXACT = 256
f32 = jnp.float32
bf16 = jnp.bfloat16


def iota(shape, axis):
    return lax.broadcasted_iota(jnp.int32, shape, axis)


def ones_where(mask):
    return jnp.where(mask, jnp.ones((), bf16), jnp.zeros((), bf16))


def fetch(sources, targets, sems):
    copies = [
        pltpu.make_async_copy(source, target, sems.at[at])
        for at, (source, target) in enumerate(zip(sources, targets))
    ]
    for copy in copies:
        copy.start()
    return copies


def dot(left, right):
    return jnp.dot(left, right, preferred_element_type=f32)


def dot_rows(left, right):
    return lax.dot_general(left, right, (((1,), (1,)), ((), ())), preferred_element_type=f32)


def member_of_slots(length_ref, owner_ref, owners, capacity, frame_count):
    videos = length_ref.shape[1]
    slots = owners * capacity
    lengths = length_ref[...].astype(f32)
    owner = owner_ref[...]
    match = (iota((owners, videos), 0) == owner).astype(f32)
    earlier = (iota((videos, videos), 0) < iota((videos, videos), 1)).astype(bf16)
    stacked = jnp.concatenate([match, jnp.broadcast_to(lengths, (8, videos))], axis=0)
    before = dot(stacked.astype(bf16), earlier)
    rank = jnp.sum(before[:owners] * match, axis=0, keepdims=True)
    starts = before[owners : owners + 1]
    slot = owner * capacity + rank.astype(jnp.int32)
    video_of_slot = (iota((slots, videos), 0) == slot).astype(f32).astype(bf16)
    high = jnp.floor(starts / 16.0) * 16.0
    low = starts - high
    tall = lambda row: jnp.broadcast_to(row, (LANES, videos)).astype(bf16)
    start = dot_rows(video_of_slot, tall(high)) + dot_rows(video_of_slot, tall(low))
    length = dot_rows(video_of_slot, tall(lengths))
    first, last = start.astype(jnp.int32), (start + length).astype(jnp.int32)
    member = jnp.concatenate(
        [
            (
                (iota((slots, LANES), 1) + at >= first) & (iota((slots, LANES), 1) + at < last)
            ).astype(f32)
            for at in range(0, frame_count, LANES)
        ],
        axis=1,
    ).astype(bf16)
    return video_of_slot, first, length, member


def code_matches(code_ref, code_total):
    frame_count = code_ref.shape[1]
    return (iota((code_total, frame_count), 0) == code_ref[...]).astype(f32).astype(bf16)


def pool_kernel(
    sizes,
    length_hbm,
    owner_hbm,
    cluster_hbm,
    code_hbm,
    frames_hbm,
    send_hbm,
    pooled_ref,
    member_ref,
    *scratch,
):
    owners, cents, capacity, longest, code_total = sizes
    length_ref, owner_ref, cluster_ref, code_ref, frames_ref, send_ref, sems, out_sems = scratch
    copies = fetch(
        (length_hbm, owner_hbm, cluster_hbm, code_hbm, frames_hbm), scratch[:5], sems
    )
    me = lax.axis_index("cent")
    frame_count, features = frames_hbm.shape
    for copy in copies[:-1]:
        copy.wait()
    slots = owners * capacity
    share = features // cents
    video_of_slot, first, length, member = member_of_slots(
        length_ref, owner_ref, owners, capacity, frame_count
    )
    member_ref[...] = member
    code = (code_ref[...] - EXACT).astype(f32)
    shifted = pltpu.roll(
        jnp.broadcast_to(code, (longest, frame_count)),
        frame_count - (longest - 1),
        1,
        stride=1,
        stride_axis=0,
    ).astype(bf16)
    at_start = jnp.concatenate(
        [
            ((iota((slots, LANES), 1) + at == first) & (length > 0)).astype(f32)
            for at in range(0, frame_count, LANES)
        ],
        axis=1,
    ).astype(bf16)
    slot_codes = dot_rows(shifted, at_start)
    rows = lambda ref: jnp.broadcast_to(ref[...], (longest, ref.shape[1])).astype(f32).astype(bf16)
    slot_length = dot_rows(rows(length_ref), video_of_slot)
    slot_cluster = dot_rows(rows(cluster_ref), video_of_slot)
    back = (longest - 1 - iota((longest, slots), 0)).astype(f32)
    slot_codes = jnp.where(back < slot_length, slot_codes, 2.0 * EXACT)
    slot_cluster = jnp.where(slot_length > 0, slot_cluster, -1.0)
    part = code_total // (owners * cents)
    high = code_ref[...] // part
    high_match = (iota((owners * cents, frame_count), 0) == high).astype(f32).astype(bf16)
    low_match = (iota((part, frame_count), 0) + high * part == code_ref[...]).astype(f32)
    counts = dot_rows(low_match.astype(bf16), high_match)
    half = part // 2
    lane = iota((half, LANES), 1)
    segment = lane // capacity
    last_codes, cluster_place, count_place = (
        segment == lax.rem(me + step, cents) for step in range(1, 4)
    )
    front = lane % capacity < capacity // 2
    for owner in range(owners):
        tile, place = divmod(owner * capacity, LANES)
        lanes = slice(tile * LANES, (tile + 1) * LANES)
        turned = lambda value, step: pltpu.roll(
            value, lax.rem((me + step) * capacity + LANES - place, LANES), 1
        )
        codes = turned(slot_codes[:half, lanes], 0)
        codes = jnp.where(last_codes, turned(slot_codes[half:, lanes], 1), codes)
        note = jnp.where(cluster_place, turned(slot_cluster[:half, lanes], 2), codes)
        for cent in range(cents):
            at = owner * cents + cent
            spread = lambda value: jnp.broadcast_to(value, (half, LANES))
            count = jnp.where(
                front, spread(counts[:half, at : at + 1]), spread(counts[half:, at : at + 1])
            )
            send_ref[owner, cent, 2 * capacity :, :] = jnp.where(count_place, count, note).astype(
                bf16
            )
    weight = 1.0 / jnp.maximum(length, 1.0)
    copies[-1].wait()
    half = share // 2
    out = []
    for cent in range(cents):
        sums = dot(member, frames_ref[:, cent * share : (cent + 1) * share])
        for side in range(2):
            pooled = (sums[:, side * half : (side + 1) * half] * weight).astype(bf16)
            at = cent * share + side * half
            pooled_ref[:, at : at + half] = pooled
            send_ref[:, cent, side * capacity : (side + 1) * capacity, :] = pooled.reshape(
                owners, capacity, half
            )
        out.append(
            pltpu.make_async_copy(send_ref.at[:, cent], send_hbm.at[:, cent], out_sems.at[cent])
        )
        out[-1].start()
    for copy in out:
        copy.wait()


def give_kernel(
    sizes,
    code_hbm,
    frames_hbm,
    pooled_ref,
    member_ref,
    give_ref,
    matches_ref,
    counts_ref,
    code_ref,
    frames_ref,
    sems,
):
    owners, cents, capacity, longest, code_total = sizes
    copies = fetch((code_hbm, frames_hbm), (code_ref, frames_ref), sems)
    me = lax.axis_index("cent")
    share = frames_hbm.shape[1] // cents
    copies[0].wait()
    matches_ref[...] = code_matches(code_ref, code_total)
    counts_ref[...] = dot_rows(matches_ref[...], member_ref[...]).astype(bf16)
    copies[1].wait()
    for step in range(1, cents, 2):
        columns = pl.ds(pl.multiple_of((me ^ step) * share, share), share)
        sums = dot(matches_ref[...], frames_ref[:, columns])
        give_ref[step // 2] = (sums - dot(counts_ref[...], pooled_ref[:, columns])).astype(bf16)


def keep_kernel(sizes, frames_hbm, pooled_ref, matches_ref, counts_ref, keep_ref, frames_ref, sems):
    owners, cents, capacity, longest, code_total = sizes
    me = lax.axis_index("cent")
    share = frames_hbm.shape[1] // cents
    spans = [
        pl.ds(pl.multiple_of((me ^ step) * share, share), share) for step in range(0, cents, 2)
    ]
    copies = fetch(
        [frames_hbm.at[:, span] for span in spans],
        [frames_ref.at[at] for at in range(cents // 2)],
        sems,
    )
    for at, span in enumerate(spans):
        removed = dot(counts_ref[...], pooled_ref[:, span])
        copies[at].wait()
        keep_ref[at] = dot(matches_ref[...], frames_ref[at]) - removed


def slot_rows(got_ref, capacity):
    sources, _, half = got_ref.shape
    return jnp.concatenate(
        [
            got_ref[:, side * capacity : (side + 1) * capacity, :].reshape(sources * capacity, half)
            for side in range(2)
        ],
        axis=1,
    )


def owner_kernel(sizes, got_ref, old_ref, code_ref, count_ref, here_ref, beside_ref, across_ref, diagonal_ref, new_ref):
    owners, cents, capacity, longest, code_total = sizes
    me = lax.axis_index("cent")
    clusters, share = old_ref.shape
    half = longest // 2
    lane = iota((half, LANES), 1)
    segment = lane // capacity
    zeros = jnp.zeros((half, LANES), f32)
    count = zeros
    cluster_row = iota((clusters, LANES), 0).astype(f32).astype(bf16)
    picks, code_tiles = [], []
    for owner in range(owners):
        front, back, cluster = zeros, zeros, zeros
        for cent in range(cents):
            note = got_ref[owner * cents + cent, 2 * capacity :, :].astype(f32)
            placed = [segment == (cent + step) % cents for step in range(4)]
            front = jnp.where(placed[0], note, front)
            back = jnp.where(placed[1], note, back)
            cluster = jnp.where(placed[2], note, cluster)
            count = count + jnp.where(placed[3], note, 0.0)
        back = pltpu.roll(back, LANES - capacity, 1)
        cluster = pltpu.roll(cluster, LANES - 2 * capacity, 1).astype(bf16)
        picks.append(ones_where(cluster_row == cluster[0:1]))
        code_tiles.append(jnp.concatenate([front, back], axis=0))
    for step in range(cents.bit_length() - 1):
        count = count + pltpu.roll(count, capacity << step, 1)
    other = pltpu.roll(count, capacity // 2, 1)
    first = lane % capacity < capacity // 2
    count_ref[...] = jnp.concatenate(
        [jnp.where(first, count, other), jnp.where(first, other, count)], axis=0
    )
    pick = jnp.concatenate(picks, axis=1)
    rows = slot_rows(got_ref, capacity)
    sums = dot(pick, rows)
    number = dot(pick, jnp.ones((rows.shape[0], LANES), bf16))
    number = jnp.concatenate([number] * (share // LANES), axis=1)
    new = (sums + old_ref[...].astype(f32)) / (number + 1.0)
    new_ref[...] = new
    anchor = new.astype(bf16)
    bits = longest.bit_length()
    digits = 30 // bits
    block = -(-code_total // digits)
    block = -(-block // 16) * 16
    word_row = iota((block, LANES), 0)
    slot_counts = []
    for codes in code_tiles:
        codes = codes.astype(jnp.int32) + EXACT
        place = jnp.where(codes < code_total, codes, -1)
        one = jnp.ones((longest, LANES), jnp.int32)
        for digit in range(1, -(-code_total // block)):
            above = (codes >= digit * block) & (codes < code_total)
            place = place - jnp.where(above, block, 0)
            one = jnp.where(above, 1 << (bits * digit), one)
        words = jnp.zeros((block, LANES), jnp.int32)
        for row in range(longest):
            words = words + jnp.where(word_row == place[row : row + 1], one[row : row + 1], 0)
        held = []
        for digit in range(-(-code_total // block)):
            height = min(block, code_total - digit * block)
            word = words[:height] >> (bits * digit) & ((1 << bits) - 1)
            held.append(word.astype(f32).astype(bf16))
        slot_counts.append(jnp.concatenate(held, axis=0))
    slot_count = jnp.concatenate(slot_counts, axis=1)
    cluster_count = dot_rows(slot_count, pick)
    high = jnp.floor(cluster_count * (1.0 / EXACT))
    low = cluster_count - high * EXACT
    moved = dot(low.astype(bf16), anchor) + EXACT * dot(high.astype(bf16), anchor)
    code_ref[...] = dot(slot_count, rows) - moved
    quarter = clusters // cents
    rows_of = lambda step: new_ref[pl.ds(pl.multiple_of((me ^ step) * quarter, quarter), quarter), :]
    for step, ref in enumerate((here_ref, beside_ref, across_ref, diagonal_ref)):
        ref[...] = rows_of(step)


def finish_kernel(sizes, got_ref, count_ref, old_ref, out_ref):
    owners, cents, capacity, longest, code_total = sizes
    share = got_ref.shape[2]
    prior = jnp.concatenate([count_ref[...] + code_prior] * (share // LANES), axis=1)
    for cent in range(cents):
        total = got_ref[cent].astype(f32)
        for owner in range(1, owners):
            total = total + got_ref[owner * cents + cent].astype(f32)
        lanes = slice(cent * share, (cent + 1) * share)
        out_ref[:, lanes] = (total + code_prior * old_ref[:, lanes]) / prior


def join_kernel(here_ref, beside_ref, across_ref, diagonal_ref, out_ref):
    me = lax.axis_index("cent")
    share = here_ref.shape[1]
    for step, ref in enumerate((here_ref, beside_ref, across_ref, diagonal_ref)):
        out_ref[:, pl.ds(pl.multiple_of((me ^ step) * share, share), share)] = ref[...]


def summed_body(frames, video_length, video_owner, video_cluster, frame_code, old_coarse, old_codes):
    owners = lax.axis_size("dp")
    cents = lax.axis_size("cent")
    frame_count, features = frames.shape
    videos = video_length.shape[1]
    clusters = old_coarse.shape[0]
    part = old_codes.shape[0]
    code_total = part * owners * cents
    capacity = max(2, 2 * videos // owners)
    longest = 2 * frame_count // videos
    share = features // cents
    devices = owners * cents
    sizes = (owners, cents, capacity, longest, code_total)
    frame_code = frame_code.reshape(1, frame_count)
    vmem = pl.BlockSpec(memory_space=pltpu.VMEM)
    hbm = pl.BlockSpec(memory_space=pltpu.HBM)
    params = pltpu.CompilerParams(vmem_limit_bytes=32 * 1024 * 1024)
    chunk = 2 * capacity + longest // 2
    slots = owners * capacity
    stay = lambda array: pltpu.with_memory_space_constraint(array, pltpu.HBM)
    swap = lambda array, bit: lax.ppermute(
        array, "cent", [(index, index ^ bit) for index in range(cents)]
    )
    row = lambda length: pltpu.VMEM((1, length), jnp.int32)
    frames_scratch = [row(frame_count), pltpu.VMEM((frame_count, features), bf16)]
    quarter = clusters // cents
    send, pooled, member = pl.pallas_call(
        functools.partial(pool_kernel, sizes),
        out_shape=(
            jax.ShapeDtypeStruct((owners, cents, chunk, share // 2), bf16),
            jax.ShapeDtypeStruct((slots, features), bf16),
            jax.ShapeDtypeStruct((slots, frame_count), bf16),
        ),
        in_specs=[hbm] * 5,
        out_specs=(hbm, vmem, vmem),
        scratch_shapes=[row(videos)] * 3
        + frames_scratch
        + [
            pltpu.VMEM((owners, cents, chunk, share // 2), bf16),
            pltpu.SemaphoreType.DMA((5,)),
            pltpu.SemaphoreType.DMA((cents,)),
        ],
        compiler_params=params,
        name="pool",
    )(*map(stay, (video_length, video_owner, video_cluster, frame_code, frames)))
    got = lax.all_to_all(
        send.reshape(devices, chunk, share // 2), ("dp", "cent"), 0, 0, tiled=True
    )
    table = (cents // 2, code_total, share)
    give, matches, slot_counts = pl.pallas_call(
        functools.partial(give_kernel, sizes),
        out_shape=(
            jax.ShapeDtypeStruct(table, bf16),
            jax.ShapeDtypeStruct((code_total, frame_count), bf16),
            jax.ShapeDtypeStruct((code_total, slots), bf16),
        ),
        in_specs=[hbm] * 2 + [vmem] * 2,
        out_specs=(vmem,) * 3,
        scratch_shapes=frames_scratch + [pltpu.SemaphoreType.DMA((2,))],
        compiler_params=params,
        cost_estimate=pl.CostEstimate(
            flops=2 * code_total * frame_count * features,
            bytes_accessed=4 * frame_count * features,
            transcendentals=0,
        ),
        name="give",
    )(stay(frame_code), stay(frames), pooled, member)
    near = swap(give, 1)
    keep = pl.pallas_call(
        functools.partial(keep_kernel, sizes),
        out_shape=jax.ShapeDtypeStruct(table, f32),
        in_specs=[hbm] + [vmem] * 3,
        out_specs=vmem,
        scratch_shapes=[
            pltpu.VMEM((cents // 2, frame_count, share), bf16),
            pltpu.SemaphoreType.DMA((cents // 2,)),
        ],
        compiler_params=params,
        cost_estimate=pl.CostEstimate(
            flops=2 * code_total * frame_count * features,
            bytes_accessed=4 * frame_count * features,
            transcendentals=0,
        ),
        name="keep",
    )(stay(frames), pooled, matches, slot_counts)
    far = swap((keep[1] + near[1].astype(f32)).astype(bf16), 2)
    piece = jax.ShapeDtypeStruct((quarter, share), f32)
    first = lax.axis_index("cent") * share
    old_part = lax.dynamic_slice_in_dim(old_coarse, first, share, 1)
    sums, count, here, beside, across, diagonal = pl.pallas_call(
        functools.partial(owner_kernel, sizes),
        out_shape=(
            jax.ShapeDtypeStruct((code_total, share), f32),
            jax.ShapeDtypeStruct((part, LANES), f32),
        )
        + (piece,) * cents,
        in_specs=[vmem, vmem],
        out_specs=(vmem,) * (2 + cents),
        scratch_shapes=[pltpu.VMEM((clusters, share), f32)],
        compiler_params=params,
        name="owner",
    )(got, old_part)
    sums = (sums + (keep[0] + near[0].astype(f32) + far.astype(f32))).astype(bf16)
    last = lax.all_to_all(sums.reshape(devices, part, share), ("dp", "cent"), 0, 0, tiled=True)
    new_coarse = pl.pallas_call(
        join_kernel,
        out_shape=jax.ShapeDtypeStruct((quarter, features), f32),
        in_specs=[vmem] * 4,
        out_specs=vmem,
        compiler_params=params,
        name="join",
    )(here, swap(beside, 1), swap(across, 2), swap(diagonal, 3))
    new_codes = pl.pallas_call(
        functools.partial(finish_kernel, sizes),
        out_shape=jax.ShapeDtypeStruct((part, features), f32),
        in_specs=[vmem] * 3,
        out_specs=vmem,
        compiler_params=params,
        name="finish",
    )(last, count, old_codes)
    return new_coarse, new_codes


def owner_slots(target, target_count, capacity):
    matches = (target[:, None] == jnp.arange(target_count, dtype=jnp.int32)[None, :]).astype(
        jnp.int32
    )
    before = jnp.cumsum(matches, axis=0) - matches
    slot_rank = jnp.sum(before * matches, axis=1)
    return target * capacity + slot_rank


def invert_slots(slot_list, slot_total):
    item_index = jnp.arange(slot_list.shape[0], dtype=jnp.int32)
    source = jnp.zeros((slot_total,), jnp.int32).at[slot_list].set(item_index)
    filled = jnp.zeros((slot_total,), jnp.int32).at[slot_list].set(1)
    return (source, filled)


def routed_body(frames, video_length, video_owner, video_cluster, frame_code, old_coarse, old_codes):
    dp_count = lax.axis_size("dp")
    cent_count = lax.axis_size("cent")
    frame_count, features = frames.shape
    video_count = video_length.shape[1]
    coarse_rows = old_coarse.shape[0]
    code_share = old_codes.shape[0]
    code_block = code_share * cent_count
    cap_video = max(2, 2 * video_count // dp_count)
    cap_frame = max(2, 2 * frame_count // dp_count)
    lengths = video_length[0]
    target = video_owner[0]
    cluster = video_cluster[0]
    video_ends = jnp.cumsum(lengths)
    video_starts = video_ends - lengths
    position = jnp.arange(frame_count, dtype=jnp.int32)
    member = (
        (position[None, :] >= video_starts[:, None]) & (position[None, :] < video_ends[:, None])
    ).astype(jnp.bfloat16)
    video_sums = jnp.dot(member, frames, preferred_element_type=jnp.float32)
    pooled = (video_sums / lengths[:, None].astype(jnp.float32)).astype(jnp.bfloat16)
    video_slot = owner_slots(target, dp_count, cap_video)
    source, filled = invert_slots(video_slot, dp_count * cap_video)
    send_rows = jnp.where(filled[:, None] > 0, pooled[source], jnp.zeros((), jnp.bfloat16))
    send_codes = jnp.where(filled > 0, cluster[source], -1)
    got_rows, got_codes = (
        lax.all_to_all(
            send_rows.reshape(dp_count, cap_video, features),
            "dp",
            split_axis=0,
            concat_axis=0,
            tiled=True,
        ),
        lax.all_to_all(
            send_codes.reshape(dp_count, cap_video), "dp", split_axis=0, concat_axis=0, tiled=True
        ),
    )
    got_rows = got_rows.reshape(-1, features)
    got_codes = got_codes.reshape(-1)
    table_index = jnp.arange(coarse_rows, dtype=jnp.int32)
    coarse_pick = (got_codes[None, :] == table_index[:, None]).astype(jnp.bfloat16)
    coarse_sum = jnp.dot(coarse_pick, got_rows, preferred_element_type=jnp.float32)
    coarse_count = jnp.sum(coarse_pick.astype(jnp.float32), axis=1)
    quarter = coarse_rows // cent_count
    part_sum, part_count = (
        lax.psum_scatter(coarse_sum, "cent", scatter_dimension=0, tiled=True),
        lax.psum_scatter(coarse_count, "cent", scatter_dimension=0, tiled=True),
    )
    first_row = lax.axis_index("cent") * quarter
    old_part = lax.dynamic_slice_in_dim(old_coarse, first_row, quarter, 0).astype(jnp.float32)
    new_coarse = (part_sum + old_part) / (part_count[:, None] + 1.0)
    anchor_table = lax.all_gather(new_coarse.astype(jnp.bfloat16), "cent", axis=0, tiled=True)
    slot_anchor = jnp.dot(coarse_pick.T, anchor_table, preferred_element_type=jnp.float32).astype(
        jnp.bfloat16
    )
    returned = lax.all_to_all(
        slot_anchor.reshape(dp_count, cap_video, features),
        "dp",
        split_axis=0,
        concat_axis=0,
        tiled=True,
    )
    video_anchor = returned.reshape(-1, features)[video_slot]
    frame_anchor = jnp.dot(member.T, video_anchor, preferred_element_type=jnp.float32)
    residual = (frames - frame_anchor).astype(jnp.bfloat16)
    code_target = frame_code // code_block
    code_offset = frame_code - code_target * code_block
    frame_slot = owner_slots(code_target, dp_count, cap_frame)
    source, filled = invert_slots(frame_slot, dp_count * cap_frame)
    slot_rows = jnp.where(filled[:, None] > 0, residual[source], jnp.zeros((), jnp.bfloat16))
    slot_codes = jnp.where(filled > 0, code_offset[source], -1)
    code_rows, code_ids = (
        lax.all_to_all(
            slot_rows.reshape(dp_count, cap_frame, features),
            "dp",
            split_axis=0,
            concat_axis=0,
            tiled=True,
        ),
        lax.all_to_all(
            slot_codes.reshape(dp_count, cap_frame), "dp", split_axis=0, concat_axis=0, tiled=True
        ),
    )
    code_index = jnp.arange(code_block, dtype=jnp.int32)
    code_pick = (code_ids.reshape(-1)[None, :] == code_index[:, None]).astype(jnp.bfloat16)
    code_sum = jnp.dot(
        code_pick, code_rows.reshape(-1, features), preferred_element_type=jnp.float32
    )
    code_count = jnp.sum(code_pick.astype(jnp.float32), axis=1)
    own_sum, own_count = (
        lax.psum_scatter(code_sum, "cent", scatter_dimension=0, tiled=True),
        lax.psum_scatter(code_count, "cent", scatter_dimension=0, tiled=True),
    )
    new_codes = (own_sum + code_prior * old_codes) / (own_count[:, None] + code_prior)
    return (new_coarse, new_codes)


def choose(mesh):
    owners, cents = mesh.shape["dp"], mesh.shape["cent"]

    def body(*arrays):
        frame_count, features = arrays[0].shape
        videos = arrays[1].shape[1]
        part = arrays[6].shape[0]
        small = (
            part * owners * cents <= 2 * EXACT
            and arrays[5].shape[0] <= EXACT
            and cents == 4
            and cents * max(2, 2 * videos // owners) == LANES
            and part == 2 * frame_count // videos
            and features % (2 * cents * LANES) == 0
        )
        return (summed_body if small else routed_body)(*arrays)

    return body


def solution(mesh):
    placed = (
        P(("dp", "cent"), None),
        P(("dp", "cent"), None),
        P(("dp", "cent"), None),
        P(("dp", "cent"), None),
        P(("dp", "cent")),
        P("dp", None),
        P(("dp", "cent"), None),
    )
    return jax.shard_map(
        choose(mesh),
        mesh=mesh,
        in_specs=placed,
        out_specs=(P(("dp", "cent"), None), P(("dp", "cent"), None)),
        check_vma=False,
    )
```

```python
import functools

import jax
import jax.numpy as jnp
from jax import lax
from jax.experimental import pallas as pl
from jax.experimental.pallas import tpu as pltpu
from jax.sharding import PartitionSpec as P

code_prior = 16.0
LANES = 128
EXACT = 256
f32 = jnp.float32
bf16 = jnp.bfloat16


def iota(shape, axis):
    return lax.broadcasted_iota(jnp.int32, shape, axis)


def ones_where(mask):
    return jnp.where(mask, jnp.ones((), bf16), jnp.zeros((), bf16))


def fetch(sources, targets, sems):
    copies = [
        pltpu.make_async_copy(source, target, sems.at[at])
        for at, (source, target) in enumerate(zip(sources, targets))
    ]
    for copy in copies:
        copy.start()
    return copies


def dot(left, right):
    return jnp.dot(left, right, preferred_element_type=f32)


def dot_rows(left, right):
    return lax.dot_general(left, right, (((1,), (1,)), ((), ())), preferred_element_type=f32)


def member_of_slots(length_ref, owner_ref, owners, capacity, frame_count):
    videos = length_ref.shape[1]
    slots = owners * capacity
    lengths = length_ref[...].astype(f32)
    owner = owner_ref[...]
    match = (iota((owners, videos), 0) == owner).astype(f32)
    earlier = (iota((videos, videos), 0) < iota((videos, videos), 1)).astype(bf16)
    stacked = jnp.concatenate([match, jnp.broadcast_to(lengths, (8, videos))], axis=0)
    before = dot(stacked.astype(bf16), earlier)
    rank = jnp.sum(before[:owners] * match, axis=0, keepdims=True)
    starts = before[owners : owners + 1]
    slot = owner * capacity + rank.astype(jnp.int32)
    video_of_slot = (iota((slots, videos), 0) == slot).astype(f32).astype(bf16)
    high = jnp.floor(starts / 16.0) * 16.0
    low = starts - high
    tall = lambda row: jnp.broadcast_to(row, (LANES, videos)).astype(bf16)
    start = dot_rows(video_of_slot, tall(high)) + dot_rows(video_of_slot, tall(low))
    length = dot_rows(video_of_slot, tall(lengths))
    first, last = start.astype(jnp.int32), (start + length).astype(jnp.int32)
    member = jnp.concatenate(
        [
            (
                (iota((slots, LANES), 1) + at >= first) & (iota((slots, LANES), 1) + at < last)
            ).astype(f32)
            for at in range(0, frame_count, LANES)
        ],
        axis=1,
    ).astype(bf16)
    return video_of_slot, first, length, member


def code_matches(code_ref, code_total):
    frame_count = code_ref.shape[1]
    return (iota((code_total, frame_count), 0) == code_ref[...]).astype(f32).astype(bf16)


def pool_kernel(
    sizes,
    length_hbm,
    owner_hbm,
    cluster_hbm,
    code_hbm,
    frames_hbm,
    send_hbm,
    pooled_ref,
    matches_ref,
    counts_ref,
    *scratch,
):
    owners, cents, capacity, longest, code_total = sizes
    length_ref, owner_ref, cluster_ref, code_ref, frames_ref, send_ref, sems, out_sems = scratch
    copies = fetch(
        (length_hbm, owner_hbm, cluster_hbm, code_hbm, frames_hbm), scratch[:5], sems
    )
    me = lax.axis_index("cent")
    frame_count, features = frames_hbm.shape
    for copy in copies[:-1]:
        copy.wait()
    slots = owners * capacity
    share = features // cents
    video_of_slot, first, length, member = member_of_slots(
        length_ref, owner_ref, owners, capacity, frame_count
    )
    code = (code_ref[...] - EXACT).astype(f32)
    shifted = pltpu.roll(
        jnp.broadcast_to(code, (longest, frame_count)),
        frame_count - (longest - 1),
        1,
        stride=1,
        stride_axis=0,
    ).astype(bf16)
    at_start = jnp.concatenate(
        [
            ((iota((slots, LANES), 1) + at == first) & (length > 0)).astype(f32)
            for at in range(0, frame_count, LANES)
        ],
        axis=1,
    ).astype(bf16)
    slot_codes = dot_rows(shifted, at_start)
    rows = lambda ref: jnp.broadcast_to(ref[...], (longest, ref.shape[1])).astype(f32).astype(bf16)
    slot_length = dot_rows(rows(length_ref), video_of_slot)
    slot_cluster = dot_rows(rows(cluster_ref), video_of_slot)
    back = (longest - 1 - iota((longest, slots), 0)).astype(f32)
    slot_codes = jnp.where(back < slot_length, slot_codes, 2.0 * EXACT)
    slot_cluster = jnp.where(slot_length > 0, slot_cluster, -1.0)
    part = code_total // (owners * cents)
    high = code_ref[...] // part
    high_match = (iota((owners * cents, frame_count), 0) == high).astype(f32).astype(bf16)
    low_match = (iota((part, frame_count), 0) + high * part == code_ref[...]).astype(f32)
    counts = dot_rows(low_match.astype(bf16), high_match)
    half = part // 2
    lane = iota((half, LANES), 1)
    segment = lane // capacity
    last_codes, cluster_place, count_place = (
        segment == lax.rem(me + step, cents) for step in range(1, 4)
    )
    front = lane % capacity < capacity // 2
    for owner in range(owners):
        tile, place = divmod(owner * capacity, LANES)
        lanes = slice(tile * LANES, (tile + 1) * LANES)
        turned = lambda value, step: pltpu.roll(
            value, lax.rem((me + step) * capacity + LANES - place, LANES), 1
        )
        codes = turned(slot_codes[:half, lanes], 0)
        codes = jnp.where(last_codes, turned(slot_codes[half:, lanes], 1), codes)
        note = jnp.where(cluster_place, turned(slot_cluster[:half, lanes], 2), codes)
        for cent in range(cents):
            at = owner * cents + cent
            spread = lambda value: jnp.broadcast_to(value, (half, LANES))
            count = jnp.where(
                front, spread(counts[:half, at : at + 1]), spread(counts[half:, at : at + 1])
            )
            send_ref[owner, cent, 2 * capacity :, :] = jnp.where(count_place, count, note).astype(
                bf16
            )
    weight = 1.0 / jnp.maximum(length, 1.0)
    copies[-1].wait()
    half = share // 2
    out = []
    for cent in range(cents):
        sums = dot(member, frames_ref[:, cent * share : (cent + 1) * share])
        for side in range(2):
            pooled = (sums[:, side * half : (side + 1) * half] * weight).astype(bf16)
            at = cent * share + side * half
            pooled_ref[:, at : at + half] = pooled
            send_ref[:, cent, side * capacity : (side + 1) * capacity, :] = pooled.reshape(
                owners, capacity, half
            )
        out.append(
            pltpu.make_async_copy(send_ref.at[:, cent], send_hbm.at[:, cent], out_sems.at[cent])
        )
        out[-1].start()
    matches_ref[...] = code_matches(code_ref, code_total)
    counts_ref[...] = dot_rows(matches_ref[...], member).astype(bf16)
    for copy in out:
        copy.wait()


def give_kernel(
    sizes, frames_hbm, pooled_ref, matches_ref, counts_ref, give_ref, frames_ref, sems
):
    owners, cents, capacity, longest, code_total = sizes
    me = lax.axis_index("cent")
    share = frames_hbm.shape[1] // cents
    copies = fetch((frames_hbm,), (frames_ref,), sems)
    spans = [
        pl.ds(pl.multiple_of((me ^ step) * share, share), share) for step in range(1, cents, 2)
    ]
    removed = [dot(counts_ref[...], pooled_ref[:, span]) for span in spans]
    copies[0].wait()
    for at, span in enumerate(spans):
        sums = dot(matches_ref[...], frames_ref[:, span])
        give_ref[at] = (sums - removed[at]).astype(bf16)


def keep_kernel(sizes, frames_hbm, pooled_ref, matches_ref, counts_ref, keep_ref, frames_ref, sems):
    owners, cents, capacity, longest, code_total = sizes
    me = lax.axis_index("cent")
    share = frames_hbm.shape[1] // cents
    spans = [
        pl.ds(pl.multiple_of((me ^ step) * share, share), share) for step in range(0, cents, 2)
    ]
    copies = fetch(
        [frames_hbm.at[:, span] for span in spans],
        [frames_ref.at[at] for at in range(cents // 2)],
        sems,
    )
    for at, span in enumerate(spans):
        removed = dot(counts_ref[...], pooled_ref[:, span])
        copies[at].wait()
        keep_ref[at] = dot(matches_ref[...], frames_ref[at]) - removed


def slot_rows(got_ref, capacity):
    sources, _, half = got_ref.shape
    return jnp.concatenate(
        [
            got_ref[:, side * capacity : (side + 1) * capacity, :].reshape(sources * capacity, half)
            for side in range(2)
        ],
        axis=1,
    )


def owner_kernel(sizes, got_ref, old_ref, code_ref, count_ref, here_ref, beside_ref, across_ref, diagonal_ref, new_ref):
    owners, cents, capacity, longest, code_total = sizes
    me = lax.axis_index("cent")
    clusters, share = old_ref.shape
    half = longest // 2
    lane = iota((half, LANES), 1)
    segment = lane // capacity
    zeros = jnp.zeros((half, LANES), f32)
    count = zeros
    cluster_row = iota((clusters, LANES), 0).astype(f32).astype(bf16)
    picks, code_tiles = [], []
    for owner in range(owners):
        front, back, cluster = zeros, zeros, zeros
        for cent in range(cents):
            note = got_ref[owner * cents + cent, 2 * capacity :, :].astype(f32)
            placed = [segment == (cent + step) % cents for step in range(4)]
            front = jnp.where(placed[0], note, front)
            back = jnp.where(placed[1], note, back)
            cluster = jnp.where(placed[2], note, cluster)
            count = count + jnp.where(placed[3], note, 0.0)
        back = pltpu.roll(back, LANES - capacity, 1)
        cluster = pltpu.roll(cluster, LANES - 2 * capacity, 1).astype(bf16)
        picks.append(ones_where(cluster_row == cluster[0:1]))
        code_tiles.append(jnp.concatenate([front, back], axis=0))
    for step in range(cents.bit_length() - 1):
        count = count + pltpu.roll(count, capacity << step, 1)
    other = pltpu.roll(count, capacity // 2, 1)
    first = lane % capacity < capacity // 2
    count_ref[...] = jnp.concatenate(
        [jnp.where(first, count, other), jnp.where(first, other, count)], axis=0
    )
    pick = jnp.concatenate(picks, axis=1)
    rows = slot_rows(got_ref, capacity)
    sums = dot(pick, rows)
    number = dot(pick, jnp.ones((rows.shape[0], LANES), bf16))
    number = jnp.concatenate([number] * (share // LANES), axis=1)
    new = (sums + old_ref[...].astype(f32)) / (number + 1.0)
    new_ref[...] = new
    anchor = new.astype(bf16)
    bits = longest.bit_length()
    digits = 30 // bits
    block = -(-code_total // digits)
    block = -(-block // 16) * 16
    word_row = iota((block, LANES), 0)
    slot_counts = []
    for codes in code_tiles:
        codes = codes.astype(jnp.int32) + EXACT
        place = jnp.where(codes < code_total, codes, -1)
        one = jnp.ones((longest, LANES), jnp.int32)
        for digit in range(1, -(-code_total // block)):
            above = (codes >= digit * block) & (codes < code_total)
            place = place - jnp.where(above, block, 0)
            one = jnp.where(above, 1 << (bits * digit), one)
        words = jnp.zeros((block, LANES), jnp.int32)
        for row in range(longest):
            words = words + jnp.where(word_row == place[row : row + 1], one[row : row + 1], 0)
        held = []
        for digit in range(-(-code_total // block)):
            height = min(block, code_total - digit * block)
            word = words[:height] >> (bits * digit) & ((1 << bits) - 1)
            held.append(word.astype(f32).astype(bf16))
        slot_counts.append(jnp.concatenate(held, axis=0))
    slot_count = jnp.concatenate(slot_counts, axis=1)
    cluster_count = dot_rows(slot_count, pick)
    high = jnp.floor(cluster_count * (1.0 / EXACT))
    low = cluster_count - high * EXACT
    moved = dot(low.astype(bf16), anchor) + EXACT * dot(high.astype(bf16), anchor)
    code_ref[...] = dot(slot_count, rows) - moved
    quarter = clusters // cents
    rows_of = lambda step: new_ref[pl.ds(pl.multiple_of((me ^ step) * quarter, quarter), quarter), :]
    for step, ref in enumerate((here_ref, beside_ref, across_ref, diagonal_ref)):
        ref[...] = rows_of(step)


def finish_kernel(sizes, got_ref, count_ref, old_ref, out_ref):
    owners, cents, capacity, longest, code_total = sizes
    share = got_ref.shape[2]
    prior = jnp.concatenate([count_ref[...] + code_prior] * (share // LANES), axis=1)
    for cent in range(cents):
        total = got_ref[cent].astype(f32)
        for owner in range(1, owners):
            total = total + got_ref[owner * cents + cent].astype(f32)
        lanes = slice(cent * share, (cent + 1) * share)
        out_ref[:, lanes] = (total + code_prior * old_ref[:, lanes]) / prior


def join_kernel(here_ref, beside_ref, across_ref, diagonal_ref, out_ref):
    me = lax.axis_index("cent")
    share = here_ref.shape[1]
    for step, ref in enumerate((here_ref, beside_ref, across_ref, diagonal_ref)):
        out_ref[:, pl.ds(pl.multiple_of((me ^ step) * share, share), share)] = ref[...]


def summed_body(frames, video_length, video_owner, video_cluster, frame_code, old_coarse, old_codes):
    owners = lax.axis_size("dp")
    cents = lax.axis_size("cent")
    frame_count, features = frames.shape
    videos = video_length.shape[1]
    clusters = old_coarse.shape[0]
    part = old_codes.shape[0]
    code_total = part * owners * cents
    capacity = max(2, 2 * videos // owners)
    longest = 2 * frame_count // videos
    share = features // cents
    devices = owners * cents
    sizes = (owners, cents, capacity, longest, code_total)
    frame_code = frame_code.reshape(1, frame_count)
    vmem = pl.BlockSpec(memory_space=pltpu.VMEM)
    hbm = pl.BlockSpec(memory_space=pltpu.HBM)
    params = pltpu.CompilerParams(vmem_limit_bytes=32 * 1024 * 1024)
    chunk = 2 * capacity + longest // 2
    slots = owners * capacity
    stay = lambda array: pltpu.with_memory_space_constraint(array, pltpu.HBM)
    swap = lambda array, bit: lax.ppermute(
        array, "cent", [(index, index ^ bit) for index in range(cents)]
    )
    row = lambda length: pltpu.VMEM((1, length), jnp.int32)
    frames_scratch = [row(frame_count), pltpu.VMEM((frame_count, features), bf16)]
    quarter = clusters // cents
    send, pooled, matches, slot_counts = pl.pallas_call(
        functools.partial(pool_kernel, sizes),
        out_shape=(
            jax.ShapeDtypeStruct((owners, cents, chunk, share // 2), bf16),
            jax.ShapeDtypeStruct((slots, features), bf16),
            jax.ShapeDtypeStruct((code_total, frame_count), bf16),
            jax.ShapeDtypeStruct((code_total, slots), bf16),
        ),
        in_specs=[hbm] * 5,
        out_specs=(hbm, vmem, vmem, vmem),
        scratch_shapes=[row(videos)] * 3
        + frames_scratch
        + [
            pltpu.VMEM((owners, cents, chunk, share // 2), bf16),
            pltpu.SemaphoreType.DMA((5,)),
            pltpu.SemaphoreType.DMA((cents,)),
        ],
        compiler_params=params,
        name="pool",
    )(*map(stay, (video_length, video_owner, video_cluster, frame_code, frames)))
    got = lax.all_to_all(
        send.reshape(devices, chunk, share // 2), ("dp", "cent"), 0, 0, tiled=True
    )
    table = (cents // 2, code_total, share)
    give = pl.pallas_call(
        functools.partial(give_kernel, sizes),
        out_shape=jax.ShapeDtypeStruct(table, bf16),
        in_specs=[hbm] + [vmem] * 3,
        out_specs=vmem,
        scratch_shapes=[frames_scratch[1], pltpu.SemaphoreType.DMA((1,))],
        compiler_params=params,
        cost_estimate=pl.CostEstimate(
            flops=2 * code_total * frame_count * features,
            bytes_accessed=4 * frame_count * features,
            transcendentals=0,
        ),
        name="give",
    )(stay(frames), pooled, matches, slot_counts)
    near = swap(give, 1)
    keep = pl.pallas_call(
        functools.partial(keep_kernel, sizes),
        out_shape=jax.ShapeDtypeStruct(table, f32),
        in_specs=[hbm] + [vmem] * 3,
        out_specs=vmem,
        scratch_shapes=[
            pltpu.VMEM((cents // 2, frame_count, share), bf16),
            pltpu.SemaphoreType.DMA((cents // 2,)),
        ],
        compiler_params=params,
        cost_estimate=pl.CostEstimate(
            flops=2 * code_total * frame_count * features,
            bytes_accessed=4 * frame_count * features,
            transcendentals=0,
        ),
        name="keep",
    )(stay(frames), pooled, matches, slot_counts)
    base, cross = lax.optimization_barrier(
        (keep[0] + near[0].astype(f32), (keep[1] + near[1].astype(f32)).astype(bf16))
    )
    far = swap(cross, 2)
    piece = jax.ShapeDtypeStruct((quarter, share), f32)
    first = lax.axis_index("cent") * share
    old_part = lax.dynamic_slice_in_dim(old_coarse, first, share, 1)
    sums, count, here, beside, across, diagonal = pl.pallas_call(
        functools.partial(owner_kernel, sizes),
        out_shape=(
            jax.ShapeDtypeStruct((code_total, share), f32),
            jax.ShapeDtypeStruct((part, LANES), f32),
        )
        + (piece,) * cents,
        in_specs=[vmem, vmem],
        out_specs=(vmem,) * (2 + cents),
        scratch_shapes=[pltpu.VMEM((clusters, share), f32)],
        compiler_params=params,
        name="owner",
    )(got, old_part)
    sums = (sums + (base + far.astype(f32))).astype(bf16)
    last = lax.all_to_all(sums.reshape(devices, part, share), ("dp", "cent"), 0, 0, tiled=True)
    new_coarse = pl.pallas_call(
        join_kernel,
        out_shape=jax.ShapeDtypeStruct((quarter, features), f32),
        in_specs=[vmem] * 4,
        out_specs=vmem,
        compiler_params=params,
        name="join",
    )(here, swap(beside, 1), swap(across, 2), swap(diagonal, 3))
    new_codes = pl.pallas_call(
        functools.partial(finish_kernel, sizes),
        out_shape=jax.ShapeDtypeStruct((part, features), f32),
        in_specs=[vmem] * 3,
        out_specs=vmem,
        compiler_params=params,
        name="finish",
    )(last, count, old_codes)
    return new_coarse, new_codes


def owner_slots(target, target_count, capacity):
    matches = (target[:, None] == jnp.arange(target_count, dtype=jnp.int32)[None, :]).astype(
        jnp.int32
    )
    before = jnp.cumsum(matches, axis=0) - matches
    slot_rank = jnp.sum(before * matches, axis=1)
    return target * capacity + slot_rank


def invert_slots(slot_list, slot_total):
    item_index = jnp.arange(slot_list.shape[0], dtype=jnp.int32)
    source = jnp.zeros((slot_total,), jnp.int32).at[slot_list].set(item_index)
    filled = jnp.zeros((slot_total,), jnp.int32).at[slot_list].set(1)
    return (source, filled)


def routed_body(frames, video_length, video_owner, video_cluster, frame_code, old_coarse, old_codes):
    dp_count = lax.axis_size("dp")
    cent_count = lax.axis_size("cent")
    frame_count, features = frames.shape
    video_count = video_length.shape[1]
    coarse_rows = old_coarse.shape[0]
    code_share = old_codes.shape[0]
    code_block = code_share * cent_count
    cap_video = max(2, 2 * video_count // dp_count)
    cap_frame = max(2, 2 * frame_count // dp_count)
    lengths = video_length[0]
    target = video_owner[0]
    cluster = video_cluster[0]
    video_ends = jnp.cumsum(lengths)
    video_starts = video_ends - lengths
    position = jnp.arange(frame_count, dtype=jnp.int32)
    member = (
        (position[None, :] >= video_starts[:, None]) & (position[None, :] < video_ends[:, None])
    ).astype(jnp.bfloat16)
    video_sums = jnp.dot(member, frames, preferred_element_type=jnp.float32)
    pooled = (video_sums / lengths[:, None].astype(jnp.float32)).astype(jnp.bfloat16)
    video_slot = owner_slots(target, dp_count, cap_video)
    source, filled = invert_slots(video_slot, dp_count * cap_video)
    send_rows = jnp.where(filled[:, None] > 0, pooled[source], jnp.zeros((), jnp.bfloat16))
    send_codes = jnp.where(filled > 0, cluster[source], -1)
    got_rows, got_codes = (
        lax.all_to_all(
            send_rows.reshape(dp_count, cap_video, features),
            "dp",
            split_axis=0,
            concat_axis=0,
            tiled=True,
        ),
        lax.all_to_all(
            send_codes.reshape(dp_count, cap_video), "dp", split_axis=0, concat_axis=0, tiled=True
        ),
    )
    got_rows = got_rows.reshape(-1, features)
    got_codes = got_codes.reshape(-1)
    table_index = jnp.arange(coarse_rows, dtype=jnp.int32)
    coarse_pick = (got_codes[None, :] == table_index[:, None]).astype(jnp.bfloat16)
    coarse_sum = jnp.dot(coarse_pick, got_rows, preferred_element_type=jnp.float32)
    coarse_count = jnp.sum(coarse_pick.astype(jnp.float32), axis=1)
    quarter = coarse_rows // cent_count
    part_sum, part_count = (
        lax.psum_scatter(coarse_sum, "cent", scatter_dimension=0, tiled=True),
        lax.psum_scatter(coarse_count, "cent", scatter_dimension=0, tiled=True),
    )
    first_row = lax.axis_index("cent") * quarter
    old_part = lax.dynamic_slice_in_dim(old_coarse, first_row, quarter, 0).astype(jnp.float32)
    new_coarse = (part_sum + old_part) / (part_count[:, None] + 1.0)
    anchor_table = lax.all_gather(new_coarse.astype(jnp.bfloat16), "cent", axis=0, tiled=True)
    slot_anchor = jnp.dot(coarse_pick.T, anchor_table, preferred_element_type=jnp.float32).astype(
        jnp.bfloat16
    )
    returned = lax.all_to_all(
        slot_anchor.reshape(dp_count, cap_video, features),
        "dp",
        split_axis=0,
        concat_axis=0,
        tiled=True,
    )
    video_anchor = returned.reshape(-1, features)[video_slot]
    frame_anchor = jnp.dot(member.T, video_anchor, preferred_element_type=jnp.float32)
    residual = (frames - frame_anchor).astype(jnp.bfloat16)
    code_target = frame_code // code_block
    code_offset = frame_code - code_target * code_block
    frame_slot = owner_slots(code_target, dp_count, cap_frame)
    source, filled = invert_slots(frame_slot, dp_count * cap_frame)
    slot_rows = jnp.where(filled[:, None] > 0, residual[source], jnp.zeros((), jnp.bfloat16))
    slot_codes = jnp.where(filled > 0, code_offset[source], -1)
    code_rows, code_ids = (
        lax.all_to_all(
            slot_rows.reshape(dp_count, cap_frame, features),
            "dp",
            split_axis=0,
            concat_axis=0,
            tiled=True,
        ),
        lax.all_to_all(
            slot_codes.reshape(dp_count, cap_frame), "dp", split_axis=0, concat_axis=0, tiled=True
        ),
    )
    code_index = jnp.arange(code_block, dtype=jnp.int32)
    code_pick = (code_ids.reshape(-1)[None, :] == code_index[:, None]).astype(jnp.bfloat16)
    code_sum = jnp.dot(
        code_pick, code_rows.reshape(-1, features), preferred_element_type=jnp.float32
    )
    code_count = jnp.sum(code_pick.astype(jnp.float32), axis=1)
    own_sum, own_count = (
        lax.psum_scatter(code_sum, "cent", scatter_dimension=0, tiled=True),
        lax.psum_scatter(code_count, "cent", scatter_dimension=0, tiled=True),
    )
    new_codes = (own_sum + code_prior * old_codes) / (own_count[:, None] + code_prior)
    return (new_coarse, new_codes)


def choose(mesh):
    owners, cents = mesh.shape["dp"], mesh.shape["cent"]

    def body(*arrays):
        frame_count, features = arrays[0].shape
        videos = arrays[1].shape[1]
        part = arrays[6].shape[0]
        small = (
            part * owners * cents <= 2 * EXACT
            and arrays[5].shape[0] <= EXACT
            and cents == 4
            and cents * max(2, 2 * videos // owners) == LANES
            and part == 2 * frame_count // videos
            and features % (2 * cents * LANES) == 0
        )
        return (summed_body if small else routed_body)(*arrays)

    return body


def solution(mesh):
    placed = (
        P(("dp", "cent"), None),
        P(("dp", "cent"), None),
        P(("dp", "cent"), None),
        P(("dp", "cent"), None),
        P(("dp", "cent")),
        P("dp", None),
        P(("dp", "cent"), None),
    )
    return jax.shard_map(
        choose(mesh),
        mesh=mesh,
        in_specs=placed,
        out_specs=(P(("dp", "cent"), None), P(("dp", "cent"), None)),
        check_vma=False,
    )
```

```python
import functools

import jax
import jax.numpy as jnp
from jax import lax
from jax.experimental import pallas as pl
from jax.experimental.pallas import tpu as pltpu
from jax.sharding import PartitionSpec as P

code_prior = 16.0
LANES = 128
EXACT = 256
f32 = jnp.float32
bf16 = jnp.bfloat16


def iota(shape, axis):
    return lax.broadcasted_iota(jnp.int32, shape, axis)


def ones_where(mask):
    return jnp.where(mask, jnp.ones((), bf16), jnp.zeros((), bf16))


def fetch(sources, targets, sems):
    copies = [
        pltpu.make_async_copy(source, target, sems.at[at])
        for at, (source, target) in enumerate(zip(sources, targets))
    ]
    for copy in copies:
        copy.start()
    return copies


def dot(left, right):
    return jnp.dot(left, right, preferred_element_type=f32)


def dot_rows(left, right):
    return lax.dot_general(left, right, (((1,), (1,)), ((), ())), preferred_element_type=f32)


def member_of_slots(length_ref, owner_ref, owners, capacity, frame_count):
    videos = length_ref.shape[1]
    slots = owners * capacity
    lengths = length_ref[...].astype(f32)
    owner = owner_ref[...]
    match = (iota((owners, videos), 0) == owner).astype(f32)
    earlier = (iota((videos, videos), 0) < iota((videos, videos), 1)).astype(bf16)
    stacked = jnp.concatenate([match, jnp.broadcast_to(lengths, (8, videos))], axis=0)
    before = dot(stacked.astype(bf16), earlier)
    rank = jnp.sum(before[:owners] * match, axis=0, keepdims=True)
    starts = before[owners : owners + 1]
    slot = owner * capacity + rank.astype(jnp.int32)
    video_of_slot = (iota((slots, videos), 0) == slot).astype(f32).astype(bf16)
    high = jnp.floor(starts / 16.0) * 16.0
    low = starts - high
    tall = lambda row: jnp.broadcast_to(row, (LANES, videos)).astype(bf16)
    start = dot_rows(video_of_slot, tall(high)) + dot_rows(video_of_slot, tall(low))
    length = dot_rows(video_of_slot, tall(lengths))
    first, last = start.astype(jnp.int32), (start + length).astype(jnp.int32)
    member = jnp.concatenate(
        [
            (
                (iota((slots, LANES), 1) + at >= first) & (iota((slots, LANES), 1) + at < last)
            ).astype(f32)
            for at in range(0, frame_count, LANES)
        ],
        axis=1,
    ).astype(bf16)
    return video_of_slot, first, length, member


def code_matches(code_ref, code_total):
    frame_count = code_ref.shape[1]
    return (iota((code_total, frame_count), 0) == code_ref[...]).astype(f32).astype(bf16)


def pool_kernel(
    sizes,
    length_hbm,
    owner_hbm,
    cluster_hbm,
    code_hbm,
    frames_hbm,
    send_hbm,
    pooled_ref,
    member_ref,
    *scratch,
):
    owners, cents, capacity, longest, code_total = sizes
    length_ref, owner_ref, cluster_ref, code_ref, frames_ref, send_ref, sems, out_sems = scratch
    copies = fetch(
        (length_hbm, owner_hbm, cluster_hbm, code_hbm, frames_hbm), scratch[:5], sems
    )
    me = lax.axis_index("cent")
    frame_count, features = frames_hbm.shape
    for copy in copies[:-1]:
        copy.wait()
    slots = owners * capacity
    share = features // cents
    video_of_slot, first, length, member = member_of_slots(
        length_ref, owner_ref, owners, capacity, frame_count
    )
    member_ref[...] = member
    code = (code_ref[...] - EXACT).astype(f32)
    shifted = pltpu.roll(
        jnp.broadcast_to(code, (longest, frame_count)),
        frame_count - (longest - 1),
        1,
        stride=1,
        stride_axis=0,
    ).astype(bf16)
    at_start = jnp.concatenate(
        [
            ((iota((slots, LANES), 1) + at == first) & (length > 0)).astype(f32)
            for at in range(0, frame_count, LANES)
        ],
        axis=1,
    ).astype(bf16)
    slot_codes = dot_rows(shifted, at_start)
    rows = lambda ref: jnp.broadcast_to(ref[...], (longest, ref.shape[1])).astype(f32).astype(bf16)
    slot_length = dot_rows(rows(length_ref), video_of_slot)
    slot_cluster = dot_rows(rows(cluster_ref), video_of_slot)
    back = (longest - 1 - iota((longest, slots), 0)).astype(f32)
    slot_codes = jnp.where(back < slot_length, slot_codes, 2.0 * EXACT)
    slot_cluster = jnp.where(slot_length > 0, slot_cluster, -1.0)
    part = code_total // (owners * cents)
    high = code_ref[...] // part
    high_match = (iota((owners * cents, frame_count), 0) == high).astype(f32).astype(bf16)
    low_match = (iota((part, frame_count), 0) + high * part == code_ref[...]).astype(f32)
    counts = dot_rows(low_match.astype(bf16), high_match)
    half = part // 2
    lane = iota((half, LANES), 1)
    segment = lane // capacity
    last_codes, cluster_place, count_place = (
        segment == lax.rem(me + step, cents) for step in range(1, 4)
    )
    front = lane % capacity < capacity // 2
    for owner in range(owners):
        tile, place = divmod(owner * capacity, LANES)
        lanes = slice(tile * LANES, (tile + 1) * LANES)
        turned = lambda value, step: pltpu.roll(
            value, lax.rem((me + step) * capacity + LANES - place, LANES), 1
        )
        codes = turned(slot_codes[:half, lanes], 0)
        codes = jnp.where(last_codes, turned(slot_codes[half:, lanes], 1), codes)
        note = jnp.where(cluster_place, turned(slot_cluster[:half, lanes], 2), codes)
        for cent in range(cents):
            at = owner * cents + cent
            spread = lambda value: jnp.broadcast_to(value, (half, LANES))
            count = jnp.where(
                front, spread(counts[:half, at : at + 1]), spread(counts[half:, at : at + 1])
            )
            send_ref[owner, cent, 2 * capacity :, :] = jnp.where(count_place, count, note).astype(
                bf16
            )
    weight = 1.0 / jnp.maximum(length, 1.0)
    copies[-1].wait()
    half = share // 2
    out = []
    for cent in range(cents):
        sums = dot(member, frames_ref[:, cent * share : (cent + 1) * share])
        for side in range(2):
            pooled = (sums[:, side * half : (side + 1) * half] * weight).astype(bf16)
            at = cent * share + side * half
            pooled_ref[:, at : at + half] = pooled
            send_ref[:, cent, side * capacity : (side + 1) * capacity, :] = pooled.reshape(
                owners, capacity, half
            )
        out.append(
            pltpu.make_async_copy(send_ref.at[:, cent], send_hbm.at[:, cent], out_sems.at[cent])
        )
        out[-1].start()
    for copy in out:
        copy.wait()


def give_kernel(
    sizes,
    code_hbm,
    frames_hbm,
    pooled_ref,
    member_ref,
    give_ref,
    matches_ref,
    counts_ref,
    code_ref,
    frames_ref,
    sems,
):
    owners, cents, capacity, longest, code_total = sizes
    copies = fetch((code_hbm, frames_hbm), (code_ref, frames_ref), sems)
    me = lax.axis_index("cent")
    share = frames_hbm.shape[1] // cents
    copies[0].wait()
    matches_ref[...] = code_matches(code_ref, code_total)
    counts_ref[...] = dot_rows(matches_ref[...], member_ref[...]).astype(bf16)
    copies[1].wait()
    for step in range(1, cents, 2):
        columns = pl.ds(pl.multiple_of((me ^ step) * share, share), share)
        sums = dot(matches_ref[...], frames_ref[:, columns])
        give_ref[step // 2] = (sums - dot(counts_ref[...], pooled_ref[:, columns])).astype(bf16)


def keep_kernel(sizes, frames_hbm, pooled_ref, matches_ref, counts_ref, keep_ref, frames_ref, sems):
    owners, cents, capacity, longest, code_total = sizes
    me = lax.axis_index("cent")
    share = frames_hbm.shape[1] // cents
    spans = [
        pl.ds(pl.multiple_of((me ^ step) * share, share), share) for step in range(0, cents, 2)
    ]
    copies = fetch(
        [frames_hbm.at[:, span] for span in spans],
        [frames_ref.at[at] for at in range(cents // 2)],
        sems,
    )
    for at, span in enumerate(spans):
        removed = dot(counts_ref[...], pooled_ref[:, span])
        copies[at].wait()
        keep_ref[at] = dot(matches_ref[...], frames_ref[at]) - removed


def slot_rows(got_ref, capacity):
    sources, _, half = got_ref.shape
    return jnp.concatenate(
        [
            got_ref[:, side * capacity : (side + 1) * capacity, :].reshape(sources * capacity, half)
            for side in range(2)
        ],
        axis=1,
    )


def owner_kernel(sizes, got_ref, old_ref, code_ref, count_ref, here_ref, beside_ref, across_ref, diagonal_ref, new_ref):
    owners, cents, capacity, longest, code_total = sizes
    me = lax.axis_index("cent")
    clusters, share = old_ref.shape
    half = longest // 2
    lane = iota((half, LANES), 1)
    segment = lane // capacity
    zeros = jnp.zeros((half, LANES), f32)
    count = zeros
    cluster_row = iota((clusters, LANES), 0).astype(f32).astype(bf16)
    picks, code_tiles = [], []
    for owner in range(owners):
        front, back, cluster = zeros, zeros, zeros
        for cent in range(cents):
            note = got_ref[owner * cents + cent, 2 * capacity :, :].astype(f32)
            placed = [segment == (cent + step) % cents for step in range(4)]
            front = jnp.where(placed[0], note, front)
            back = jnp.where(placed[1], note, back)
            cluster = jnp.where(placed[2], note, cluster)
            count = count + jnp.where(placed[3], note, 0.0)
        back = pltpu.roll(back, LANES - capacity, 1)
        cluster = pltpu.roll(cluster, LANES - 2 * capacity, 1).astype(bf16)
        picks.append(ones_where(cluster_row == cluster[0:1]))
        code_tiles.append(jnp.concatenate([front, back], axis=0))
    for step in range(cents.bit_length() - 1):
        count = count + pltpu.roll(count, capacity << step, 1)
    other = pltpu.roll(count, capacity // 2, 1)
    first = lane % capacity < capacity // 2
    count_ref[...] = jnp.concatenate(
        [jnp.where(first, count, other), jnp.where(first, other, count)], axis=0
    )
    pick = jnp.concatenate(picks, axis=1)
    rows = slot_rows(got_ref, capacity)
    sums = dot(pick, rows)
    number = dot(pick, jnp.ones((rows.shape[0], LANES), bf16))
    number = jnp.concatenate([number] * (share // LANES), axis=1)
    new = (sums + old_ref[...].astype(f32)) / (number + 1.0)
    new_ref[...] = new
    anchor = new.astype(bf16)
    bits = longest.bit_length()
    digits = 30 // bits
    block = -(-code_total // digits)
    block = -(-block // 16) * 16
    word_row = iota((block, LANES), 0)
    slot_counts = []
    for codes in code_tiles:
        codes = codes.astype(jnp.int32) + EXACT
        place = jnp.where(codes < code_total, codes, -1)
        one = jnp.ones((longest, LANES), jnp.int32)
        for digit in range(1, -(-code_total // block)):
            above = (codes >= digit * block) & (codes < code_total)
            place = place - jnp.where(above, block, 0)
            one = jnp.where(above, 1 << (bits * digit), one)
        words = jnp.zeros((block, LANES), jnp.int32)
        for row in range(longest):
            words = words + jnp.where(word_row == place[row : row + 1], one[row : row + 1], 0)
        held = []
        for digit in range(-(-code_total // block)):
            height = min(block, code_total - digit * block)
            word = words[:height] >> (bits * digit) & ((1 << bits) - 1)
            held.append(word.astype(f32).astype(bf16))
        slot_counts.append(jnp.concatenate(held, axis=0))
    slot_count = jnp.concatenate(slot_counts, axis=1)
    cluster_count = dot_rows(slot_count, pick)
    high = jnp.floor(cluster_count * (1.0 / EXACT))
    low = cluster_count - high * EXACT
    moved = dot(low.astype(bf16), anchor) + EXACT * dot(high.astype(bf16), anchor)
    code_ref[...] = dot(slot_count, rows) - moved
    quarter = clusters // cents
    rows_of = lambda step: new_ref[pl.ds(pl.multiple_of((me ^ step) * quarter, quarter), quarter), :]
    for step, ref in enumerate((here_ref, beside_ref, across_ref, diagonal_ref)):
        ref[...] = rows_of(step)


def finish_kernel(sizes, got_ref, count_ref, old_ref, out_hbm, out_ref, sems):
    owners, cents, capacity, longest, code_total = sizes
    share = got_ref.shape[2]
    prior = jnp.concatenate([count_ref[...] + code_prior] * (share // LANES), axis=1)
    out = []
    for cent in range(cents):
        total = got_ref[cent].astype(f32)
        for owner in range(1, owners):
            total = total + got_ref[owner * cents + cent].astype(f32)
        lanes = slice(cent * share, (cent + 1) * share)
        out_ref[cent] = (total + code_prior * old_ref[:, lanes]) / prior
        out.append(pltpu.make_async_copy(out_ref.at[cent], out_hbm.at[:, lanes], sems.at[cent]))
        out[-1].start()
    for copy in out:
        copy.wait()


def join_kernel(here_ref, beside_ref, across_ref, diagonal_ref, out_ref):
    me = lax.axis_index("cent")
    share = here_ref.shape[1]
    for step, ref in enumerate((here_ref, beside_ref, across_ref, diagonal_ref)):
        out_ref[:, pl.ds(pl.multiple_of((me ^ step) * share, share), share)] = ref[...]


def summed_body(frames, video_length, video_owner, video_cluster, frame_code, old_coarse, old_codes):
    owners = lax.axis_size("dp")
    cents = lax.axis_size("cent")
    frame_count, features = frames.shape
    videos = video_length.shape[1]
    clusters = old_coarse.shape[0]
    part = old_codes.shape[0]
    code_total = part * owners * cents
    capacity = max(2, 2 * videos // owners)
    longest = 2 * frame_count // videos
    share = features // cents
    devices = owners * cents
    sizes = (owners, cents, capacity, longest, code_total)
    frame_code = frame_code.reshape(1, frame_count)
    vmem = pl.BlockSpec(memory_space=pltpu.VMEM)
    hbm = pl.BlockSpec(memory_space=pltpu.HBM)
    params = pltpu.CompilerParams(vmem_limit_bytes=32 * 1024 * 1024)
    chunk = 2 * capacity + longest // 2
    slots = owners * capacity
    stay = lambda array: pltpu.with_memory_space_constraint(array, pltpu.HBM)
    swap = lambda array, bit: lax.ppermute(
        array, "cent", [(index, index ^ bit) for index in range(cents)]
    )
    row = lambda length: pltpu.VMEM((1, length), jnp.int32)
    frames_scratch = [row(frame_count), pltpu.VMEM((frame_count, features), bf16)]
    quarter = clusters // cents
    send, pooled, member = pl.pallas_call(
        functools.partial(pool_kernel, sizes),
        out_shape=(
            jax.ShapeDtypeStruct((owners, cents, chunk, share // 2), bf16),
            jax.ShapeDtypeStruct((slots, features), bf16),
            jax.ShapeDtypeStruct((slots, frame_count), bf16),
        ),
        in_specs=[hbm] * 5,
        out_specs=(hbm, vmem, vmem),
        scratch_shapes=[row(videos)] * 3
        + frames_scratch
        + [
            pltpu.VMEM((owners, cents, chunk, share // 2), bf16),
            pltpu.SemaphoreType.DMA((5,)),
            pltpu.SemaphoreType.DMA((cents,)),
        ],
        compiler_params=params,
        name="pool",
    )(*map(stay, (video_length, video_owner, video_cluster, frame_code, frames)))
    got = lax.all_to_all(
        send.reshape(devices, chunk, share // 2), ("dp", "cent"), 0, 0, tiled=True
    )
    table = (cents // 2, code_total, share)
    give, matches, slot_counts = pl.pallas_call(
        functools.partial(give_kernel, sizes),
        out_shape=(
            jax.ShapeDtypeStruct(table, bf16),
            jax.ShapeDtypeStruct((code_total, frame_count), bf16),
            jax.ShapeDtypeStruct((code_total, slots), bf16),
        ),
        in_specs=[hbm] * 2 + [vmem] * 2,
        out_specs=(vmem,) * 3,
        scratch_shapes=frames_scratch + [pltpu.SemaphoreType.DMA((2,))],
        compiler_params=params,
        cost_estimate=pl.CostEstimate(
            flops=2 * code_total * frame_count * features,
            bytes_accessed=4 * frame_count * features,
            transcendentals=0,
        ),
        name="give",
    )(stay(frame_code), stay(frames), pooled, member)
    near = swap(give, 1)
    keep = pl.pallas_call(
        functools.partial(keep_kernel, sizes),
        out_shape=jax.ShapeDtypeStruct(table, f32),
        in_specs=[hbm] + [vmem] * 3,
        out_specs=vmem,
        scratch_shapes=[
            pltpu.VMEM((cents // 2, frame_count, share), bf16),
            pltpu.SemaphoreType.DMA((cents // 2,)),
        ],
        compiler_params=params,
        cost_estimate=pl.CostEstimate(
            flops=2 * code_total * frame_count * features,
            bytes_accessed=4 * frame_count * features,
            transcendentals=0,
        ),
        name="keep",
    )(stay(frames), pooled, matches, slot_counts)
    far = swap((keep[1] + near[1].astype(f32)).astype(bf16), 2)
    piece = jax.ShapeDtypeStruct((quarter, share), f32)
    first = lax.axis_index("cent") * share
    old_part = lax.dynamic_slice_in_dim(old_coarse, first, share, 1)
    sums, count, here, beside, across, diagonal = pl.pallas_call(
        functools.partial(owner_kernel, sizes),
        out_shape=(
            jax.ShapeDtypeStruct((code_total, share), f32),
            jax.ShapeDtypeStruct((part, LANES), f32),
        )
        + (piece,) * cents,
        in_specs=[vmem, vmem],
        out_specs=(vmem,) * (2 + cents),
        scratch_shapes=[pltpu.VMEM((clusters, share), f32)],
        compiler_params=params,
        name="owner",
    )(got, old_part)
    sums = (sums + (keep[0] + near[0].astype(f32) + far.astype(f32))).astype(bf16)
    last = lax.all_to_all(sums.reshape(devices, part, share), ("dp", "cent"), 0, 0, tiled=True)
    new_coarse = pl.pallas_call(
        join_kernel,
        out_shape=jax.ShapeDtypeStruct((quarter, features), f32),
        in_specs=[vmem] * 4,
        out_specs=vmem,
        compiler_params=params,
        name="join",
    )(here, swap(beside, 1), swap(across, 2), swap(diagonal, 3))
    new_codes = pl.pallas_call(
        functools.partial(finish_kernel, sizes),
        out_shape=jax.ShapeDtypeStruct((part, features), f32),
        in_specs=[vmem] * 3,
        out_specs=hbm,
        scratch_shapes=[
            pltpu.VMEM((cents, part, share), f32),
            pltpu.SemaphoreType.DMA((cents,)),
        ],
        compiler_params=params,
        name="finish",
    )(last, count, old_codes)
    return new_coarse, new_codes


def owner_slots(target, target_count, capacity):
    matches = (target[:, None] == jnp.arange(target_count, dtype=jnp.int32)[None, :]).astype(
        jnp.int32
    )
    before = jnp.cumsum(matches, axis=0) - matches
    slot_rank = jnp.sum(before * matches, axis=1)
    return target * capacity + slot_rank


def invert_slots(slot_list, slot_total):
    item_index = jnp.arange(slot_list.shape[0], dtype=jnp.int32)
    source = jnp.zeros((slot_total,), jnp.int32).at[slot_list].set(item_index)
    filled = jnp.zeros((slot_total,), jnp.int32).at[slot_list].set(1)
    return (source, filled)


def routed_body(frames, video_length, video_owner, video_cluster, frame_code, old_coarse, old_codes):
    dp_count = lax.axis_size("dp")
    cent_count = lax.axis_size("cent")
    frame_count, features = frames.shape
    video_count = video_length.shape[1]
    coarse_rows = old_coarse.shape[0]
    code_share = old_codes.shape[0]
    code_block = code_share * cent_count
    cap_video = max(2, 2 * video_count // dp_count)
    cap_frame = max(2, 2 * frame_count // dp_count)
    lengths = video_length[0]
    target = video_owner[0]
    cluster = video_cluster[0]
    video_ends = jnp.cumsum(lengths)
    video_starts = video_ends - lengths
    position = jnp.arange(frame_count, dtype=jnp.int32)
    member = (
        (position[None, :] >= video_starts[:, None]) & (position[None, :] < video_ends[:, None])
    ).astype(jnp.bfloat16)
    video_sums = jnp.dot(member, frames, preferred_element_type=jnp.float32)
    pooled = (video_sums / lengths[:, None].astype(jnp.float32)).astype(jnp.bfloat16)
    video_slot = owner_slots(target, dp_count, cap_video)
    source, filled = invert_slots(video_slot, dp_count * cap_video)
    send_rows = jnp.where(filled[:, None] > 0, pooled[source], jnp.zeros((), jnp.bfloat16))
    send_codes = jnp.where(filled > 0, cluster[source], -1)
    got_rows, got_codes = (
        lax.all_to_all(
            send_rows.reshape(dp_count, cap_video, features),
            "dp",
            split_axis=0,
            concat_axis=0,
            tiled=True,
        ),
        lax.all_to_all(
            send_codes.reshape(dp_count, cap_video), "dp", split_axis=0, concat_axis=0, tiled=True
        ),
    )
    got_rows = got_rows.reshape(-1, features)
    got_codes = got_codes.reshape(-1)
    table_index = jnp.arange(coarse_rows, dtype=jnp.int32)
    coarse_pick = (got_codes[None, :] == table_index[:, None]).astype(jnp.bfloat16)
    coarse_sum = jnp.dot(coarse_pick, got_rows, preferred_element_type=jnp.float32)
    coarse_count = jnp.sum(coarse_pick.astype(jnp.float32), axis=1)
    quarter = coarse_rows // cent_count
    part_sum, part_count = (
        lax.psum_scatter(coarse_sum, "cent", scatter_dimension=0, tiled=True),
        lax.psum_scatter(coarse_count, "cent", scatter_dimension=0, tiled=True),
    )
    first_row = lax.axis_index("cent") * quarter
    old_part = lax.dynamic_slice_in_dim(old_coarse, first_row, quarter, 0).astype(jnp.float32)
    new_coarse = (part_sum + old_part) / (part_count[:, None] + 1.0)
    anchor_table = lax.all_gather(new_coarse.astype(jnp.bfloat16), "cent", axis=0, tiled=True)
    slot_anchor = jnp.dot(coarse_pick.T, anchor_table, preferred_element_type=jnp.float32).astype(
        jnp.bfloat16
    )
    returned = lax.all_to_all(
        slot_anchor.reshape(dp_count, cap_video, features),
        "dp",
        split_axis=0,
        concat_axis=0,
        tiled=True,
    )
    video_anchor = returned.reshape(-1, features)[video_slot]
    frame_anchor = jnp.dot(member.T, video_anchor, preferred_element_type=jnp.float32)
    residual = (frames - frame_anchor).astype(jnp.bfloat16)
    code_target = frame_code // code_block
    code_offset = frame_code - code_target * code_block
    frame_slot = owner_slots(code_target, dp_count, cap_frame)
    source, filled = invert_slots(frame_slot, dp_count * cap_frame)
    slot_rows = jnp.where(filled[:, None] > 0, residual[source], jnp.zeros((), jnp.bfloat16))
    slot_codes = jnp.where(filled > 0, code_offset[source], -1)
    code_rows, code_ids = (
        lax.all_to_all(
            slot_rows.reshape(dp_count, cap_frame, features),
            "dp",
            split_axis=0,
            concat_axis=0,
            tiled=True,
        ),
        lax.all_to_all(
            slot_codes.reshape(dp_count, cap_frame), "dp", split_axis=0, concat_axis=0, tiled=True
        ),
    )
    code_index = jnp.arange(code_block, dtype=jnp.int32)
    code_pick = (code_ids.reshape(-1)[None, :] == code_index[:, None]).astype(jnp.bfloat16)
    code_sum = jnp.dot(
        code_pick, code_rows.reshape(-1, features), preferred_element_type=jnp.float32
    )
    code_count = jnp.sum(code_pick.astype(jnp.float32), axis=1)
    own_sum, own_count = (
        lax.psum_scatter(code_sum, "cent", scatter_dimension=0, tiled=True),
        lax.psum_scatter(code_count, "cent", scatter_dimension=0, tiled=True),
    )
    new_codes = (own_sum + code_prior * old_codes) / (own_count[:, None] + code_prior)
    return (new_coarse, new_codes)


def choose(mesh):
    owners, cents = mesh.shape["dp"], mesh.shape["cent"]

    def body(*arrays):
        frame_count, features = arrays[0].shape
        videos = arrays[1].shape[1]
        part = arrays[6].shape[0]
        small = (
            part * owners * cents <= 2 * EXACT
            and arrays[5].shape[0] <= EXACT
            and cents == 4
            and cents * max(2, 2 * videos // owners) == LANES
            and part == 2 * frame_count // videos
            and features % (2 * cents * LANES) == 0
        )
        return (summed_body if small else routed_body)(*arrays)

    return body


def solution(mesh):
    placed = (
        P(("dp", "cent"), None),
        P(("dp", "cent"), None),
        P(("dp", "cent"), None),
        P(("dp", "cent"), None),
        P(("dp", "cent")),
        P("dp", None),
        P(("dp", "cent"), None),
    )
    return jax.shard_map(
        choose(mesh),
        mesh=mesh,
        in_specs=placed,
        out_specs=(P(("dp", "cent"), None), P(("dp", "cent"), None)),
        check_vma=False,
    )
```
